256 devices in a mesh: lon: 16 (over z, x_hi), lat: 16 (over x_lo, y, core).
Axes of the slice: x: 4 (x_hi: 2, x_lo: 2; x = x_hi * 2 + x_lo), y: 4, z: 8, core: 2. Of those that a mesh axis runs over, the one named last changes fastest.
Arguments:
- inputs: bfloat16 [2, 96, 192, 512], P(None, 'lat', 'lon'), may hold values from -6 to 6
- cotangent: bfloat16 [2, 96, 192, 512], P(None, 'lat', 'lon'), may hold values from -6 to 6
- pad_mask: int32 [96, 192], P('lat', 'lon'), may hold values 0 or 1
- rel_index: int32 [144, 144], replicated, may hold values from 0 to 758
- bias_table: float32 [759, 16], replicated, may hold values from -4 to 4
- ln_gain: float32 [512], replicated, may hold values from 0.1 to 1.9
- w_qkv: bfloat16 [512, 1536], replicated, may hold values from -4 to 4
- w_out: bfloat16 [512, 512], replicated, may hold values from -0.25 to 0.25
Outputs:
- grad_inputs: float32 [2, 96, 192, 512], P(None, 'lat', 'lon')
- grad_gain: float32 [512], replicated
- grad_wqkv: float32 [512, 1536], replicated
- grad_wout: float32 [512, 512], replicated
- grad_table: float32 [759, 16], replicated
The draws below stay inside these ranges and needn't reach their ends.
All inputs are finite; a program needn't handle non-finite values. No bound on the sum of `pad_mask` on one device may be relied on, other than what follows from the above.
Results may differ from the reference program's by a relative error of at most 0.0095.
The reference program's roundings to bfloat16 on the way count: a program that leaves them out, or rounds other values in their place, can miss the bound.
Values may be sent and summed in bfloat16 or wider, within the bound.
A program may use at most 64 MiB of HBM per device.

```python
import jax
import jax.numpy as jnp
from jax import lax

D = 512
HEADS = 16
WLEV = 2
WLAT = 6
WLON = 12
LEV = 2
WT = 144
NBIAS = 759
NLAT = 96
NLON = 192
TOKENS = 36864


def draw_w_qkv(key, part):
    key = jax.random.fold_in(key, 7)
    base = jnp.clip(jax.random.normal(key, (D, 3 * D), jnp.float32), -4.0, 4.0) * D ** (-0.5)
    return base.astype(jnp.bfloat16)


def set_ends(drawn, own_key, low, top_value):
    spot = [jax.random.randint(jax.random.fold_in(own_key, axis), (), 0, length) for axis, length in enumerate(drawn.shape)]
    widest = drawn.shape.index(max(drawn.shape))
    beside = spot[:widest] + [(spot[widest] + 1) % drawn.shape[widest]] + spot[widest + 1:]
    return drawn.at[tuple(spot)].set(low).at[tuple(beside)].set(top_value)


def levels(stream_key, shape, cuts, smallest, largest):
    def one(axis_at, shards_of):
        heights = jax.random.uniform(jax.random.fold_in(jax.random.fold_in(stream_key, 6), axis_at), (shards_of,), jnp.float32, smallest / len(cuts), largest / len(cuts))
        return jnp.repeat(jnp.exp(heights), shape[axis_at] // shards_of).reshape((-1,) + (1,) * (len(shape) - axis_at - 1))

    factor_of = one(*cuts[0])
    for cut in cuts[1:]:
        factor_of = factor_of * one(*cut)
    return factor_of


def bell_draw(key, dims, deviation, most, shards=(), kind=jnp.bfloat16):
    result = deviation * jax.random.normal(key, dims, jnp.float32)
    if shards:
        result = result * levels(key, dims, shards, -0.22, 0.18)
    return jnp.clip(result, -most, most).astype(kind)


def setup_inputs(seed: int = 0) -> dict:
    splits = jax.random.split(jax.random.key(seed), 9)
    inputs = bell_draw(splits[0], (LEV, NLAT, NLON, D), 1.0, 6.0, ((1, 16), (2, 16)))
    cotangent = bell_draw(splits[1], (LEV, NLAT, NLON, D), 1.0, 6.0, ((1, 16), (2, 16)))
    pad_mask = set_ends((jax.random.randint(splits[2], (NLAT, NLON), 0, 4) < 3).astype(jnp.int32), jax.random.fold_in(splits[2], 1), 0, 1)
    rel_index = set_ends(jax.random.randint(splits[3], (WT, WT), 0, NBIAS), jax.random.fold_in(splits[3], 1), 0, NBIAS - 1).astype(jnp.int32)
    bias_table = bell_draw(splits[4], (NBIAS, HEADS), 1.0, 4.0, (), jnp.float32)
    ln_gain = jnp.clip(1.0 + 0.18 * jax.random.normal(splits[5], (D,), jnp.float32), 0.1, 1.9)
    w_qkv = draw_w_qkv(jax.random.fold_in(splits[8], 71), 0)
    w_out = bell_draw(splits[7], (D, D), D ** -0.5, 0.25)
    return {"inputs": inputs, "cotangent": cotangent, "pad_mask": pad_mask, "rel_index": rel_index, "bias_table": bias_table, "ln_gain": ln_gain, "w_qkv": w_qkv, "w_out": w_out}


EPSILON = 1e-05
MASKED = -30000.0

def to_windows(array_in):
    lev_count, row_count, col_count, feat_count = array_in.shape
    pieces = array_in.reshape(lev_count // WLEV, WLEV, row_count // WLAT, WLAT, col_count // WLON, WLON, feat_count)
    pieces = pieces.transpose(0, 2, 4, 1, 3, 5, 6)
    return pieces.reshape(-1, WLEV * WLAT * WLON, feat_count)

def from_windows(array_in, lev_count, row_count, col_count):
    feat_count = array_in.shape[-1]
    pieces = array_in.reshape(lev_count // WLEV, row_count // WLAT, col_count // WLON, WLEV, WLAT, WLON, feat_count)
    pieces = pieces.transpose(0, 3, 1, 4, 2, 5, 6)
    return pieces.reshape(lev_count, row_count, col_count, feat_count)

def window_grads(inputs, cotangent, valid_keys, group_ids, rel_index, bias_table, ln_gain, w_qkv, w_out):
    lev_count, row_count, col_count, feat_count = inputs.shape
    head_count = bias_table.shape[1]
    head_size = feat_count // head_count
    score_scale = head_size ** (-0.5)
    values_f = inputs.astype(jnp.float32)
    center = values_f - lax.optimization_barrier(jnp.mean(values_f, axis=-1, keepdims=True))
    variance = lax.optimization_barrier(jnp.mean(center * center, axis=-1, keepdims=True))
    inv_std = lax.rsqrt(variance + EPSILON)
    standard = center * inv_std
    normed = (standard * ln_gain).astype(jnp.bfloat16)
    window_in = to_windows(normed)
    window_count, window_size = (window_in.shape[0], window_in.shape[1])
    tokens_in = window_in.reshape(-1, feat_count)
    flat_cot = to_windows(cotangent).reshape(-1, feat_count)
    key_valid = to_windows(jnp.broadcast_to(valid_keys[None, :, :, None], (lev_count, row_count, col_count, 1)))[..., 0]
    key_group = to_windows(jnp.broadcast_to(group_ids[None, :, :, None], (lev_count, row_count, col_count, 1)))[..., 0]
    projected = jnp.dot(tokens_in, w_qkv, preferred_element_type=jnp.float32)
    shape_heads = (window_count, window_size, head_count, head_size)
    query_heads = projected[:, :feat_count].astype(jnp.bfloat16).reshape(shape_heads)
    key_heads = projected[:, feat_count:2 * feat_count].astype(jnp.bfloat16).reshape(shape_heads)
    value_heads = projected[:, 2 * feat_count:].astype(jnp.bfloat16).reshape(shape_heads)
    bias_pairs = jnp.take(bias_table, rel_index, axis=0).transpose(2, 0, 1)
    same_group = key_group[:, :, None] == key_group[:, None, :]
    key_seen = (key_valid[:, None, :] > 0.5) | jnp.eye(window_size, dtype=bool)[None]
    allowed = (same_group & key_seen)[:, None]
    scores = jnp.einsum('nqhd,nkhd->nhqk', query_heads.astype(jnp.float32), key_heads.astype(jnp.float32)) * score_scale
    scores = jnp.where(allowed, scores + bias_pairs[None], MASKED)
    row_max = lax.optimization_barrier(jnp.max(scores, axis=-1, keepdims=True))
    exponent = jnp.exp(scores - row_max)
    attn_probs = exponent / lax.optimization_barrier(jnp.sum(exponent, axis=-1, keepdims=True))
    probs_b = attn_probs.astype(jnp.bfloat16)
    attended = jnp.einsum('nhqk,nkhd->nqhd', probs_b.astype(jnp.float32), value_heads.astype(jnp.float32))
    attended = attended.astype(jnp.bfloat16).reshape(-1, feat_count)
    grad_wout = lax.dot_general(attended, flat_cot, (((0,), (0,)), ((), ())), preferred_element_type=jnp.float32)
    grad_att = lax.dot_general(flat_cot, w_out, (((1,), (1,)), ((), ())), preferred_element_type=jnp.float32)
    grad_att = grad_att.astype(jnp.bfloat16).reshape(shape_heads)
    grad_probs = jnp.einsum('nqhd,nkhd->nhqk', grad_att.astype(jnp.float32), value_heads.astype(jnp.float32))
    grad_values = jnp.einsum('nhqk,nqhd->nkhd', probs_b.astype(jnp.float32), grad_att.astype(jnp.float32)).astype(jnp.bfloat16)
    grad_scores = attn_probs * (grad_probs - lax.optimization_barrier(jnp.sum(attn_probs * grad_probs, axis=-1, keepdims=True)))
    pair_sums = lax.optimization_barrier(jnp.sum(grad_scores, axis=0)).transpose(1, 2, 0).reshape(-1, head_count)
    grad_table = jax.ops.segment_sum(pair_sums, rel_index.reshape(-1).astype(jnp.int32), num_segments=bias_table.shape[0])
    scores_b = grad_scores.astype(jnp.bfloat16).astype(jnp.float32)
    grad_query = (jnp.einsum('nhqk,nkhd->nqhd', scores_b, key_heads.astype(jnp.float32)) * score_scale).astype(jnp.bfloat16)
    grad_keys = (jnp.einsum('nhqk,nqhd->nkhd', scores_b, query_heads.astype(jnp.float32)) * score_scale).astype(jnp.bfloat16)
    grad_proj = jnp.concatenate([grad_query.reshape(-1, feat_count), grad_keys.reshape(-1, feat_count), grad_values.reshape(-1, feat_count)], axis=1)
    grad_wqkv = lax.dot_general(tokens_in, grad_proj, (((0,), (0,)), ((), ())), preferred_element_type=jnp.float32)
    grad_normed = lax.dot_general(grad_proj, w_qkv, (((1,), (1,)), ((), ())), preferred_element_type=jnp.float32)
    grad_normed = from_windows(grad_normed.reshape(window_count, window_size, feat_count), lev_count, row_count, col_count)
    grad_gain = lax.optimization_barrier(jnp.sum(grad_normed * standard, axis=(0, 1, 2)))
    grad_hat = grad_normed * ln_gain
    grad_in = inv_std * (grad_hat - lax.optimization_barrier(jnp.mean(grad_hat, axis=-1, keepdims=True)) - standard * lax.optimization_barrier(jnp.mean(grad_hat * standard, axis=-1, keepdims=True)))
    return (grad_in, (grad_gain, grad_wqkv, grad_wout, grad_table))

def reference(inputs, cotangent, pad_mask, rel_index, bias_table, ln_gain, w_qkv, w_out):
    half_lat = WLAT // 2
    half_lon = WLON // 2
    shifted = jnp.roll(inputs, (-half_lat, -half_lon), axis=(1, 2))
    shifted_cot = jnp.roll(cotangent, (-half_lat, -half_lon), axis=(1, 2))
    valid_keys = jnp.roll(pad_mask, (-half_lat, -half_lon), axis=(0, 1)).astype(jnp.float32)
    group_rows = (jnp.arange(NLAT) >= NLAT - half_lat).astype(jnp.int32)
    group_ids = jnp.broadcast_to(group_rows[:, None], (NLAT, NLON))
    block_count = NLAT // WLAT
    blocks_in = shifted.reshape(LEV, block_count, WLAT, NLON, D).transpose(1, 0, 2, 3, 4)
    blocks_cot = shifted_cot.reshape(LEV, block_count, WLAT, NLON, D).transpose(1, 0, 2, 3, 4)
    blocks_valid = valid_keys.reshape(block_count, WLAT, NLON)
    blocks_group = group_ids.reshape(block_count, WLAT, NLON)

    def scan_step(totals, block_in):
        grad_block, grad_parts = window_grads(block_in[0], block_in[1], block_in[2], block_in[3], rel_index, bias_table, ln_gain, w_qkv, w_out)
        return (jax.tree.map(lambda a, b: a + b, totals, grad_parts), grad_block)
    zeros = (jnp.zeros((D,), jnp.float32), jnp.zeros((D, 3 * D), jnp.float32), jnp.zeros((D, D), jnp.float32), jnp.zeros((NBIAS, HEADS), jnp.float32))
    totals, grad_blocks = lax.scan(scan_step, zeros, (blocks_in, blocks_cot, blocks_valid, blocks_group))
    grad_shifted = grad_blocks.transpose(1, 0, 2, 3, 4).reshape(LEV, NLAT, NLON, D)
    grad_inputs = jnp.roll(grad_shifted, (half_lat, half_lon), axis=(1, 2))
    grad_scale = float(TOKENS) ** (-0.5)
    return (grad_inputs, totals[0] * grad_scale, totals[1] * grad_scale, totals[2] * grad_scale, totals[3] * grad_scale)
```

```python
import jax
import jax.numpy as jnp
from jax import lax
from jax.experimental import pallas as pl
from jax.experimental.pallas import tpu as pltpu
from jax.sharding import PartitionSpec as P

F32 = jnp.float32
BF16 = jnp.bfloat16
I32 = jnp.int32
MESH = pl.DeviceIdType.MESH

EPSILON = 1e-05
MASKED = -30000.0
WT = 144
FEAT = 512
HEADS = 16
HEAD_SIZE = 32
NBIAS = 759
SCORE_SCALE = HEAD_SIZE ** (-0.5)
GRAD_SCALE = 36864.0 ** (-0.5)

NN = (((1,), (0,)), ((), ()))
NT = (((1,), (1,)), ((), ()))

HALO = 0
CORE = 9
RS1 = 13
RS2 = 19
RS3 = 25
AG1 = 39
AG2 = 53
AG3 = 59
SIB = 65
TCORE = 73
TX = 74
TY = 77
TZ = 80
TXG = 87
TSIB = 90
BACK = 91
SEMS = 94


def mm(a, b, dims=NN):
    return lax.dot_general(a, b, dims, preferred_element_type=F32)


def iota(shape, dim):
    return lax.broadcasted_iota(I32, shape, dim)


def body(
    x_ref, cot_ref, pad_ref, rel_ref, bias_ref, gain_ref, wqkv_ref, wout_ref,
    big_ref, gin_ref, table_ref, ggain_ref,
    xw, cw, pads, padf, relt, tab, bias, allow, std, istd, nrm, nrmt, cotf,
    proj, projt, gatt, gattt, attt, gradt, ds,
    sib_send, sib_recv, own_half, pay, r1, s1, r2, s2, r3,
    tsum, tb, rt0, t1, rt1, t2, rt2, t3, rt3, tf,
    back_send, back_recv, ginf, ssem, rsem,
):
    lon = lax.axis_index("lon")
    lat = lax.axis_index("lat")
    z, xhi = lon // 2, lon % 2
    xlo, rest = lat // 8, lat % 8
    y, core = rest // 2, rest % 2
    x = xhi * 2 + xlo

    def at_x(value):
        return (z * 2 + value // 2, (value % 2) * 8 + rest)

    def at_y(value):
        return (lon, xlo * 8 + value * 2 + core)

    def at_z(value):
        return (value * 2 + xhi, lat)

    sibling = (lon, xlo * 8 + y * 2 + (1 - core))
    west, east = (lon + 15) % 16, (lon + 1) % 16
    south, north = (lat + 15) % 16, (lat + 1) % 16

    def copy(src, dst, index, device):
        made = pltpu.make_async_remote_copy(
            src_ref=src, dst_ref=dst, send_sem=ssem.at[index], recv_sem=rsem.at[index],
            device_id=device, device_id_type=MESH,
        )
        return made

    barrier = pltpu.get_barrier_semaphore()
    partners = [sibling, (west, lat), (lon, south), (west, south), (east, lat), (lon, north), (east, north)]
    partners += [at_x((x + d) % 4) for d in range(1, 4)]
    partners += [at_y((y + d) % 4) for d in range(1, 4)]
    partners += [at_z((z + d) % 8) for d in range(1, 8)]
    for device in partners:
        pl.semaphore_signal(barrier, inc=1, device_id=device, device_id_type=MESH)
    pl.semaphore_wait(barrier, len(partners))

    halo = []
    places = (
        ((3, 0), (0, 6), (west, lat)),
        ((0, 6), (3, 0), (lon, south)),
        ((0, 0), (3, 6), (west, south)),
    )
    for n, (source, target, device) in enumerate(places):
        for m, (field, window) in enumerate(((x_ref, xw), (cot_ref, cw))):
            halo.append(copy(
                field.at[pl.ds(source[0], 3), pl.ds(source[1], 6)],
                window.at[pl.ds(target[0], 3), pl.ds(target[1], 6)],
                HALO + 3 * n + m, device,
            ))
        halo.append(copy(pad_ref, pads.at[n], HALO + 3 * n + 2, device))
    for made in halo:
        made.start()
    pltpu.sync_copy(x_ref.at[pl.ds(3, 3), pl.ds(6, 6)], xw.at[pl.ds(0, 3), pl.ds(0, 6)])
    pltpu.sync_copy(cot_ref.at[pl.ds(3, 3), pl.ds(6, 6)], cw.at[pl.ds(0, 3), pl.ds(0, 6)])

    token = iota((WT, WT), 0)
    order = (iota((WT, WT), 1) == (token % 2) * 72 + token // 2).astype(BF16)
    rel = rel_ref[...]
    low = mm(mm(order, (rel & 255).astype(F32).astype(BF16), NT).astype(BF16), order, NT)
    high = mm(mm(order, (rel >> 8).astype(F32).astype(BF16), NT).astype(BF16), order, NT)
    relt[...] = jnp.zeros((WT, 256), I32)
    relt[:, :WT] = (high * 256.0 + low).astype(I32)
    tab[...] = jnp.zeros((HEADS, 1, 768), F32)
    for head in range(HEADS):
        tab[head, :, :NBIAS] = bias_ref[head:head + 1, :]

    def lookup(head, carry):
        for part in range(2):
            index = relt[:, 128 * part:128 * part + 128]
            lane, chunk = index & 127, index >> 7
            found = jnp.zeros((WT, 128), F32)
            for c in range(6):
                row = jnp.broadcast_to(tab[head, :, 128 * c:128 * c + 128], (WT, 128))
                taken = jnp.take_along_axis(row, lane, axis=1, mode="promise_in_bounds")
                found = jnp.where(chunk == c, taken, found)
            if part == 0:
                bias[head, :, 0:128] = found
            else:
                bias[head, :, 128:WT] = found[:, 0:WT - 128]
        return carry

    lax.fori_loop(0, HEADS, lookup, 0)

    for made in halo:
        made.wait_recv()

    padf[...] = jnp.zeros((32, 128), F32)
    padf[0:6, 0:12] = pad_ref[...].astype(F32)
    for n in range(3):
        padf[8 * n + 8:8 * n + 14, 0:12] = pads[n].astype(F32)

    def spot(token_at):
        row, col = token_at // 24, (token_at % 24) // 2
        slot = (row >= 3).astype(I32) * 2 + (col >= 6).astype(I32)
        return row, slot, row + jnp.where(row < 3, 3, -3), col + jnp.where(col < 6, 6, -6)

    row, slot, source_row, unused = spot(iota((WT, 32), 0))
    row_pick = (iota((WT, 32), 1) == slot * 8 + source_row).astype(BF16)
    unused, unused, unused, source_col = spot(iota((WT, 128), 0))
    picked = mm(row_pick, padf[...].astype(BF16))
    valid = jnp.sum(jnp.where(iota((WT, 128), 1) == source_col, picked, 0.0), axis=1, keepdims=True)
    key, query = iota((WT, WT), 0), iota((WT, WT), 1)
    same_group = ((key >= 72) == (query >= 72)) | (lat != 15)
    allow[...] = (same_group & ((valid > 0.5) | (key == query))).astype(F32)

    tokens = xw[...].astype(F32).reshape(WT, FEAT)
    center = tokens - jnp.mean(tokens, axis=-1, keepdims=True)
    variance = jnp.mean(center * center, axis=-1, keepdims=True)
    inv_std = lax.rsqrt(variance + EPSILON)
    standard = center * inv_std
    std[...] = standard
    istd[...] = inv_std
    normed = (standard * gain_ref[...]).astype(BF16)
    nrm[...] = normed
    nrmt[...] = normed.T
    cotf[...] = cw[...].reshape(WT, FEAT)
    proj[...] = mm(nrm[...], wqkv_ref[...]).astype(BF16)
    projt[...] = proj[...].T
    gatt[...] = mm(cotf[...], wout_ref[...], NT).astype(BF16)
    gattt[...] = gatt[...].T

    def heads(group, carry):
        lanes = pl.ds(pl.multiple_of(group * 128, 128), 128)
        lanes_k = pl.ds(pl.multiple_of(FEAT + group * 128, 128), 128)
        lanes_v = pl.ds(pl.multiple_of(2 * FEAT + group * 128, 128), 128)
        q_group, k_group, v_group = proj[:, lanes], proj[:, lanes_k], proj[:, lanes_v]
        ga_group = gatt[:, lanes]
        lane_head = iota((1, 128), 1) // HEAD_SIZE
        for j in range(4):
            head = group * 4 + j
            rows = pl.ds(pl.multiple_of(head * HEAD_SIZE, HEAD_SIZE), HEAD_SIZE)
            rows_k = pl.ds(pl.multiple_of(FEAT + head * HEAD_SIZE, HEAD_SIZE), HEAD_SIZE)
            rows_v = pl.ds(pl.multiple_of(2 * FEAT + head * HEAD_SIZE, HEAD_SIZE), HEAD_SIZE)
            mine = (lane_head == j).astype(F32).astype(BF16)
            scores = mm(k_group * mine, q_group, NT) * SCORE_SCALE
            scores = jnp.where(allow[...] > 0.5, scores + bias[head], MASKED)
            exponent = jnp.exp(scores - jnp.max(scores, axis=0, keepdims=True))
            probs = exponent * (1.0 / jnp.sum(exponent, axis=0, keepdims=True))
            probs_b = probs.astype(BF16)
            attt[rows, :] = mm(projt[rows_v, :], probs_b).astype(BF16)
            gradt[rows_v, :] = mm(gattt[rows, :], probs_b, NT).astype(BF16)
            grad_probs = mm(v_group * mine, ga_group, NT)
            inner = jnp.sum(probs * grad_probs, axis=0, keepdims=True)
            grad_scores = probs * (grad_probs - inner)
            ds[head] = grad_scores
            grad_b = grad_scores.astype(BF16)
            gradt[rows, :] = (mm(projt[rows_k, :], grad_b) * SCORE_SCALE).astype(BF16)
            gradt[rows_k, :] = (mm(projt[rows, :], grad_b, NT) * SCORE_SCALE).astype(BF16)
        return carry

    lax.fori_loop(0, 4, heads, 0)

    def half_block(which, block):
        if block < 3:
            rows = pl.ds(pl.multiple_of(block * FEAT + which * 256, 256), 256)
            out = mm(nrmt[...], gradt[rows, :], NT)
            return out[:, 0:128], out[:, 128:256]
        rows = pl.ds(pl.multiple_of(which * 256, 256), 256)
        out = mm(attt[rows, :], cotf[...])
        return (
            jnp.concatenate([out[:, 0:128], out[:, 128:256]], axis=0),
            jnp.concatenate([out[:, 256:384], out[:, 384:512]], axis=0),
        )

    core_copies = []
    for block in range(4):
        first, second = half_block(1 - core, block)
        sib_send[0, 512 * block:512 * block + 512, :] = first.astype(BF16)
        sib_send[1, 512 * block:512 * block + 512, :] = second.astype(BF16)
        made = copy(
            sib_send.at[:, pl.ds(512 * block, 512)], sib_recv.at[:, pl.ds(512 * block, 512)],
            CORE + block, sibling,
        )
        made.start()
        core_copies.append(made)
    for block in range(4):
        first, second = half_block(core, block)
        own_half[0, 512 * block:512 * block + 512, :] = first
        own_half[1, 512 * block:512 * block + 512, :] = second
    for block in range(4):
        core_copies[block].wait_recv()

        def add_block(step, carry, block=block):
            rows = pl.ds(pl.multiple_of(512 * block + 128 * step, 128), 128)
            pay[:, rows, :] = (own_half[:, rows, :] + sib_recv[:, rows, :].astype(F32)).astype(BF16)
            return carry

        lax.fori_loop(0, 4, add_block, 0)

    def rows_of(start, count):
        return pl.ds(pl.multiple_of(start, 16), count)

    major, minor = (x, y), (y, x)
    at_major, at_minor = (at_x, at_y), (at_y, at_x)
    rs1 = [[], []]
    for d in range(1, 4):
        for p in range(2):
            to = (major[p] + d) % 4
            made = copy(pay.at[p, rows_of(512 * to, 512)], r1.at[p, d - 1], RS1 + 3 * p + d - 1, at_major[p](to))
            made.start()
            rs1[p].append(made)

    ones = iota((96, WT), 0)
    sub = iota((8, WT), 0)

    def scatter(step, total):
        rows = pl.ds(pl.multiple_of(8 * step, 8), 8)
        indices = relt[rows, 0:WT]
        for k in range(8):
            index = indices[k:k + 1, :]
            upper = (ones == (index >> 3)).astype(F32).astype(BF16)
            match = sub == (index & 7)
            pieces = [
                jnp.where(match, jnp.broadcast_to(ds[h, rows, :][k:k + 1, :], (8, WT)), 0.0)
                for h in range(HEADS)
            ]
            total = total + mm(upper, jnp.concatenate(pieces, axis=0).astype(BF16), NT)
        return total

    total = lax.fori_loop(0, WT // 8, scatter, jnp.zeros((96, 128), F32))
    tsum[...] = total.T
    spread = (iota((96, 768), 1) // 8 == iota((96, 768), 0)).astype(F32)
    wide = lax.dot_general(tsum[...], spread, NN, precision=lax.Precision.HIGHEST, preferred_element_type=F32)
    wide = jnp.where(iota((128, 768), 1) % 8 == iota((128, 768), 0) % 8, wide, 0.0)
    wide = jnp.sum(wide.reshape(HEADS, 8, 768), axis=1)
    tb[...] = jnp.zeros((128, 128), F32)
    for c in range(6):
        tb[16 * c:16 * c + 16, :] = wide[:, 128 * c:128 * c + 128]

    grad_normed = mm(gradt[...].T, wqkv_ref[...], NT)
    standard = std[...]
    grad_gain = jnp.sum(grad_normed * standard, axis=0, keepdims=True)
    for c in range(4):
        tb[96 + c:97 + c, :] = grad_gain[:, 128 * c:128 * c + 128]
    tcore = copy(tb.at[rows_of(64 * (1 - core), 64)], rt0, TCORE, sibling)
    tcore.start()
    grad_hat = grad_normed * gain_ref[...]
    grad_in = istd[...] * (
        grad_hat
        - jnp.mean(grad_hat, axis=-1, keepdims=True)
        - standard * jnp.mean(grad_hat * standard, axis=-1, keepdims=True)
    )
    back_send[...] = grad_in.astype(BF16).reshape(6, 12, 2, FEAT)
    back = []
    returns = (
        ((0, 6), (3, 0), (east, lat)),
        ((3, 0), (0, 6), (lon, north)),
        ((3, 6), (0, 0), (east, north)),
    )
    for n, (source, target, device) in enumerate(returns):
        made = copy(
            back_send.at[pl.ds(source[0], 3), pl.ds(source[1], 6)],
            back_recv.at[pl.ds(target[0], 3), pl.ds(target[1], 6)],
            BACK + n, device,
        )
        made.start()
        back.append(made)
    ginf[...] = grad_in.reshape(6, 12, 2, FEAT)

    rs2 = [[], []]
    for p in range(2):
        for made in rs1[p]:
            made.wait_recv()

        def add_one(step, carry, p=p):
            rows = pl.ds(pl.multiple_of(128 * step, 128), 128)
            own = pl.ds(pl.multiple_of(512 * major[p] + 128 * step, 128), 128)
            value = pay[p, own, :].astype(F32)
            for d in range(3):
                value = value + r1[p, d, rows, :].astype(F32)
            s1[p, rows, :] = value.astype(BF16)
            return carry

        lax.fori_loop(0, 4, add_one, 0)
        for d in range(1, 4):
            to = (minor[p] + d) % 4
            made = copy(s1.at[p, rows_of(128 * to, 128)], r2.at[p, d - 1], RS2 + 3 * p + d - 1, at_minor[p](to))
            made.start()
            rs2[p].append(made)

    tcore.wait_recv()
    t1[...] = tb[rows_of(64 * core, 64), :] + rt0[...]
    tx = []
    for d in range(1, 4):
        to = (x + d) % 4
        made = copy(t1.at[rows_of(16 * to, 16)], rt1.at[d - 1], TX + d - 1, at_x(to))
        made.start()
        tx.append(made)

    rs3 = [[], []]
    for p in range(2):
        for made in rs2[p]:
            made.wait_recv()
        value = s1[p, rows_of(128 * minor[p], 128), :].astype(F32)
        for d in range(3):
            value = value + r2[p, d].astype(F32)
        s2[p] = value.astype(BF16)
        for d in range(1, 8):
            to = (z + d) % 8
            made = copy(s2.at[p, rows_of(16 * to, 16)], r3.at[p, d - 1], RS3 + 7 * p + d - 1, at_z(to))
            made.start()
            rs3[p].append(made)

    for made in tx:
        made.wait_recv()
    value = t1[rows_of(16 * x, 16), :]
    for d in range(3):
        value = value + rt1[d]
    t2[...] = value
    ty = []
    for d in range(1, 4):
        made = copy(t2, rt2.at[d - 1], TY + d - 1, at_y((y + d) % 4))
        made.start()
        ty.append(made)

    base1 = [512 * major[p] for p in range(2)]
    base2 = [base1[p] + 128 * minor[p] for p in range(2)]
    base3 = [base2[p] + 16 * z for p in range(2)]

    def gather(p, base, count, index, device):
        part = big_ref.at[core, p, rows_of(base, count)]
        made = copy(part, part, index, device)
        made.start()
        return made

    ag1 = [[], []]
    for p in range(2):
        for made in rs3[p]:
            made.wait_recv()
        value = s2[p, rows_of(16 * z, 16), :].astype(F32)
        for d in range(7):
            value = value + r3[p, d].astype(F32)
        big_ref[core, p, rows_of(base3[p], 16), :] = value.astype(BF16)
        for d in range(1, 8):
            ag1[p].append(gather(p, base3[p], 16, AG1 + 7 * p + d - 1, at_z((z + d) % 8)))

    for made in ty:
        made.wait_recv()
    value = t2[...]
    for d in range(3):
        value = value + rt2[d]
    t3[...] = value
    tz = []
    for d in range(1, 8):
        made = copy(t3, rt3.at[d - 1], TZ + d - 1, at_z((z + d) % 8))
        made.start()
        tz.append(made)

    ag2 = [[], []]
    for p in range(2):
        for made in ag1[p]:
            made.wait_recv()
        for d in range(1, 4):
            ag2[p].append(gather(p, base2[p], 128, AG2 + 3 * p + d - 1, at_minor[p]((minor[p] + d) % 4)))

    for made in tz:
        made.wait_recv()
    value = t3[...]
    for d in range(7):
        value = value + rt3[d]
    trow = 64 * core + 16 * x
    tf[rows_of(trow, 16), :] = value * GRAD_SCALE
    txg = []
    for d in range(1, 4):
        made = copy(tf.at[rows_of(trow, 16)], tf.at[rows_of(trow, 16)], TXG + d - 1, at_x((x + d) % 4))
        made.start()
        txg.append(made)

    ag3 = [[], []]
    sib = []

    def forward(p, block, index):
        part = big_ref.at[core, p, rows_of(512 * block, 512)]
        made = copy(part, part, index, sibling)
        made.start()
        sib.append(made)

    for p in range(2):
        for made in ag2[p]:
            made.wait_recv()
        for d in range(1, 4):
            ag3[p].append(gather(p, base1[p], 512, AG3 + 3 * p + d - 1, at_major[p]((major[p] + d) % 4)))
        forward(p, major[p], SIB + 4 * p)

    for made in back:
        made.wait_recv()
    gin_ref[0:3, 0:6] = back_recv[0:3, 0:6].astype(F32)
    gin_ref[0:3, 6:12] = back_recv[0:3, 6:12].astype(F32)
    gin_ref[3:6, 0:6] = back_recv[3:6, 0:6].astype(F32)
    gin_ref[3:6, 6:12] = ginf[0:3, 0:6]

    for made in txg:
        made.wait_recv()
    thalf = tf.at[rows_of(64 * core, 64)]
    tsib = copy(thalf, thalf, TSIB, sibling)
    tsib.start()

    for d in range(1, 4):
        for p in range(2):
            ag3[p][d - 1].wait_recv()
            forward(p, (major[p] + 4 - d) % 4, SIB + 4 * p + d)

    tsib.wait_recv()
    for c in range(5):
        table_ref[:, 128 * c:128 * c + 128] = tf[16 * c:16 * c + 16, :]
    table_ref[:, 640:NBIAS] = tf[80:96, 0:NBIAS - 640]
    for c in range(4):
        ggain_ref[:, 128 * c:128 * c + 128] = tf[96 + c:97 + c, :]

    for made in sib:
        made.wait_recv()
    every = halo + core_copies + rs1[0] + rs1[1] + rs2[0] + rs2[1] + rs3[0] + rs3[1]
    every += ag1[0] + ag1[1] + ag2[0] + ag2[1] + ag3[0] + ag3[1] + sib
    every += [tcore] + tx + ty + tz + txg + [tsib] + back
    for made in every:
        made.wait_send()


def per_device(inputs, cotangent, pad_mask, rel_index, bias_table, ln_gain, w_qkv, w_out):
    vmem = pl.BlockSpec(memory_space=pltpu.VMEM)
    anywhere = pl.BlockSpec(memory_space=pl.ANY)
    big, grad_in, table, gain = pl.pallas_call(
        body,
        out_shape=(
            jax.ShapeDtypeStruct((2, 2, 2048, 128), BF16),
            jax.ShapeDtypeStruct((6, 12, 2, FEAT), F32),
            jax.ShapeDtypeStruct((HEADS, NBIAS), F32),
            jax.ShapeDtypeStruct((1, FEAT), F32),
        ),
        in_specs=[anywhere, anywhere] + [vmem] * 6,
        out_specs=[vmem] * 4,
        scratch_shapes=[
            pltpu.VMEM((6, 12, 2, FEAT), BF16),
            pltpu.VMEM((6, 12, 2, FEAT), BF16),
            pltpu.VMEM((3, 6, 12), I32),
            pltpu.VMEM((32, 128), F32),
            pltpu.VMEM((WT, 256), I32),
            pltpu.VMEM((HEADS, 1, 768), F32),
            pltpu.VMEM((HEADS, WT, WT), F32),
            pltpu.VMEM((WT, WT), F32),
            pltpu.VMEM((WT, FEAT), F32),
            pltpu.VMEM((WT, 1), F32),
            pltpu.VMEM((WT, FEAT), BF16),
            pltpu.VMEM((FEAT, WT), BF16),
            pltpu.VMEM((WT, FEAT), BF16),
            pltpu.VMEM((WT, 3 * FEAT), BF16),
            pltpu.VMEM((3 * FEAT, WT), BF16),
            pltpu.VMEM((WT, FEAT), BF16),
            pltpu.VMEM((FEAT, WT), BF16),
            pltpu.VMEM((FEAT, WT), BF16),
            pltpu.VMEM((3 * FEAT, WT), BF16),
            pltpu.VMEM((HEADS, WT, WT), F32),
            pltpu.VMEM((2, 2048, 128), BF16),
            pltpu.VMEM((2, 2048, 128), BF16),
            pltpu.VMEM((2, 2048, 128), F32),
            pltpu.VMEM((2, 2048, 128), BF16),
            pltpu.VMEM((2, 3, 512, 128), BF16),
            pltpu.VMEM((2, 512, 128), BF16),
            pltpu.VMEM((2, 3, 128, 128), BF16),
            pltpu.VMEM((2, 128, 128), BF16),
            pltpu.VMEM((2, 7, 16, 128), BF16),
            pltpu.VMEM((128, 96), F32),
            pltpu.VMEM((128, 128), F32),
            pltpu.VMEM((64, 128), F32),
            pltpu.VMEM((64, 128), F32),
            pltpu.VMEM((3, 16, 128), F32),
            pltpu.VMEM((16, 128), F32),
            pltpu.VMEM((3, 16, 128), F32),
            pltpu.VMEM((16, 128), F32),
            pltpu.VMEM((7, 16, 128), F32),
            pltpu.VMEM((128, 128), F32),
            pltpu.VMEM((6, 12, 2, FEAT), BF16),
            pltpu.VMEM((6, 12, 2, FEAT), BF16),
            pltpu.VMEM((6, 12, 2, FEAT), F32),
            pltpu.SemaphoreType.DMA((SEMS,)),
            pltpu.SemaphoreType.DMA((SEMS,)),
        ],
        compiler_params=pltpu.CompilerParams(
            collective_id=0, has_side_effects=True, vmem_limit_bytes=48 * 1024 * 1024
        ),
    )(
        inputs.transpose(1, 2, 0, 3),
        cotangent.transpose(1, 2, 0, 3),
        pad_mask,
        rel_index,
        bias_table.T,
        ln_gain.reshape(1, FEAT),
        w_qkv,
        w_out,
    )
    wqkv = big[:, :, :1536].reshape(2, 2, 3, FEAT, 128).transpose(3, 2, 0, 1, 4).reshape(FEAT, 3 * FEAT)
    wout = big[:, :, 1536:].reshape(2, 2, 2, 256, 128).transpose(0, 3, 1, 2, 4).reshape(FEAT, FEAT)
    return (
        grad_in.transpose(2, 0, 1, 3),
        gain.reshape(FEAT),
        wqkv.astype(F32) * GRAD_SCALE,
        wout.astype(F32) * GRAD_SCALE,
        table.T,
    )


def solution(mesh):
    in_specs = (
        P(None, "lat", "lon", None),
        P(None, "lat", "lon", None),
        P("lat", "lon"),
        P(),
        P(),
        P(),
        P(),
        P(),
    )
    out_specs = (P(None, "lat", "lon", None), P(), P(), P(), P())
    return jax.shard_map(
        per_device, mesh=mesh, in_specs=in_specs, out_specs=out_specs, check_vma=False
    )
```

```python
import jax
import jax.numpy as jnp
from jax import lax
from jax.experimental import pallas as pl
from jax.experimental.pallas import tpu as pltpu
from jax.sharding import PartitionSpec as P

F32 = jnp.float32
BF16 = jnp.bfloat16
I32 = jnp.int32
MESH = pl.DeviceIdType.MESH

EPSILON = 1e-05
MASKED = -30000.0
WT = 144
FEAT = 512
HEADS = 16
HEAD_SIZE = 32
NBIAS = 759
SCORE_SCALE = HEAD_SIZE ** (-0.5)
GRAD_SCALE = 36864.0 ** (-0.5)

NN = (((1,), (0,)), ((), ()))
NT = (((1,), (1,)), ((), ()))

HALO = 0
CORE = 9
RS1 = 13
RS2 = 19
RS3 = 25
AG1 = 39
AG2 = 53
AG3 = 59
SIB = 65
TCORE = 73
TX = 74
TY = 77
TZ = 80
TXG = 87
TSIB = 90
BACK = 91
SEMS = 94


def mm(a, b, dims=NN):
    return lax.dot_general(a, b, dims, preferred_element_type=F32)


def iota(shape, dim):
    return lax.broadcasted_iota(I32, shape, dim)


def body(
    x_ref, cot_ref, pad_hbm, rel_hbm, bias_hbm, gain_hbm, wqkv_hbm, wout_hbm,
    big_ref, gin_ref, table_ref, ggain_ref,
    pad_ref, rel_ref, bias_ref, gain_ref, wqkv_ref, wout_ref,
    xw, cw, pads, padf, relt, tab, edge, edge_bias, bias, allow, std, istd, nrm, nrmt, cotf,
    proj, projt, gatt, gattt, attt, gradt, ds,
    sib_send, sib_recv, own_half, pay, r1, s1, r2, s2, r3,
    tsum, tb, rt0, t1, rt1, t2, rt2, t3, rt3, tf,
    back_send, back_recv, ginf, ssem, rsem, lsem,
):
    lon = lax.axis_index("lon")
    lat = lax.axis_index("lat")
    z, xhi = lon // 2, lon % 2
    xlo, rest = lat // 8, lat % 8
    y, core = rest // 2, rest % 2
    x = xhi * 2 + xlo

    def at_x(value):
        return (z * 2 + value // 2, (value % 2) * 8 + rest)

    def at_y(value):
        return (lon, xlo * 8 + value * 2 + core)

    def at_z(value):
        return (value * 2 + xhi, lat)

    sibling = (lon, xlo * 8 + y * 2 + (1 - core))
    west, east = (lon + 15) % 16, (lon + 1) % 16
    south, north = (lat + 15) % 16, (lat + 1) % 16

    started = []

    def copy(src, dst, index, device):
        made = pltpu.make_async_remote_copy(
            src_ref=src, dst_ref=dst, send_sem=ssem.at[index], recv_sem=rsem.at[index],
            device_id=device, device_id_type=MESH,
        )
        started.append(made)
        return made

    loads = {}
    for n, (name, src, dst) in enumerate((
        ("rel", rel_hbm, rel_ref),
        ("bias", bias_hbm, bias_ref),
        ("pad", pad_hbm, pad_ref),
        ("x", x_ref.at[pl.ds(3, 3), pl.ds(6, 6)], xw.at[pl.ds(0, 3), pl.ds(0, 6)]),
        ("cot", cot_ref.at[pl.ds(3, 3), pl.ds(6, 6)], cw.at[pl.ds(0, 3), pl.ds(0, 6)]),
        ("gain", gain_hbm, gain_ref),
        ("wqkv", wqkv_hbm, wqkv_ref),
        ("wout", wout_hbm, wout_ref),
    )):
        loads[name] = pltpu.make_async_copy(src, dst, lsem.at[n])
        loads[name].start()

    barrier = pltpu.get_barrier_semaphore()
    partners = [sibling, (west, lat), (lon, south), (west, south), (east, lat), (lon, north), (east, north)]
    partners += [at_x((x + d) % 4) for d in range(1, 4)]
    partners += [at_y((y + d) % 4) for d in range(1, 4)]
    partners += [at_z((z + d) % 8) for d in range(1, 8)]
    for device in partners:
        pl.semaphore_signal(barrier, inc=1, device_id=device, device_id_type=MESH)
    pl.semaphore_wait(barrier, len(partners))

    halo = []
    places = (
        ((3, 0), (0, 6), (west, lat)),
        ((0, 6), (3, 0), (lon, south)),
        ((0, 0), (3, 6), (west, south)),
    )
    for n, (source, target, device) in enumerate(places):
        for m, (field, window) in enumerate(((x_ref, xw), (cot_ref, cw))):
            halo.append(copy(
                field.at[pl.ds(source[0], 3), pl.ds(source[1], 6)],
                window.at[pl.ds(target[0], 3), pl.ds(target[1], 6)],
                HALO + 3 * n + m, device,
            ))
        halo.append(copy(pad_hbm, pads.at[n], HALO + 3 * n + 2, device))
    for made in halo:
        made.start()
    for name in ("rel", "bias"):
        loads[name].wait()

    token = iota((WT, WT), 0)
    order = (iota((WT, WT), 1) == (token % 2) * 72 + token // 2).astype(BF16)
    rel = rel_ref[...]
    low = mm(mm(order, (rel & 255).astype(F32).astype(BF16), NT).astype(BF16), order, NT)
    high = mm(mm(order, (rel >> 8).astype(F32).astype(BF16), NT).astype(BF16), order, NT)
    relt[...] = jnp.zeros((WT, 256), I32)
    relt[:, :WT] = (high * 256.0 + low).astype(I32)
    tab[...] = jnp.zeros((HEADS, 1, 768), F32)
    for head in range(HEADS):
        tab[head, :, :NBIAS] = bias_ref[head:head + 1, :]

    def gather_heads(index, put):
        lane, chunk = index & 127, index >> 7
        inside = [chunk == c for c in range(6)]
        for head in range(HEADS):
            found = jnp.zeros(index.shape, F32)
            for c in range(6):
                row = jnp.broadcast_to(tab[head, :, 128 * c:128 * c + 128], index.shape)
                taken = jnp.take_along_axis(row, lane, axis=1, mode="promise_in_bounds")
                found = jnp.where(inside[c], taken, found)
            put(head, found)

    def lookup(step, carry):
        rows = pl.ds(pl.multiple_of(8 * step, 8), 8)

        def put(head, found):
            bias[head, rows, 0:128] = found

        gather_heads(relt[rows, 0:128], put)
        return carry

    lax.fori_loop(0, WT // 8, lookup, 0)
    rest_index = relt[:, 128:256].T
    for part in range(2):
        edge[part] = rest_index[0:16, 0:128] if part == 0 else jnp.concatenate(
            [rest_index[0:16, 128:WT], jnp.zeros((16, 256 - WT), I32)], axis=1
        )

    def lookup_rest(step, carry):
        part, half = step // 2, pl.ds(pl.multiple_of(8 * (step % 2), 8), 8)

        def put(head, found):
            edge_bias[head, part, half, :] = found

        gather_heads(edge[part, half, :], put)
        return carry

    lax.fori_loop(0, 4, lookup_rest, 0)
    for head in range(HEADS):
        bias[head, 0:128, 128:WT] = edge_bias[head, 0].T
        bias[head, 128:WT, 128:WT] = edge_bias[head, 1].T[0:16, :]

    for made in halo:
        made.wait_recv()
    for name in ("pad", "x", "cot", "gain", "wqkv", "wout"):
        loads[name].wait()

    padf[...] = jnp.zeros((32, 128), F32)
    padf[0:6, 0:12] = pad_ref[...].astype(F32)
    for n in range(3):
        padf[8 * n + 8:8 * n + 14, 0:12] = pads[n].astype(F32)

    def spot(token_at):
        row, col = token_at // 24, (token_at % 24) // 2
        slot = (row >= 3).astype(I32) * 2 + (col >= 6).astype(I32)
        return row, slot, row + jnp.where(row < 3, 3, -3), col + jnp.where(col < 6, 6, -6)

    row, slot, source_row, unused = spot(iota((WT, 32), 0))
    row_pick = (iota((WT, 32), 1) == slot * 8 + source_row).astype(BF16)
    unused, unused, unused, source_col = spot(iota((WT, 128), 0))
    picked = mm(row_pick, padf[...].astype(BF16))
    valid = jnp.sum(jnp.where(iota((WT, 128), 1) == source_col, picked, 0.0), axis=1, keepdims=True)
    key, query = iota((WT, WT), 0), iota((WT, WT), 1)
    same_group = ((key >= 72) == (query >= 72)) | (lat != 15)
    allow[...] = (same_group & ((valid > 0.5) | (key == query))).astype(F32)

    tokens = xw[...].astype(F32).reshape(WT, FEAT)
    center = tokens - jnp.mean(tokens, axis=-1, keepdims=True)
    variance = jnp.mean(center * center, axis=-1, keepdims=True)
    inv_std = lax.rsqrt(variance + EPSILON)
    standard = center * inv_std
    std[...] = standard
    istd[...] = inv_std
    normed = (standard * gain_ref[...]).astype(BF16)
    nrm[...] = normed
    nrmt[...] = normed.T
    cotf[...] = cw[...].reshape(WT, FEAT)
    proj[...] = mm(nrm[...], wqkv_ref[...]).astype(BF16)
    projt[...] = proj[...].T
    gatt[...] = mm(cotf[...], wout_ref[...], NT).astype(BF16)
    gattt[...] = gatt[...].T

    def heads(group, carry):
        lanes = pl.ds(pl.multiple_of(group * 128, 128), 128)
        lanes_k = pl.ds(pl.multiple_of(FEAT + group * 128, 128), 128)
        lanes_v = pl.ds(pl.multiple_of(2 * FEAT + group * 128, 128), 128)
        q_group, k_group, v_group = proj[:, lanes], proj[:, lanes_k], proj[:, lanes_v]
        ga_group = gatt[:, lanes]
        lane_head = iota((1, 128), 1) // HEAD_SIZE
        for j in range(4):
            head = group * 4 + j
            rows = pl.ds(pl.multiple_of(head * HEAD_SIZE, HEAD_SIZE), HEAD_SIZE)
            rows_k = pl.ds(pl.multiple_of(FEAT + head * HEAD_SIZE, HEAD_SIZE), HEAD_SIZE)
            rows_v = pl.ds(pl.multiple_of(2 * FEAT + head * HEAD_SIZE, HEAD_SIZE), HEAD_SIZE)
            mine = (lane_head == j).astype(F32).astype(BF16)
            scores = mm(k_group * mine, q_group, NT) * SCORE_SCALE
            scores = jnp.where(allow[...] > 0.5, scores + bias[head], MASKED)
            exponent = jnp.exp(scores - jnp.max(scores, axis=0, keepdims=True))
            probs = exponent * (1.0 / jnp.sum(exponent, axis=0, keepdims=True))
            probs_b = probs.astype(BF16)
            attt[rows, :] = mm(projt[rows_v, :], probs_b).astype(BF16)
            gradt[rows_v, :] = mm(gattt[rows, :], probs_b, NT).astype(BF16)
            grad_probs = mm(v_group * mine, ga_group, NT)
            inner = jnp.sum(probs * grad_probs, axis=0, keepdims=True)
            grad_scores = probs * (grad_probs - inner)
            ds[head] = grad_scores
            grad_b = grad_scores.astype(BF16)
            gradt[rows, :] = (mm(projt[rows_k, :], grad_b) * SCORE_SCALE).astype(BF16)
            gradt[rows_k, :] = (mm(projt[rows, :], grad_b, NT) * SCORE_SCALE).astype(BF16)
        return carry

    lax.fori_loop(0, 4, heads, 0)

    def half_block(which, block):
        if block < 3:
            rows = pl.ds(pl.multiple_of(block * FEAT + which * 256, 256), 256)
            out = mm(nrmt[...], gradt[rows, :], NT)
            return out[:, 0:128], out[:, 128:256]
        rows = pl.ds(pl.multiple_of(which * 256, 256), 256)
        out = mm(attt[rows, :], cotf[...])
        return (
            jnp.concatenate([out[:, 0:128], out[:, 128:256]], axis=0),
            jnp.concatenate([out[:, 256:384], out[:, 384:512]], axis=0),
        )

    core_copies = []
    for block in range(4):
        first, second = half_block(1 - core, block)
        sib_send[0, 512 * block:512 * block + 512, :] = first.astype(BF16)
        sib_send[1, 512 * block:512 * block + 512, :] = second.astype(BF16)
        made = copy(
            sib_send.at[:, pl.ds(512 * block, 512)], sib_recv.at[:, pl.ds(512 * block, 512)],
            CORE + block, sibling,
        )
        made.start()
        core_copies.append(made)
    for block in range(4):
        first, second = half_block(core, block)
        own_half[0, 512 * block:512 * block + 512, :] = first
        own_half[1, 512 * block:512 * block + 512, :] = second
    for block in range(4):
        core_copies[block].wait_recv()

        def add_block(step, carry, block=block):
            rows = pl.ds(pl.multiple_of(512 * block + 128 * step, 128), 128)
            pay[:, rows, :] = (own_half[:, rows, :] + sib_recv[:, rows, :].astype(F32)).astype(BF16)
            return carry

        lax.fori_loop(0, 4, add_block, 0)

    def rows_of(start, count):
        return pl.ds(pl.multiple_of(start, 16), count)

    major, minor = (x, y), (y, x)
    at_major, at_minor = (at_x, at_y), (at_y, at_x)
    rs1 = [[], []]
    for d in range(1, 4):
        for p in range(2):
            to = (major[p] + d) % 4
            made = copy(pay.at[p, rows_of(512 * to, 512)], r1.at[p, d - 1], RS1 + 3 * p + d - 1, at_major[p](to))
            made.start()
            rs1[p].append(made)

    ones = iota((96, WT), 0)
    sub = iota((8, WT), 0)

    def scatter(step, total):
        rows = pl.ds(pl.multiple_of(8 * step, 8), 8)
        indices = relt[rows, 0:WT]
        for k in range(8):
            index = indices[k:k + 1, :]
            upper = (ones == (index >> 3)).astype(F32).astype(BF16)
            match = sub == (index & 7)
            pieces = [
                jnp.where(match, jnp.broadcast_to(ds[h, rows, :][k:k + 1, :], (8, WT)), 0.0)
                for h in range(HEADS)
            ]
            total = total + mm(upper, jnp.concatenate(pieces, axis=0).astype(BF16), NT)
        return total

    total = lax.fori_loop(0, WT // 8, scatter, jnp.zeros((96, 128), F32))
    tsum[...] = total.T
    spread = (iota((96, 768), 1) // 8 == iota((96, 768), 0)).astype(F32)
    wide = lax.dot_general(tsum[...], spread, NN, precision=lax.Precision.HIGHEST, preferred_element_type=F32)
    wide = jnp.where(iota((128, 768), 1) % 8 == iota((128, 768), 0) % 8, wide, 0.0)
    wide = jnp.sum(wide.reshape(HEADS, 8, 768), axis=1)
    tb[...] = jnp.zeros((128, 128), F32)
    for c in range(6):
        tb[16 * c:16 * c + 16, :] = wide[:, 128 * c:128 * c + 128]

    grad_normed = mm(gradt[...].T, wqkv_ref[...], NT)
    standard = std[...]
    grad_gain = jnp.sum(grad_normed * standard, axis=0, keepdims=True)
    for c in range(4):
        tb[96 + c:97 + c, :] = grad_gain[:, 128 * c:128 * c + 128]
    tcore = copy(tb.at[rows_of(64 * (1 - core), 64)], rt0, TCORE, sibling)
    tcore.start()
    grad_hat = grad_normed * gain_ref[...]
    grad_in = istd[...] * (
        grad_hat
        - jnp.mean(grad_hat, axis=-1, keepdims=True)
        - standard * jnp.mean(grad_hat * standard, axis=-1, keepdims=True)
    )
    back_send[...] = grad_in.astype(BF16).reshape(6, 12, 2, FEAT)
    back = []
    returns = (
        ((0, 6), (3, 0), (east, lat)),
        ((3, 0), (0, 6), (lon, north)),
        ((3, 6), (0, 0), (east, north)),
    )
    for n, (source, target, device) in enumerate(returns):
        made = copy(
            back_send.at[pl.ds(source[0], 3), pl.ds(source[1], 6)],
            back_recv.at[pl.ds(target[0], 3), pl.ds(target[1], 6)],
            BACK + n, device,
        )
        made.start()
        back.append(made)
    ginf[...] = grad_in.reshape(6, 12, 2, FEAT)

    rs2 = [[], []]
    for p in range(2):
        for made in rs1[p]:
            made.wait_recv()

        def add_one(step, carry, p=p):
            rows = pl.ds(pl.multiple_of(128 * step, 128), 128)
            own = pl.ds(pl.multiple_of(512 * major[p] + 128 * step, 128), 128)
            value = pay[p, own, :].astype(F32)
            for d in range(3):
                value = value + r1[p, d, rows, :].astype(F32)
            s1[p, rows, :] = value.astype(BF16)
            return carry

        lax.fori_loop(0, 4, add_one, 0)
        for d in range(1, 4):
            to = (minor[p] + d) % 4
            made = copy(s1.at[p, rows_of(128 * to, 128)], r2.at[p, d - 1], RS2 + 3 * p + d - 1, at_minor[p](to))
            made.start()
            rs2[p].append(made)

    tcore.wait_recv()
    t1[...] = tb[rows_of(64 * core, 64), :] + rt0[...]
    tx = []
    for d in range(1, 4):
        to = (x + d) % 4
        made = copy(t1.at[rows_of(16 * to, 16)], rt1.at[d - 1], TX + d - 1, at_x(to))
        made.start()
        tx.append(made)

    rs3 = [[], []]
    for p in range(2):
        for made in rs2[p]:
            made.wait_recv()
        value = s1[p, rows_of(128 * minor[p], 128), :].astype(F32)
        for d in range(3):
            value = value + r2[p, d].astype(F32)
        s2[p] = value.astype(BF16)
        for d in range(1, 8):
            to = (z + d) % 8
            made = copy(s2.at[p, rows_of(16 * to, 16)], r3.at[p, d - 1], RS3 + 7 * p + d - 1, at_z(to))
            made.start()
            rs3[p].append(made)

    for made in tx:
        made.wait_recv()
    value = t1[rows_of(16 * x, 16), :]
    for d in range(3):
        value = value + rt1[d]
    t2[...] = value
    ty = []
    for d in range(1, 4):
        made = copy(t2, rt2.at[d - 1], TY + d - 1, at_y((y + d) % 4))
        made.start()
        ty.append(made)

    base1 = [512 * major[p] for p in range(2)]
    base2 = [base1[p] + 128 * minor[p] for p in range(2)]
    base3 = [base2[p] + 16 * z for p in range(2)]

    def gather(p, base, count, index, device):
        part = big_ref.at[core, p, rows_of(base, count)]
        made = copy(part, part, index, device)
        made.start()
        return made

    ag1 = [[], []]
    for p in range(2):
        for made in rs3[p]:
            made.wait_recv()
        value = s2[p, rows_of(16 * z, 16), :].astype(F32)
        for d in range(7):
            value = value + r3[p, d].astype(F32)
        big_ref[core, p, rows_of(base3[p], 16), :] = value.astype(BF16)
        for d in range(1, 8):
            ag1[p].append(gather(p, base3[p], 16, AG1 + 7 * p + d - 1, at_z((z + d) % 8)))

    for made in ty:
        made.wait_recv()
    value = t2[...]
    for d in range(3):
        value = value + rt2[d]
    t3[...] = value
    tz = []
    for d in range(1, 8):
        made = copy(t3, rt3.at[d - 1], TZ + d - 1, at_z((z + d) % 8))
        made.start()
        tz.append(made)

    ag2 = [[], []]
    for p in range(2):
        for made in ag1[p]:
            made.wait_recv()
        for d in range(1, 4):
            ag2[p].append(gather(p, base2[p], 128, AG2 + 3 * p + d - 1, at_minor[p]((minor[p] + d) % 4)))

    for made in tz:
        made.wait_recv()
    value = t3[...]
    for d in range(7):
        value = value + rt3[d]
    trow = 64 * core + 16 * x
    tf[rows_of(trow, 16), :] = value * GRAD_SCALE
    txg = []
    for d in range(1, 4):
        made = copy(tf.at[rows_of(trow, 16)], tf.at[rows_of(trow, 16)], TXG + d - 1, at_x((x + d) % 4))
        made.start()
        txg.append(made)

    ag3 = [[], []]
    sib = []

    def forward(p, block, index):
        part = big_ref.at[core, p, rows_of(512 * block, 512)]
        made = copy(part, part, index, sibling)
        made.start()
        sib.append(made)

    for p in range(2):
        for made in ag2[p]:
            made.wait_recv()
        for d in range(1, 4):
            ag3[p].append(gather(p, base1[p], 512, AG3 + 3 * p + d - 1, at_major[p]((major[p] + d) % 4)))
        forward(p, major[p], SIB + 4 * p)

    for made in back:
        made.wait_recv()
    gin_ref[0:3, 0:6] = back_recv[0:3, 0:6].astype(F32)
    gin_ref[0:3, 6:12] = back_recv[0:3, 6:12].astype(F32)
    gin_ref[3:6, 0:6] = back_recv[3:6, 0:6].astype(F32)
    gin_ref[3:6, 6:12] = ginf[0:3, 0:6]

    for made in txg:
        made.wait_recv()
    thalf = tf.at[rows_of(64 * core, 64)]
    tsib = copy(thalf, thalf, TSIB, sibling)
    tsib.start()

    for d in range(1, 4):
        for p in range(2):
            ag3[p][d - 1].wait_recv()
            forward(p, (major[p] + 4 - d) % 4, SIB + 4 * p + d)

    tsib.wait_recv()
    for c in range(5):
        table_ref[:, 128 * c:128 * c + 128] = tf[16 * c:16 * c + 16, :]
    table_ref[:, 640:NBIAS] = tf[80:96, 0:NBIAS - 640]
    for c in range(4):
        ggain_ref[:, 128 * c:128 * c + 128] = tf[96 + c:97 + c, :]

    for made in sib:
        made.wait_recv()
    for made in started:
        made.wait_send()


def widen(big, gin, table, gain, gin_out, gain_out, wqkv_out, wout_out, table_out, wqkv, wout, sem):
    made = [
        pltpu.make_async_copy(gin, gin_out, sem.at[0]),
        pltpu.make_async_copy(gain, gain_out, sem.at[1]),
        pltpu.make_async_copy(table, table_out, sem.at[2]),
    ]
    for one in made:
        one.start()
    for step in range(4):
        rows = slice(128 * step, 128 * step + 128)
        for block in range(3):
            for core in range(2):
                for p in range(2):
                    lanes = slice(512 * block + 256 * core + 128 * p, 512 * block + 256 * core + 128 * p + 128)
                    source = slice(512 * block + 128 * step, 512 * block + 128 * step + 128)
                    wqkv[rows, lanes] = big[core, p, source, :].astype(F32) * GRAD_SCALE
        one = pltpu.make_async_copy(wqkv.at[pl.ds(128 * step, 128)], wqkv_out.at[pl.ds(128 * step, 128)], sem.at[3 + step])
        one.start()
        made.append(one)
        core, half = step // 2, step % 2
        for p in range(2):
            for u in range(2):
                source = slice(1536 + 256 * u + 128 * half, 1536 + 256 * u + 128 * half + 128)
                wout[rows, 256 * p + 128 * u:256 * p + 128 * u + 128] = big[core, p, source, :].astype(F32) * GRAD_SCALE
        one = pltpu.make_async_copy(wout.at[pl.ds(128 * step, 128)], wout_out.at[pl.ds(128 * step, 128)], sem.at[7 + step])
        one.start()
        made.append(one)
    for one in made:
        one.wait()


def per_device(inputs, cotangent, pad_mask, rel_index, bias_table, ln_gain, w_qkv, w_out):
    vmem = pl.BlockSpec(memory_space=pltpu.VMEM)
    hbm = pl.BlockSpec(memory_space=pltpu.HBM)
    big, grad_in, table, gain = pl.pallas_call(
        body,
        out_shape=(
            jax.ShapeDtypeStruct((2, 2, 2048, 128), BF16),
            jax.ShapeDtypeStruct((6, 12, 2, FEAT), F32),
            jax.ShapeDtypeStruct((HEADS, NBIAS), F32),
            jax.ShapeDtypeStruct((1, FEAT), F32),
        ),
        in_specs=[hbm] * 8,
        out_specs=[vmem] * 4,
        scratch_shapes=[
            pltpu.VMEM((6, 12), I32),
            pltpu.VMEM((WT, WT), I32),
            pltpu.VMEM((HEADS, NBIAS), F32),
            pltpu.VMEM((1, FEAT), F32),
            pltpu.VMEM((FEAT, 3 * FEAT), BF16),
            pltpu.VMEM((FEAT, FEAT), BF16),
            pltpu.VMEM((6, 12, 2, FEAT), BF16),
            pltpu.VMEM((6, 12, 2, FEAT), BF16),
            pltpu.VMEM((3, 6, 12), I32),
            pltpu.VMEM((32, 128), F32),
            pltpu.VMEM((WT, 256), I32),
            pltpu.VMEM((HEADS, 1, 768), F32),
            pltpu.VMEM((2, 16, 128), I32),
            pltpu.VMEM((HEADS, 2, 16, 128), F32),
            pltpu.VMEM((HEADS, WT, WT), F32),
            pltpu.VMEM((WT, WT), F32),
            pltpu.VMEM((WT, FEAT), F32),
            pltpu.VMEM((WT, 1), F32),
            pltpu.VMEM((WT, FEAT), BF16),
            pltpu.VMEM((FEAT, WT), BF16),
            pltpu.VMEM((WT, FEAT), BF16),
            pltpu.VMEM((WT, 3 * FEAT), BF16),
            pltpu.VMEM((3 * FEAT, WT), BF16),
            pltpu.VMEM((WT, FEAT), BF16),
            pltpu.VMEM((FEAT, WT), BF16),
            pltpu.VMEM((FEAT, WT), BF16),
            pltpu.VMEM((3 * FEAT, WT), BF16),
            pltpu.VMEM((HEADS, WT, WT), F32),
            pltpu.VMEM((2, 2048, 128), BF16),
            pltpu.VMEM((2, 2048, 128), BF16),
            pltpu.VMEM((2, 2048, 128), F32),
            pltpu.VMEM((2, 2048, 128), BF16),
            pltpu.VMEM((2, 3, 512, 128), BF16),
            pltpu.VMEM((2, 512, 128), BF16),
            pltpu.VMEM((2, 3, 128, 128), BF16),
            pltpu.VMEM((2, 128, 128), BF16),
            pltpu.VMEM((2, 7, 16, 128), BF16),
            pltpu.VMEM((128, 96), F32),
            pltpu.VMEM((128, 128), F32),
            pltpu.VMEM((64, 128), F32),
            pltpu.VMEM((64, 128), F32),
            pltpu.VMEM((3, 16, 128), F32),
            pltpu.VMEM((16, 128), F32),
            pltpu.VMEM((3, 16, 128), F32),
            pltpu.VMEM((16, 128), F32),
            pltpu.VMEM((7, 16, 128), F32),
            pltpu.VMEM((128, 128), F32),
            pltpu.VMEM((6, 12, 2, FEAT), BF16),
            pltpu.VMEM((6, 12, 2, FEAT), BF16),
            pltpu.VMEM((6, 12, 2, FEAT), F32),
            pltpu.SemaphoreType.DMA((SEMS,)),
            pltpu.SemaphoreType.DMA((SEMS,)),
            pltpu.SemaphoreType.DMA((8,)),
        ],
        compiler_params=pltpu.CompilerParams(
            collective_id=0, has_side_effects=True, vmem_limit_bytes=48 * 1024 * 1024
        ),
    )(
        *(
            pltpu.with_memory_space_constraint(one, pltpu.HBM)
            for one in (
                inputs.transpose(1, 2, 0, 3),
                cotangent.transpose(1, 2, 0, 3),
                pad_mask,
                rel_index,
                bias_table.T,
                ln_gain.reshape(1, FEAT),
                w_qkv,
                w_out,
            )
        )
    )
    grad_in, gain, wqkv, wout, table = pl.pallas_call(
        widen,
        out_shape=(
            jax.ShapeDtypeStruct((6, 12, 2, FEAT), F32),
            jax.ShapeDtypeStruct((1, FEAT), F32),
            jax.ShapeDtypeStruct((FEAT, 3 * FEAT), F32),
            jax.ShapeDtypeStruct((FEAT, FEAT), F32),
            jax.ShapeDtypeStruct((HEADS, NBIAS), F32),
        ),
        in_specs=[vmem] * 4,
        out_specs=[hbm] * 5,
        scratch_shapes=[
            pltpu.VMEM((FEAT, 3 * FEAT), F32),
            pltpu.VMEM((FEAT, FEAT), F32),
            pltpu.SemaphoreType.DMA((11,)),
        ],
        compiler_params=pltpu.CompilerParams(vmem_limit_bytes=24 * 1024 * 1024),
    )(big, grad_in, table, gain)
    return grad_in.transpose(2, 0, 1, 3), gain.reshape(FEAT), wqkv, wout, table.T


def solution(mesh):
    in_specs = (
        P(None, "lat", "lon", None),
        P(None, "lat", "lon", None),
        P("lat", "lon"),
        P(),
        P(),
        P(),
        P(),
        P(),
    )
    out_specs = (P(None, "lat", "lon", None), P(), P(), P(), P())
    return jax.shard_map(
        per_device, mesh=mesh, in_specs=in_specs, out_specs=out_specs, check_vma=False
    )
```

```python
import jax
import jax.numpy as jnp
from jax import lax
from jax.experimental import pallas as pl
from jax.experimental.pallas import tpu as pltpu
from jax.sharding import PartitionSpec as P

F32 = jnp.float32
BF16 = jnp.bfloat16
I32 = jnp.int32
MESH = pl.DeviceIdType.MESH

EPSILON = 1e-05
MASKED = -30000.0
WT = 144
FEAT = 512
HEADS = 16
HEAD_SIZE = 32
NBIAS = 759
SCORE_SCALE = HEAD_SIZE ** (-0.5)
GRAD_SCALE = 36864.0 ** (-0.5)

NN = (((1,), (0,)), ((), ()))
NT = (((1,), (1,)), ((), ()))

XS, COTS, PADS, PAIR, RS1, RS2, RS3, AG1, AG2, AG3, SIB = 0, 1, 2, 5, 9, 12, 13, 14, 15, 16, 17
TX, TY, TZ, TXG, TSIB, BACK = 18, 19, 20, 21, 22, 23
SENDS = 24
R_RS1, R_RS2, R_RS3, R_AG1, R_AG2, R_AG3, R_SIB = 9, 12, 14, 15, 16, 19, 25
R_TX, R_TY, R_TZ, R_TXG, R_TSIB, R_BACK = 26, 27, 28, 29, 30, 31
RECVS = 32

RING4 = (2, 1, 3)
RING8 = (4, 3, 5, 2, 6, 1, 7)


def mm(a, b, dims=NN):
    return lax.dot_general(a, b, dims, preferred_element_type=F32)


def iota(shape, dim):
    return lax.broadcasted_iota(I32, shape, dim)


def body(
    x_ref, cot_ref, pad_hbm, rel_hbm, bias_hbm, gain_hbm, wqkv_hbm, wout_hbm,
    big_ref, gin_ref, table_ref, ggain_ref,
    pad_ref, rel_ref, bias_ref, gain_ref, wq, wo, wqt, wot,
    xw, cw, pads, padf, relt, tab, edge, edge_bias, bias, validb, allow, std, istd, nrm, nrmt, cotf,
    proj, projt, gatt, gattt, attt, gradt, gnat, probs, ds, gn_send, gn_recv,
    pay, r1, s1, r2, s2, r3, g1,
    tb, rt1, t2, rt2, t3, rt3, tf, tf_recv,
    back_send, back_recv, ginf, ssem, rsem, lsem,
):
    lon = lax.axis_index("lon")
    lat = lax.axis_index("lat")
    z, xhi = lon // 2, lon % 2
    xlo, rest = lat // 8, lat % 8
    y, core = rest // 2, rest % 2
    x = xhi * 2 + xlo

    def at_x(value):
        return (z * 2 + value // 2, (value % 2) * 8 + rest)

    def at_y(value):
        return (lon, xlo * 8 + value * 2 + core)

    def at_z(value):
        return (value * 2 + xhi, lat)

    sibling = (lon, xlo * 8 + y * 2 + (1 - core))
    west, east = (lon + 15) % 16, (lon + 1) % 16
    south, north = (lat + 15) % 16, (lat + 1) % 16

    def send(src, dst, out, into, device):
        pltpu.make_async_remote_copy(
            src_ref=src, dst_ref=dst, send_sem=ssem.at[out], recv_sem=rsem.at[into],
            device_id=device, device_id_type=MESH,
        ).start()

    def arrived(bytes_of, into):
        pltpu.make_async_copy(bytes_of, bytes_of, rsem.at[into]).wait()

    def left(bytes_of, out):
        pltpu.make_async_copy(bytes_of, bytes_of, ssem.at[out]).wait()

    def span(start, count):
        return pl.ds(pl.multiple_of(start, 16), count)

    loads = {}
    heads_at = 256 * core
    parts = [
        ("rel", rel_hbm, rel_ref),
        ("bias", bias_hbm.at[pl.ds(pl.multiple_of(8 * core, 8), 8)], bias_ref),
        ("x", x_ref.at[pl.ds(3, 3), pl.ds(6, 6)], xw.at[pl.ds(0, 3), pl.ds(0, 6)]),
        ("cot", cot_ref.at[pl.ds(3, 3), pl.ds(6, 6)], cw.at[pl.ds(0, 3), pl.ds(0, 6)]),
        ("pad", pad_hbm, pad_ref),
        ("gain", gain_hbm, gain_ref),
        ("wo", wout_hbm.at[span(heads_at, 256)], wo),
    ]
    for block in range(3):
        lanes = pl.ds(pl.multiple_of(FEAT * block + heads_at, 128), 256)
        parts.append(("wq%d" % block, wqkv_hbm.at[:, lanes], wq.at[:, pl.ds(256 * block, 256)]))
    for n, (name, src, dst) in enumerate(parts):
        loads[name] = pltpu.make_async_copy(src, dst, lsem.at[n])
        loads[name].start()

    barrier = pltpu.get_barrier_semaphore()
    partners = [sibling, (west, lat), (lon, south), (west, south), (east, lat), (lon, north), (east, north)]
    partners += [at_x((x + d) % 4) for d in RING4]
    partners += [at_y((y + d) % 4) for d in RING4]
    partners += [at_z((z + d) % 8) for d in RING8]
    for device in partners:
        pl.semaphore_signal(barrier, inc=1, device_id=device, device_id_type=MESH)
    pl.semaphore_wait(barrier, len(partners))

    places = (
        ((0, 0), (3, 6), (west, south)),
        ((3, 0), (0, 6), (west, lat)),
        ((0, 6), (3, 0), (lon, south)),
    )
    three = pl.ds(0, 9)

    def send_quarters(field, window, index):
        for source, target, device in places:
            send(
                field.at[pl.ds(source[0], 3), pl.ds(source[1], 6)],
                window.at[pl.ds(target[0], 3), pl.ds(target[1], 6)],
                index, index, device,
            )

    send_quarters(x_ref, xw, XS)
    for n, (unused, unused, device) in enumerate(places):
        send(pad_hbm, pads.at[n], PADS + n, PADS + n, device)
    send_quarters(cot_ref, cw, COTS)

    for name in ("rel", "bias"):
        loads[name].wait()
    token = iota((WT, WT), 0)
    order = (iota((WT, WT), 1) == (token % 2) * 72 + token // 2).astype(BF16)
    rel = rel_ref[...]
    low = mm(mm(order, (rel & 255).astype(F32).astype(BF16), NT).astype(BF16), order, NT)
    high = mm(mm(order, (rel >> 8).astype(F32).astype(BF16), NT).astype(BF16), order, NT)
    relt[...] = jnp.zeros((WT, 256), I32)
    relt[:, :WT] = (high * 256.0 + low).astype(I32)
    tab[...] = jnp.zeros((8, 1, 768), F32)
    for head in range(8):
        tab[head, :, :NBIAS] = bias_ref[head:head + 1, :]

    def gather_heads(index, put):
        lane, chunk = index & 127, index >> 7
        inside = [chunk == c for c in range(6)]
        for head in range(8):
            found = jnp.zeros(index.shape, F32)
            for c in range(6):
                row = jnp.broadcast_to(tab[head, :, 128 * c:128 * c + 128], index.shape)
                taken = jnp.take_along_axis(row, lane, axis=1, mode="promise_in_bounds")
                found = jnp.where(inside[c], taken, found)
            put(head, found)

    def lookup(step, carry):
        rows = pl.ds(pl.multiple_of(8 * step, 8), 8)

        def put(head, found):
            bias[head, rows, 0:128] = found

        gather_heads(relt[rows, 0:128], put)
        return carry

    lax.fori_loop(0, WT // 8, lookup, 0)
    rest_index = relt[:, 128:256].T
    edge[0] = rest_index[0:16, 0:128]
    edge[1] = jnp.concatenate([rest_index[0:16, 128:WT], jnp.zeros((16, 256 - WT), I32)], axis=1)

    def lookup_rest(step, carry):
        part, half = step // 2, pl.ds(pl.multiple_of(8 * (step % 2), 8), 8)

        def put(head, found):
            edge_bias[head, part, half, :] = found

        gather_heads(edge[part, half, :], put)
        return carry

    lax.fori_loop(0, 4, lookup_rest, 0)
    for head in range(8):
        bias[head, 0:128, 128:WT] = edge_bias[head, 0].T
        bias[head, 128:WT, 128:WT] = edge_bias[head, 1].T[0:16, :]

    for name in ("wo", "wq0", "wq1", "wq2", "pad", "x", "cot", "gain"):
        loads[name].wait()
    wot[...] = wo[...].T
    for block in range(3):
        wqt[256 * block:256 * block + 256, :] = wq[:, 256 * block:256 * block + 256].T

    arrived(xw.at[:, three], XS)
    tokens = xw[...].astype(F32).reshape(WT, FEAT)
    center = tokens - jnp.mean(tokens, axis=-1, keepdims=True)
    variance = jnp.mean(center * center, axis=-1, keepdims=True)
    inv_std = lax.rsqrt(variance + EPSILON)
    standard = center * inv_std
    std[...] = standard
    istd[...] = inv_std
    nrm[0] = (standard * gain_ref[...]).astype(BF16)
    send(nrm.at[0], nrm.at[1], PAIR, PAIR, sibling)

    def project(w):
        proj[w] = mm(nrm[w], wq[...]).astype(BF16)
        projt[w] = proj[w].T
        nrmt[w] = nrm[w].T

    project(0)

    for n in range(3):
        arrived(pads.at[n], PADS + n)
    padf[...] = jnp.zeros((32, 128), F32)
    padf[0:6, 0:12] = pad_ref[...].astype(F32)
    for n, slot_at in enumerate((3, 1, 2)):
        padf[8 * slot_at:8 * slot_at + 6, 0:12] = pads[n].astype(F32)

    def spot(token_at):
        row, col = token_at // 24, (token_at % 24) // 2
        slot = (row >= 3).astype(I32) * 2 + (col >= 6).astype(I32)
        return slot, row + jnp.where(row < 3, 3, -3), col + jnp.where(col < 6, 6, -6)

    slot, source_row, unused = spot(iota((WT, 32), 0))
    row_pick = (iota((WT, 32), 1) == slot * 8 + source_row).astype(BF16)
    unused, unused, source_col = spot(iota((WT, 128), 0))
    picked = mm(row_pick, padf[...].astype(BF16))
    valid = jnp.sum(jnp.where(iota((WT, 128), 1) == source_col, picked, 0.0), axis=1, keepdims=True)
    validb[0] = jnp.broadcast_to(valid, (WT, 128)).astype(BF16)
    send(validb.at[0], validb.at[1], PAIR + 1, PAIR + 1, sibling)

    def see(w):
        key, query = iota((WT, WT), 0), iota((WT, WT), 1)
        across = lat + w * (1 - 2 * core) == 15
        same_group = ((key >= 72) == (query >= 72)) | jnp.logical_not(across)
        valid_key = validb[w].astype(F32)[:, 0:1] > 0.5
        allow[w] = (same_group & (valid_key | (key == query))).astype(F32)

    see(0)
    arrived(cw.at[:, three], COTS)
    cotf[0] = cw[...].reshape(WT, FEAT)
    send(cotf.at[0], cotf.at[1], PAIR + 2, PAIR + 2, sibling)

    def project_cot(w):
        gatt[w] = mm(cotf[w], wot[...]).astype(BF16)
        gattt[w] = gatt[w].T

    project_cot(0)

    def picks(group):
        lanes = [pl.ds(pl.multiple_of(256 * b + group * 128, 128), 128) for b in range(3)]
        head_of_lane = iota((1, 128), 1) // HEAD_SIZE
        mine = [(head_of_lane == j).astype(F32).astype(BF16) for j in range(4)]
        return lanes, mine

    def rows_of(head):
        return [pl.ds(pl.multiple_of(256 * b + head * HEAD_SIZE, HEAD_SIZE), HEAD_SIZE) for b in range(3)]

    def forward_heads(w):
        def step(group, carry):
            lanes, mine = picks(group)
            k_group, ga_group = proj[w, :, lanes[1]], gatt[w, :, lanes[0]]
            qt_group = projt[w, span(128 * group, 128), :]
            grad_values = jnp.zeros((WT, 128), F32)
            for j in range(4):
                head = group * 4 + j
                rows = rows_of(head)
                scores = mm(k_group * mine[j], qt_group) * SCORE_SCALE
                scores = jnp.where(allow[w] > 0.5, scores + bias[head], MASKED)
                exponent = jnp.exp(scores - jnp.max(scores, axis=0, keepdims=True))
                prob = exponent * (1.0 / jnp.sum(exponent, axis=0, keepdims=True))
                probs[w, head] = prob
                prob_b = prob.astype(BF16)
                attt[w, rows[0], :] = mm(projt[w, rows[2], :], prob_b).astype(BF16)
                grad_values = grad_values + mm(prob_b, ga_group * mine[j])
            gnat[w, :, lanes[2]] = grad_values.astype(BF16)
            return carry

        lax.fori_loop(0, 2, step, 0)

    def backward_heads(w):
        def step(group, carry):
            lanes, mine = picks(group)
            q_group, v_group = proj[w, :, lanes[0]], proj[w, :, lanes[2]]
            gat_group = gattt[w, span(128 * group, 128), :]
            grad_keys = jnp.zeros((WT, 128), F32)
            for j in range(4):
                head = group * 4 + j
                rows = rows_of(head)
                prob = probs[w, head]
                grad_probs = mm(v_group * mine[j], gat_group)
                inner = jnp.sum(prob * grad_probs, axis=0, keepdims=True)
                grad_scores = prob * (grad_probs - inner)
                if w == 0:
                    ds[head] = grad_scores
                else:
                    ds[head] = ds[head] + grad_scores
                grad_b = grad_scores.astype(BF16)
                gradt[w, rows[0], :] = (mm(projt[w, rows[1], :], grad_b) * SCORE_SCALE).astype(BF16)
                grad_keys = grad_keys + mm(grad_b, q_group * mine[j])
            gnat[w, :, lanes[1]] = (grad_keys * SCORE_SCALE).astype(BF16)
            return carry

        lax.fori_loop(0, 2, step, 0)

    forward_heads(0)
    arrived(nrm.at[1], PAIR)
    project(1)
    arrived(validb.at[1], PAIR + 1)
    see(1)
    arrived(cotf.at[1], PAIR + 2)
    project_cot(1)
    forward_heads(1)

    major, minor = (x, y), (y, x)
    at_major, at_minor = (at_x, at_y), (at_y, at_x)
    chunk_at = (0, 1024, 1536)
    chunk_rows = (256, 128, 128)

    def columns(block):
        lanes = slice(256 * block, 256 * block + 256)
        return mm(nrmt[0], gnat[0, :, lanes]) + mm(nrmt[1], gnat[1, :, lanes])

    def scatter_pay(e):
        count = chunk_rows[e]
        for d in RING4:
            for p in range(2):
                to = (major[p] + d) % 4
                send(
                    pay.at[p, span(chunk_at[e] + count * to, count)],
                    r1.at[p, d - 1, pl.ds(128 * e + 128 * (e > 0), count)],
                    RS1 + e, R_RS1 + e, at_major[p](to),
                )

    out = columns(2)
    for p in range(2):
        pay[p, 0:512, :] = out[:, 128 * p:128 * p + 128].astype(BF16)
    out = mm(attt[0], cotf[0]) + mm(attt[1], cotf[1])
    for p in range(2):
        for u in range(2):
            lanes = slice(256 * p + 128 * u, 256 * p + 128 * u + 128)
            pay[p, 512 + 256 * u:768 + 256 * u, :] = out[:, lanes].astype(BF16)
    scatter_pay(0)
    backward_heads(0)
    backward_heads(1)
    out = columns(1)
    for p in range(2):
        pay[p, 1024:1536, :] = out[:, 128 * p:128 * p + 128].astype(BF16)
    scatter_pay(1)
    for w in range(2):
        gnat[w, :, 0:256] = gradt[w].T
    out = columns(0)
    for p in range(2):
        pay[p, 1536:2048, :] = out[:, 128 * p:128 * p + 128].astype(BF16)
    scatter_pay(2)

    gn_send[...] = mm(gnat[1], wqt[...])
    send(gn_send, gn_recv, PAIR + 3, PAIR + 3, sibling)
    grad_normed = mm(gnat[0], wqt[...])

    ones = iota((48, WT), 0)
    sub = iota((16, WT), 0)

    def scatter(step, total):
        rows = pl.ds(pl.multiple_of(8 * step, 8), 8)
        indices = relt[rows, 0:WT]
        for k in range(8):
            index = indices[k:k + 1, :]
            upper = (ones == (index >> 4)).astype(F32).astype(BF16)
            match = sub == (index & 15)
            pieces = [
                jnp.where(match, jnp.broadcast_to(ds[h, rows, :][k:k + 1, :], (16, WT)), 0.0)
                for h in range(8)
            ]
            total = total + mm(upper, jnp.concatenate(pieces, axis=0).astype(BF16), NT)
        return total

    total = lax.fori_loop(0, WT // 8, scatter, jnp.zeros((48, 128), F32))

    for e in range(3):
        count = chunk_rows[e]
        rows = slice(128 * e + 128 * (e > 0), 128 * e + 128 * (e > 0) + count)
        arrived(r1.at[:, :, pl.ds(rows.start, count)], R_RS1 + e)
        for p in range(2):
            value = pay[p, span(chunk_at[e] + count * major[p], count), :].astype(F32)
            for d in range(3):
                value = value + r1[p, d, rows, :].astype(F32)
            s1[p, rows, :] = value.astype(BF16)
    for d in RING4:
        for p in range(2):
            to = (minor[p] + d) % 4
            send(s1.at[p, span(128 * to, 128)], r2.at[p, d - 1], RS2, R_RS2 + p, at_minor[p](to))

    arrived(gn_recv, PAIR + 3)
    grad_normed = grad_normed + gn_recv[...]
    standard = std[...]
    grad_gain = jnp.sum(grad_normed * standard, axis=0, keepdims=True)
    grad_hat = grad_normed * gain_ref[...]
    grad_in = istd[...] * (
        grad_hat
        - jnp.mean(grad_hat, axis=-1, keepdims=True)
        - standard * jnp.mean(grad_hat * standard, axis=-1, keepdims=True)
    )
    back_send[...] = grad_in.astype(BF16).reshape(6, 12, 2, FEAT)
    returns = (
        ((3, 6), (0, 0), (east, north)),
        ((0, 6), (3, 0), (east, lat)),
        ((3, 0), (0, 6), (lon, north)),
    )
    for source, target, device in returns:
        send(
            back_send.at[pl.ds(source[0], 3), pl.ds(source[1], 6)],
            back_recv.at[pl.ds(target[0], 3), pl.ds(target[1], 6)],
            BACK, R_BACK, device,
        )
    ginf[...] = grad_in.reshape(6, 12, 2, FEAT)

    for p in range(2):
        arrived(r2.at[p], R_RS2 + p)
        value = s1[p, span(128 * minor[p], 128), :].astype(F32)
        for d in range(3):
            value = value + r2[p, d].astype(F32)
        s2[p] = value.astype(BF16)
    for d in RING8:
        to = (z + d) % 8
        send(s2.at[:, span(16 * to, 16)], r3.at[d - 1], RS3, R_RS3, at_z(to))

    turned = total.T
    upper_part = turned.astype(BF16)
    lower_part = (turned - upper_part.astype(F32)).astype(BF16)
    spread = (iota((48, 768), 1) // 16 == iota((48, 768), 0)).astype(F32).astype(BF16)
    wide = mm(upper_part, spread) + mm(lower_part, spread)
    wide = jnp.where(iota((128, 768), 1) % 16 == iota((128, 768), 0) % 16, wide, 0.0)
    wide = jnp.sum(wide.reshape(8, 16, 768), axis=1)
    tb[...] = jnp.zeros((64, 128), F32)
    for c in range(6):
        tb[8 * c:8 * c + 8, :] = wide[:, 128 * c:128 * c + 128]
    for c in range(4):
        tb[48 + c:49 + c, :] = grad_gain[:, 128 * c:128 * c + 128]
    for d in RING4:
        to = (x + d) % 4
        send(tb.at[span(16 * to, 16)], rt1.at[d - 1], TX, R_TX, at_x(to))

    arrived(r3, R_RS3)
    for p in range(2):
        value = s2[p, span(16 * z, 16), :].astype(F32)
        for d in range(7):
            value = value + r3[d, p].astype(F32)
        g1[p, span(16 * z, 16), :] = value.astype(BF16)
    mine_z = g1.at[:, span(16 * z, 16)]
    for d in RING8:
        send(mine_z, mine_z, AG1, R_AG1, at_z((z + d) % 8))

    arrived(rt1, R_TX)
    value = tb[span(16 * x, 16), :]
    for d in range(3):
        value = value + rt1[d]
    t2[...] = value
    for d in RING4:
        send(t2, rt2.at[d - 1], TY, R_TY, at_y((y + d) % 4))

    base1 = [512 * major[p] for p in range(2)]
    base2 = [base1[p] + 128 * minor[p] for p in range(2)]
    arrived(pay.at[0, pl.ds(0, 224)], R_AG1)
    into2 = {1: R_AG2, 3: R_AG2 + 1, 2: R_AG2 + 2}
    into3 = {1: [R_AG3] * 4, 3: [R_AG3 + 1] * 4, 2: [R_AG3 + 2, R_AG3 + 3, R_AG3 + 4, R_AG3 + 5]}

    def spread_major(p, e):
        rows = span(base1[p] + 128 * ((minor[p] + 4 - e) % 4), 128)
        part = big_ref.at[core, p, rows]
        for d in RING4:
            send(g1.at[p] if e == 0 else part, part, AG3, into3[d][e], at_major[p]((major[p] + d) % 4))

    for d in RING4:
        for p in range(2):
            send(g1.at[p], big_ref.at[core, p, span(base2[p], 128)], AG2, into2[d], at_minor[p]((minor[p] + d) % 4))
    for p in range(2):
        spread_major(p, 0)
    for p in range(2):
        big_ref[core, p, span(base2[p], 128), :] = g1[p]

    arrived(rt2, R_TY)
    value = t2[...]
    for d in range(3):
        value = value + rt2[d]
    t3[...] = value
    for d in RING8:
        send(t3, rt3.at[d - 1], TZ, R_TZ, at_z((z + d) % 8))

    def forward(p, row, count):
        part = big_ref.at[core, p, span(row, count)]
        send(part, part, SIB, R_SIB, sibling)

    for e in (1, 3, 2):
        arrived(g1, into2[e])
        for p in range(2):
            spread_major(p, e)
    for p in range(2):
        forward(p, base1[p], 512)

    arrived(back_recv.at[:, three], R_BACK)
    gin_ref[0:3, 0:6] = back_recv[0:3, 0:6].astype(F32)
    gin_ref[0:3, 6:12] = back_recv[0:3, 6:12].astype(F32)
    gin_ref[3:6, 0:6] = back_recv[3:6, 0:6].astype(F32)
    gin_ref[3:6, 6:12] = ginf[0:3, 0:6]

    arrived(rt3, R_TZ)
    value = t3[...]
    for d in range(7):
        value = value + rt3[d]
    mine_t = tf.at[span(16 * x, 16)]
    mine_t[...] = value * GRAD_SCALE
    for d in RING4:
        send(mine_t, mine_t, TXG, R_TXG, at_x((x + d) % 4))

    left(xw.at[:, three], XS)
    left(cw.at[:, three], COTS)
    for n in range(3):
        left(pads.at[n], PADS + n)
    left(nrm.at[1], PAIR)
    left(validb.at[1], PAIR + 1)
    left(cotf.at[1], PAIR + 2)
    left(gn_recv, PAIR + 3)
    for e in range(3):
        left(pay.at[0, pl.ds(0, 6 * chunk_rows[e])], RS1 + e)
    left(pay.at[0, pl.ds(0, 768)], RS2)
    left(r3, RS3)
    left(pay.at[0, pl.ds(0, 224)], AG1)
    left(rt1, TX)
    left(rt2, TY)
    left(rt3, TZ)
    left(back_recv.at[:, three], BACK)

    for d in (1, 3):
        arrived(pay.at[0, pl.ds(0, 1024)], into3[d][0])
        for p in range(2):
            forward(p, 512 * ((major[p] + 4 - d) % 4), 512)
        if d == 1:
            arrived(rt1, R_TXG)
            send(tf, tf_recv, TSIB, R_TSIB, sibling)
    for e in (0, 1, 3, 2):
        arrived(g1, into3[2][e])
        for p in range(2):
            forward(p, 512 * ((major[p] + 2) % 4) + 128 * ((minor[p] + 4 - e) % 4), 128)
    left(pay.at[0, pl.ds(0, 768)], AG2)
    left(pay.at[:, pl.ds(0, 1536)], AG3)
    left(rt1, TXG)

    arrived(tf_recv, R_TSIB)
    left(tf, TSIB)
    for half, at in ((tf, core), (tf_recv, 1 - core)):
        rows = pl.ds(pl.multiple_of(8 * at, 8), 8)
        for c in range(5):
            table_ref[rows, 128 * c:128 * c + 128] = half[8 * c:8 * c + 8, :]
        table_ref[rows, 640:NBIAS] = half[40:48, 0:NBIAS - 640]
    for c in range(4):
        ggain_ref[:, 128 * c:128 * c + 128] = tf[48 + c:49 + c, :] + tf_recv[48 + c:49 + c, :]

    arrived(big_ref.at[1 - core], R_SIB)
    left(pay, SIB)


def widen(big, gin, table, gain, gin_out, gain_out, wqkv_out, wout_out, table_out, wqkv, wout, sem):
    made = [
        pltpu.make_async_copy(gin, gin_out, sem.at[0]),
        pltpu.make_async_copy(gain, gain_out, sem.at[1]),
        pltpu.make_async_copy(table, table_out, sem.at[2]),
    ]
    for one in made:
        one.start()
    for step in range(4):
        rows = slice(128 * step, 128 * step + 128)
        for block in range(3):
            start = (512 * step + 384, 512 * step + 256, 512 * (step // 2) + 128 * (step % 2))[block]
            for core in range(2):
                for p in range(2):
                    lanes = slice(512 * block + 256 * core + 128 * p, 512 * block + 256 * core + 128 * p + 128)
                    wqkv[rows, lanes] = big[core, p, start:start + 128, :].astype(F32) * GRAD_SCALE
        one = pltpu.make_async_copy(wqkv.at[pl.ds(128 * step, 128)], wqkv_out.at[pl.ds(128 * step, 128)], sem.at[3 + step])
        one.start()
        made.append(one)
        core, half = step // 2, step % 2
        for p in range(2):
            for u in range(2):
                start = 1024 + 512 * u + 128 * half
                lanes = slice(256 * p + 128 * u, 256 * p + 128 * u + 128)
                wout[rows, lanes] = big[core, p, start:start + 128, :].astype(F32) * GRAD_SCALE
        one = pltpu.make_async_copy(wout.at[pl.ds(128 * step, 128)], wout_out.at[pl.ds(128 * step, 128)], sem.at[7 + step])
        one.start()
        made.append(one)
    for one in made:
        one.wait()


def per_device(inputs, cotangent, pad_mask, rel_index, bias_table, ln_gain, w_qkv, w_out):
    vmem = pl.BlockSpec(memory_space=pltpu.VMEM)
    hbm = pl.BlockSpec(memory_space=pltpu.HBM)
    big, grad_in, table, gain = pl.pallas_call(
        body,
        out_shape=(
            jax.ShapeDtypeStruct((2, 2, 2048, 128), BF16),
            jax.ShapeDtypeStruct((6, 12, 2, FEAT), F32),
            jax.ShapeDtypeStruct((HEADS, NBIAS), F32),
            jax.ShapeDtypeStruct((1, FEAT), F32),
        ),
        in_specs=[hbm] * 8,
        out_specs=[vmem] * 4,
        scratch_shapes=[
            pltpu.VMEM((6, 12), I32),
            pltpu.VMEM((WT, WT), I32),
            pltpu.VMEM((8, NBIAS), F32),
            pltpu.VMEM((1, FEAT), F32),
            pltpu.VMEM((FEAT, 768), BF16),
            pltpu.VMEM((256, FEAT), BF16),
            pltpu.VMEM((768, FEAT), BF16),
            pltpu.VMEM((FEAT, 256), BF16),
            pltpu.VMEM((6, 12, 2, FEAT), BF16),
            pltpu.VMEM((6, 12, 2, FEAT), BF16),
            pltpu.VMEM((3, 6, 12), I32),
            pltpu.VMEM((32, 128), F32),
            pltpu.VMEM((WT, 256), I32),
            pltpu.VMEM((8, 1, 768), F32),
            pltpu.VMEM((2, 16, 128), I32),
            pltpu.VMEM((8, 2, 16, 128), F32),
            pltpu.VMEM((8, WT, WT), F32),
            pltpu.VMEM((2, WT, 128), BF16),
            pltpu.VMEM((2, WT, WT), F32),
            pltpu.VMEM((WT, FEAT), F32),
            pltpu.VMEM((WT, 1), F32),
            pltpu.VMEM((2, WT, FEAT), BF16),
            pltpu.VMEM((2, FEAT, WT), BF16),
            pltpu.VMEM((2, WT, FEAT), BF16),
            pltpu.VMEM((2, WT, 768), BF16),
            pltpu.VMEM((2, 768, WT), BF16),
            pltpu.VMEM((2, WT, 256), BF16),
            pltpu.VMEM((2, 256, WT), BF16),
            pltpu.VMEM((2, 256, WT), BF16),
            pltpu.VMEM((2, 256, WT), BF16),
            pltpu.VMEM((2, WT, 768), BF16),
            pltpu.VMEM((2, 8, WT, WT), F32),
            pltpu.VMEM((8, WT, WT), F32),
            pltpu.VMEM((WT, FEAT), F32),
            pltpu.VMEM((WT, FEAT), F32),
            pltpu.VMEM((2, 2048, 128), BF16),
            pltpu.VMEM((2, 3, 512, 128), BF16),
            pltpu.VMEM((2, 512, 128), BF16),
            pltpu.VMEM((2, 3, 128, 128), BF16),
            pltpu.VMEM((2, 128, 128), BF16),
            pltpu.VMEM((7, 2, 16, 128), BF16),
            pltpu.VMEM((2, 128, 128), BF16),
            pltpu.VMEM((64, 128), F32),
            pltpu.VMEM((3, 16, 128), F32),
            pltpu.VMEM((16, 128), F32),
            pltpu.VMEM((3, 16, 128), F32),
            pltpu.VMEM((16, 128), F32),
            pltpu.VMEM((7, 16, 128), F32),
            pltpu.VMEM((64, 128), F32),
            pltpu.VMEM((64, 128), F32),
            pltpu.VMEM((6, 12, 2, FEAT), BF16),
            pltpu.VMEM((6, 12, 2, FEAT), BF16),
            pltpu.VMEM((6, 12, 2, FEAT), F32),
            pltpu.SemaphoreType.DMA((SENDS,)),
            pltpu.SemaphoreType.DMA((RECVS,)),
            pltpu.SemaphoreType.DMA((10,)),
        ],
        compiler_params=pltpu.CompilerParams(
            collective_id=0, has_side_effects=True, vmem_limit_bytes=48 * 1024 * 1024
        ),
    )(
        *(
            pltpu.with_memory_space_constraint(one, pltpu.HBM)
            for one in (
                inputs.transpose(1, 2, 0, 3),
                cotangent.transpose(1, 2, 0, 3),
                pad_mask,
                rel_index,
                bias_table.T,
                ln_gain.reshape(1, FEAT),
                w_qkv,
                w_out,
            )
        )
    )
    grad_in, gain, wqkv, wout, table = pl.pallas_call(
        widen,
        out_shape=(
            jax.ShapeDtypeStruct((6, 12, 2, FEAT), F32),
            jax.ShapeDtypeStruct((1, FEAT), F32),
            jax.ShapeDtypeStruct((FEAT, 3 * FEAT), F32),
            jax.ShapeDtypeStruct((FEAT, FEAT), F32),
            jax.ShapeDtypeStruct((HEADS, NBIAS), F32),
        ),
        in_specs=[vmem] * 4,
        out_specs=[hbm] * 5,
        scratch_shapes=[
            pltpu.VMEM((FEAT, 3 * FEAT), F32),
            pltpu.VMEM((FEAT, FEAT), F32),
            pltpu.SemaphoreType.DMA((11,)),
        ],
        compiler_params=pltpu.CompilerParams(vmem_limit_bytes=24 * 1024 * 1024),
    )(big, grad_in, table, gain)
    return grad_in.transpose(2, 0, 1, 3), gain.reshape(FEAT), wqkv, wout, table.T


def solution(mesh):
    in_specs = (
        P(None, "lat", "lon", None),
        P(None, "lat", "lon", None),
        P("lat", "lon"),
        P(),
        P(),
        P(),
        P(),
        P(),
    )
    out_specs = (P(None, "lat", "lon", None), P(), P(), P(), P())
    return jax.shard_map(
        per_device, mesh=mesh, in_specs=in_specs, out_specs=out_specs, check_vma=False
    )
```

```python
import jax
import jax.numpy as jnp
from jax import lax
from jax.experimental import pallas as pl
from jax.experimental.pallas import tpu as pltpu
from jax.sharding import PartitionSpec as P

F32 = jnp.float32
BF16 = jnp.bfloat16
I32 = jnp.int32
MESH = pl.DeviceIdType.MESH

EPSILON = 1e-05
MASKED = -30000.0
WT = 144
FEAT = 512
HEADS = 16
HEAD_SIZE = 32
NBIAS = 759
SCORE_SCALE = HEAD_SIZE ** (-0.5)
GRAD_SCALE = 36864.0 ** (-0.5)

NN = (((1,), (0,)), ((), ()))
NT = (((1,), (1,)), ((), ()))

XS, COTS, PADS, PAIR, RS1, RS2, RS3, AG1, AG2, AG3, SIB = 0, 1, 2, 5, 9, 12, 13, 14, 15, 16, 17
TX, TY, TZ, TXG, TSIB, BACK = 18, 19, 20, 21, 22, 23
SENDS = 24
R_RS1, R_RS2, R_RS3, R_AG1, R_AG2, R_AG3, R_SIB = 9, 12, 14, 15, 16, 19, 25
R_TX, R_TY, R_TZ, R_TXG, R_TSIB, R_BACK = 26, 27, 28, 29, 30, 31
RECVS = 32

RING4 = (2, 1, 3)
RING8 = (4, 3, 5, 2, 6, 1, 7)


def mm(a, b, dims=NN):
    return lax.dot_general(a, b, dims, preferred_element_type=F32)


def iota(shape, dim):
    return lax.broadcasted_iota(I32, shape, dim)


def body(
    x_ref, cot_ref, pad_hbm, rel_hbm, bias_hbm, gain_hbm, wqkv_hbm, wout_hbm,
    big_ref, gin_ref, table_ref, ggain_ref,
    pad_ref, rel_ref, bias_ref, gain_ref, wq, wo, wqt, wot,
    xw, cw, pads, padf, relt, tab, edge_row, edge, edge_bias, bias, bias_rest, validb, allow, allow_rest, std, istd, nrm, nrmt, cotf,
    proj, projt, gatt, gattt, attt, gradt, gnat, probs, probs_rest, values_rest, ds, ds_rest, gn_send, gn_recv,
    pay, r1, s1, r2, s2, r3, g1,
    tb, rt1, t2, rt2, t3, rt3, tf, tf_recv,
    back_send, back_recv, ginf, ssem, rsem, lsem,
):
    lon = lax.axis_index("lon")
    lat = lax.axis_index("lat")
    z, xhi = lon // 2, lon % 2
    xlo, rest = lat // 8, lat % 8
    y, core = rest // 2, rest % 2
    x = xhi * 2 + xlo

    def at_x(value):
        return (z * 2 + value // 2, (value % 2) * 8 + rest)

    def at_y(value):
        return (lon, xlo * 8 + value * 2 + core)

    def at_z(value):
        return (value * 2 + xhi, lat)

    sibling = (lon, xlo * 8 + y * 2 + (1 - core))
    west, east = (lon + 15) % 16, (lon + 1) % 16
    south, north = (lat + 15) % 16, (lat + 1) % 16

    def send(src, dst, out, into, device):
        pltpu.make_async_remote_copy(
            src_ref=src, dst_ref=dst, send_sem=ssem.at[out], recv_sem=rsem.at[into],
            device_id=device, device_id_type=MESH,
        ).start()

    def arrived(bytes_of, into):
        pltpu.make_async_copy(bytes_of, bytes_of, rsem.at[into]).wait()

    def left(bytes_of, out):
        pltpu.make_async_copy(bytes_of, bytes_of, ssem.at[out]).wait()

    def span(start, count):
        return pl.ds(pl.multiple_of(start, 16), count)

    loads = {}
    heads_at = 256 * core
    parts = [
        ("rel", rel_hbm, rel_ref),
        ("bias", bias_hbm.at[pl.ds(pl.multiple_of(8 * core, 8), 8)], bias_ref),
        ("x", x_ref.at[pl.ds(3, 3), pl.ds(6, 6)], xw.at[pl.ds(0, 3), pl.ds(0, 6)]),
        ("cot", cot_ref.at[pl.ds(3, 3), pl.ds(6, 6)], cw.at[pl.ds(0, 3), pl.ds(0, 6)]),
        ("pad", pad_hbm, pad_ref),
        ("gain", gain_hbm, gain_ref),
        ("wo", wout_hbm.at[span(heads_at, 256)], wo),
    ]
    for block in range(3):
        lanes = pl.ds(pl.multiple_of(FEAT * block + heads_at, 128), 256)
        parts.append(("wq%d" % block, wqkv_hbm.at[:, lanes], wq.at[:, pl.ds(256 * block, 256)]))
    for n, (name, src, dst) in enumerate(parts):
        loads[name] = pltpu.make_async_copy(src, dst, lsem.at[n])
        loads[name].start()

    barrier = pltpu.get_barrier_semaphore()
    partners = [sibling, (west, lat), (lon, south), (west, south), (east, lat), (lon, north), (east, north)]
    partners += [at_x((x + d) % 4) for d in RING4]
    partners += [at_y((y + d) % 4) for d in RING4]
    partners += [at_z((z + d) % 8) for d in RING8]
    for device in partners:
        pl.semaphore_signal(barrier, inc=1, device_id=device, device_id_type=MESH)
    pl.semaphore_wait(barrier, len(partners))

    places = (
        ((0, 0), (3, 6), (west, south)),
        ((3, 0), (0, 6), (west, lat)),
        ((0, 6), (3, 0), (lon, south)),
    )
    three = pl.ds(0, 9)

    def send_quarters(field, window, index):
        for source, target, device in places:
            send(
                field.at[pl.ds(source[0], 3), pl.ds(source[1], 6)],
                window.at[pl.ds(target[0], 3), pl.ds(target[1], 6)],
                index, index, device,
            )

    send_quarters(x_ref, xw, XS)
    for n, (unused, unused, device) in enumerate(places):
        send(pad_hbm, pads.at[n], PADS + n, PADS + n, device)
    send_quarters(cot_ref, cw, COTS)

    for name in ("rel", "bias"):
        loads[name].wait()
    token = iota((WT, WT), 0)
    order = (iota((WT, WT), 1) == (token % 2) * 72 + token // 2).astype(BF16)
    rel = rel_ref[...]
    low = mm(mm(order, (rel & 255).astype(F32).astype(BF16), NT).astype(BF16), order, NT)
    high = mm(mm(order, (rel >> 8).astype(F32).astype(BF16), NT).astype(BF16), order, NT)
    index = (high * 256.0 + low).astype(I32)
    relt[...] = index[:, 0:128]
    edge_row[...] = jnp.zeros((16, 256), I32)
    edge_row[:, 0:WT] = index.T[128:WT, :]
    ds_rest[...] = jnp.zeros((256, 128), F32)
    edge[0] = edge_row[:, 0:128]
    edge[1] = edge_row[:, 128:256]
    tab[...] = jnp.zeros((8, 1, 768), F32)
    for head in range(8):
        tab[head, :, :NBIAS] = bias_ref[head:head + 1, :]

    def gather_heads(index, put):
        lane, chunk = index & 127, index >> 7
        inside = [chunk == c for c in range(6)]
        for head in range(8):
            found = jnp.zeros(index.shape, F32)
            for c in range(6):
                row = jnp.broadcast_to(tab[head, :, 128 * c:128 * c + 128], index.shape)
                taken = jnp.take_along_axis(row, lane, axis=1, mode="promise_in_bounds")
                found = jnp.where(inside[c], taken, found)
            put(head, found)

    def lookup(step, carry):
        rows = pl.ds(pl.multiple_of(8 * step, 8), 8)

        def put(head, found):
            bias[head, rows, :] = found

        gather_heads(relt[rows, :], put)
        return carry

    lax.fori_loop(0, WT // 8, lookup, 0)
    def lookup_rest(step, carry):
        part, half = step // 2, pl.ds(pl.multiple_of(8 * (step % 2), 8), 8)

        def put(head, found):
            edge_bias[part, pl.ds(pl.multiple_of(16 * head + 8 * (step % 2), 8), 8), :] = found

        gather_heads(edge[part, half, :], put)
        return carry

    lax.fori_loop(0, 4, lookup_rest, 0)
    bias_rest[0:128, :] = edge_bias[0].T
    bias_rest[128:WT, :] = edge_bias[1].T[0:16, :]
    deal = ((iota((WT, 128), 0) - 128) == iota((WT, 128), 1) % 16).astype(F32).astype(BF16)
    gather_up = (iota((128, WT), 0) % 16 == (iota((128, WT), 1) - 128)).astype(F32).astype(BF16)
    own_rows = (iota((256, 128), 0) // HEAD_SIZE == iota((256, 128), 1) // 16).astype(F32)
    own_cols = (iota((128, 256), 0) // 16 == iota((128, 256), 1) // HEAD_SIZE).astype(F32)

    for name in ("wo", "wq0", "wq1", "wq2", "pad", "x", "cot", "gain"):
        loads[name].wait()
    wot[...] = wo[...].T
    for block in range(3):
        wqt[256 * block:256 * block + 256, :] = wq[:, 256 * block:256 * block + 256].T

    arrived(xw.at[:, three], XS)
    tokens = xw[...].astype(F32).reshape(WT, FEAT)
    center = tokens - jnp.mean(tokens, axis=-1, keepdims=True)
    variance = jnp.mean(center * center, axis=-1, keepdims=True)
    inv_std = lax.rsqrt(variance + EPSILON)
    standard = center * inv_std
    std[...] = standard
    istd[...] = inv_std
    nrm[0] = (standard * gain_ref[...]).astype(BF16)
    send(nrm.at[0], nrm.at[1], PAIR, PAIR, sibling)

    def project(w):
        proj[w] = mm(nrm[w], wq[...]).astype(BF16)
        projt[w] = proj[w].T
        nrmt[w] = nrm[w].T

    project(0)

    for n in range(3):
        arrived(pads.at[n], PADS + n)
    padf[...] = jnp.zeros((32, 128), F32)
    padf[0:6, 0:12] = pad_ref[...].astype(F32)
    for n, slot_at in enumerate((3, 1, 2)):
        padf[8 * slot_at:8 * slot_at + 6, 0:12] = pads[n].astype(F32)

    def spot(token_at):
        row, col = token_at // 24, (token_at % 24) // 2
        slot = (row >= 3).astype(I32) * 2 + (col >= 6).astype(I32)
        return slot, row + jnp.where(row < 3, 3, -3), col + jnp.where(col < 6, 6, -6)

    slot, source_row, unused = spot(iota((WT, 32), 0))
    row_pick = (iota((WT, 32), 1) == slot * 8 + source_row).astype(BF16)
    unused, unused, source_col = spot(iota((WT, 128), 0))
    picked = mm(row_pick, padf[...].astype(BF16))
    valid = jnp.sum(jnp.where(iota((WT, 128), 1) == source_col, picked, 0.0), axis=1, keepdims=True)
    validb[0] = jnp.broadcast_to(valid, (WT, 128)).astype(BF16)
    send(validb.at[0], validb.at[1], PAIR + 1, PAIR + 1, sibling)

    def see(w):
        key, query = iota((WT, WT), 0), iota((WT, WT), 1)
        across = lat + w * (1 - 2 * core) == 15
        same_group = ((key >= 72) == (query >= 72)) | jnp.logical_not(across)
        valid_key = validb[w].astype(F32)[:, 0:1] > 0.5
        seen = (same_group & (valid_key | (key == query))).astype(F32)
        allow[w] = seen[:, 0:128]
        allow_rest[w] = mm(seen.astype(BF16), deal)

    see(0)
    arrived(cw.at[:, three], COTS)
    cotf[0] = cw[...].reshape(WT, FEAT)
    send(cotf.at[0], cotf.at[1], PAIR + 2, PAIR + 2, sibling)

    def project_cot(w):
        gatt[w] = mm(cotf[w], wot[...]).astype(BF16)
        gattt[w] = gatt[w].T

    project_cot(0)

    lane_head = iota((1, 128), 1) // HEAD_SIZE
    mine = [(lane_head == j).astype(F32).astype(BF16) for j in range(4)]

    def apart(group):
        return jnp.concatenate([group * mine[j] for j in range(4)], axis=0)

    def own_blocks(wide):
        return [wide[32 * j:32 * j + 32, 128 * j:128 * j + 128].astype(BF16) for j in range(4)]

    def softmax(scores, seen, added):
        scores = jnp.where(seen > 0.5, scores * SCORE_SCALE + added, MASKED)
        exponent = jnp.exp(scores - jnp.max(scores, axis=0, keepdims=True))
        return exponent * (1.0 / jnp.sum(exponent, axis=0, keepdims=True))

    def softmax_grad(prob, grad_probs):
        return prob * (grad_probs - jnp.sum(prob * grad_probs, axis=0, keepdims=True))

    def fold(wide):
        return mm((wide * own_rows).astype(BF16), gather_up)[:, 128:WT].astype(BF16)

    def forward_heads(w):
        rest_queries = (mm(projt[w, 0:256, :], deal) * own_rows).astype(BF16)
        prob = softmax(mm(proj[w, :, 256:512], rest_queries), allow_rest[w], bias_rest[...])
        probs_rest[w] = prob
        prob_b = prob.astype(BF16)
        attt[w, :, 128:WT] = fold(mm(projt[w, 512:768, :], prob_b))
        rest_cot = (mm(gather_up, gatt[w]) * own_cols).astype(BF16)
        values_rest[...] = mm(prob_b, rest_cot)

        for group in range(2):
            here = slice(128 * group, 128 * group + 128)
            keys_at, values_at = slice(256 + here.start, 256 + here.stop), slice(512 + here.start, 512 + here.stop)
            scores = mm(apart(proj[w, :, keys_at]), projt[w, here, 0:128])
            four = []
            for j in range(4):
                head = group * 4 + j
                prob = softmax(scores[WT * j:WT * j + WT], allow[w], bias[head])
                probs[w, head] = prob
                four.append(prob.astype(BF16))
            four = jnp.concatenate(four, axis=1)
            for j, block in enumerate(own_blocks(mm(projt[w, values_at, :], four))):
                attt[w, 32 * (4 * group + j):32 * (4 * group + j) + 32, 0:128] = block
            grad_values = values_rest[:, here] + mm(four, apart(gatt[w, 0:128, here]))
            gnat[w, :, values_at] = grad_values.astype(BF16)

    def backward_heads(w):
        rest_cot = (mm(gattt[w], deal) * own_rows).astype(BF16)
        grad_scores = softmax_grad(probs_rest[w], mm(proj[w, :, 512:768], rest_cot))
        if w == 0:
            ds_rest[0:WT, :] = grad_scores
        else:
            ds_rest[0:WT, :] = ds_rest[0:WT, :] + grad_scores
        grad_b = grad_scores.astype(BF16)
        gradt[w, :, 128:WT] = fold(mm(projt[w, 256:512, :], grad_b) * SCORE_SCALE)
        rest_queries = (mm(gather_up, proj[w, :, 0:256]) * own_cols).astype(BF16)
        values_rest[...] = mm(grad_b, rest_queries)

        for group in range(2):
            here = slice(128 * group, 128 * group + 128)
            keys_at, values_at = slice(256 + here.start, 256 + here.stop), slice(512 + here.start, 512 + here.stop)
            grad_probs = mm(apart(proj[w, :, values_at]), gattt[w, here, 0:128])
            four = []
            for j in range(4):
                head = group * 4 + j
                grad_scores = softmax_grad(probs[w, head], grad_probs[WT * j:WT * j + WT])
                if w == 0:
                    ds[head] = grad_scores
                else:
                    ds[head] = ds[head] + grad_scores
                four.append(grad_scores.astype(BF16))
            four = jnp.concatenate(four, axis=1)
            for j, block in enumerate(own_blocks(mm(projt[w, keys_at, :], four) * SCORE_SCALE)):
                gradt[w, 32 * (4 * group + j):32 * (4 * group + j) + 32, 0:128] = block
            grad_keys = values_rest[:, here] + mm(four, apart(proj[w, 0:128, here]))
            gnat[w, :, keys_at] = (grad_keys * SCORE_SCALE).astype(BF16)

    forward_heads(0)
    arrived(nrm.at[1], PAIR)
    project(1)
    arrived(validb.at[1], PAIR + 1)
    see(1)
    arrived(cotf.at[1], PAIR + 2)
    project_cot(1)
    forward_heads(1)

    major, minor = (x, y), (y, x)
    at_major, at_minor = (at_x, at_y), (at_y, at_x)
    chunk_at = (0, 1024, 1536)
    chunk_rows = (256, 128, 128)

    def columns(block):
        lanes = slice(256 * block, 256 * block + 256)
        return mm(nrmt[0], gnat[0, :, lanes]) + mm(nrmt[1], gnat[1, :, lanes])

    def scatter_pay(e):
        count = chunk_rows[e]
        for d in RING4:
            for p in range(2):
                to = (major[p] + d) % 4
                send(
                    pay.at[p, span(chunk_at[e] + count * to, count)],
                    r1.at[p, d - 1, pl.ds(128 * e + 128 * (e > 0), count)],
                    RS1 + e, R_RS1 + e, at_major[p](to),
                )

    out = columns(2)
    for p in range(2):
        pay[p, 0:512, :] = out[:, 128 * p:128 * p + 128].astype(BF16)
    out = mm(attt[0], cotf[0]) + mm(attt[1], cotf[1])
    for p in range(2):
        for u in range(2):
            lanes = slice(256 * p + 128 * u, 256 * p + 128 * u + 128)
            pay[p, 512 + 256 * u:768 + 256 * u, :] = out[:, lanes].astype(BF16)
    scatter_pay(0)
    backward_heads(0)
    backward_heads(1)
    out = columns(1)
    for p in range(2):
        pay[p, 1024:1536, :] = out[:, 128 * p:128 * p + 128].astype(BF16)
    scatter_pay(1)
    for w in range(2):
        gnat[w, :, 0:256] = gradt[w].T
    out = columns(0)
    for p in range(2):
        pay[p, 1536:2048, :] = out[:, 128 * p:128 * p + 128].astype(BF16)
    scatter_pay(2)

    gn_send[...] = mm(gnat[1], wqt[...])
    send(gn_send, gn_recv, PAIR + 3, PAIR + 3, sibling)
    grad_normed = mm(gnat[0], wqt[...])

    def table_part(pairs):
        upper, pieces = [], []
        for index, rows_in in pairs:
            lanes = index.shape[1]
            upper.append((iota((48, lanes), 0) == (index >> 4)).astype(F32).astype(BF16))
            match = iota((16, lanes), 0) == (index & 15)
            pieces.append(jnp.concatenate(
                [jnp.where(match, jnp.broadcast_to(row, (16, lanes)), 0.0) for row in rows_in], axis=0
            ).astype(BF16))
        return mm(jnp.concatenate(pieces, axis=1), jnp.concatenate(upper, axis=1), NT)

    def scatter(step, total):
        rows = pl.ds(pl.multiple_of(8 * step, 8), 8)
        indices = relt[rows, :]
        values = [ds[h, rows, :] for h in range(8)]
        return total + table_part([(indices[k:k + 1, :], [one[k:k + 1, :] for one in values]) for k in range(8)])

    total = lax.fori_loop(0, WT // 8, scatter, jnp.zeros((128, 48), F32))

    for e in range(3):
        count = chunk_rows[e]
        rows = slice(128 * e + 128 * (e > 0), 128 * e + 128 * (e > 0) + count)
        arrived(r1.at[:, :, pl.ds(rows.start, count)], R_RS1 + e)
        for p in range(2):
            value = pay[p, span(chunk_at[e] + count * major[p], count), :].astype(F32)
            for d in range(3):
                value = value + r1[p, d, rows, :].astype(F32)
            s1[p, rows, :] = value.astype(BF16)
    for d in RING4:
        for p in range(2):
            to = (minor[p] + d) % 4
            send(s1.at[p, span(128 * to, 128)], r2.at[p, d - 1], RS2, R_RS2 + p, at_minor[p](to))

    arrived(gn_recv, PAIR + 3)
    grad_normed = grad_normed + gn_recv[...]
    standard = std[...]
    grad_gain = jnp.sum(grad_normed * standard, axis=0, keepdims=True)
    grad_hat = grad_normed * gain_ref[...]
    grad_in = istd[...] * (
        grad_hat
        - jnp.mean(grad_hat, axis=-1, keepdims=True)
        - standard * jnp.mean(grad_hat * standard, axis=-1, keepdims=True)
    )
    back_send[...] = grad_in.astype(BF16).reshape(6, 12, 2, FEAT)
    returns = (
        ((3, 6), (0, 0), (east, north)),
        ((0, 6), (3, 0), (east, lat)),
        ((3, 0), (0, 6), (lon, north)),
    )
    for source, target, device in returns:
        send(
            back_send.at[pl.ds(source[0], 3), pl.ds(source[1], 6)],
            back_recv.at[pl.ds(target[0], 3), pl.ds(target[1], 6)],
            BACK, R_BACK, device,
        )
    ginf[...] = grad_in.reshape(6, 12, 2, FEAT)

    for p in range(2):
        arrived(r2.at[p], R_RS2 + p)
        value = s1[p, span(128 * minor[p], 128), :].astype(F32)
        for d in range(3):
            value = value + r2[p, d].astype(F32)
        s2[p] = value.astype(BF16)
    for d in RING8:
        to = (z + d) % 8
        send(s2.at[:, span(16 * to, 16)], r3.at[d - 1], RS3, R_RS3, at_z(to))

    turned_rest = ds_rest[...].T
    turned = total
    for half in range(2):
        turned = turned + table_part([
            (edge_row[n:n + 1, :], [turned_rest[16 * h + n:16 * h + n + 1, :] for h in range(8)])
            for n in range(8 * half, 8 * half + 8)
        ])
    upper_part = turned.astype(BF16)
    lower_part = (turned - upper_part.astype(F32)).astype(BF16)
    spread = (iota((48, 768), 1) // 16 == iota((48, 768), 0)).astype(F32).astype(BF16)
    wide = mm(upper_part, spread) + mm(lower_part, spread)
    wide = jnp.where(iota((128, 768), 1) % 16 == iota((128, 768), 0) % 16, wide, 0.0)
    wide = jnp.sum(wide.reshape(8, 16, 768), axis=1)
    tb[...] = jnp.zeros((64, 128), F32)
    for c in range(6):
        tb[8 * c:8 * c + 8, :] = wide[:, 128 * c:128 * c + 128]
    for c in range(4):
        tb[48 + c:49 + c, :] = grad_gain[:, 128 * c:128 * c + 128]
    for d in RING4:
        to = (x + d) % 4
        send(tb.at[span(16 * to, 16)], rt1.at[d - 1], TX, R_TX, at_x(to))

    arrived(r3, R_RS3)
    for p in range(2):
        value = s2[p, span(16 * z, 16), :].astype(F32)
        for d in range(7):
            value = value + r3[d, p].astype(F32)
        g1[p, span(16 * z, 16), :] = value.astype(BF16)
    mine_z = g1.at[:, span(16 * z, 16)]
    for d in RING8:
        send(mine_z, mine_z, AG1, R_AG1, at_z((z + d) % 8))

    arrived(rt1, R_TX)
    value = tb[span(16 * x, 16), :]
    for d in range(3):
        value = value + rt1[d]
    t2[...] = value
    for d in RING4:
        send(t2, rt2.at[d - 1], TY, R_TY, at_y((y + d) % 4))

    base1 = [512 * major[p] for p in range(2)]
    base2 = [base1[p] + 128 * minor[p] for p in range(2)]
    arrived(pay.at[0, pl.ds(0, 224)], R_AG1)
    into2 = {1: R_AG2, 3: R_AG2 + 1, 2: R_AG2 + 2}
    into3 = {1: [R_AG3] * 4, 3: [R_AG3 + 1] * 4, 2: [R_AG3 + 2, R_AG3 + 3, R_AG3 + 4, R_AG3 + 5]}

    def spread_major(p, e):
        rows = span(base1[p] + 128 * ((minor[p] + 4 - e) % 4), 128)
        part = big_ref.at[core, p, rows]
        for d in RING4:
            send(g1.at[p] if e == 0 else part, part, AG3, into3[d][e], at_major[p]((major[p] + d) % 4))

    for d in RING4:
        for p in range(2):
            send(g1.at[p], big_ref.at[core, p, span(base2[p], 128)], AG2, into2[d], at_minor[p]((minor[p] + d) % 4))
    for p in range(2):
        spread_major(p, 0)
    for p in range(2):
        big_ref[core, p, span(base2[p], 128), :] = g1[p]

    arrived(rt2, R_TY)
    value = t2[...]
    for d in range(3):
        value = value + rt2[d]
    t3[...] = value
    for d in RING8:
        send(t3, rt3.at[d - 1], TZ, R_TZ, at_z((z + d) % 8))

    def forward(p, row, count):
        part = big_ref.at[core, p, span(row, count)]
        send(part, part, SIB, R_SIB, sibling)

    for e in (1, 3, 2):
        arrived(g1, into2[e])
        for p in range(2):
            spread_major(p, e)
    for p in range(2):
        forward(p, base1[p], 512)

    arrived(back_recv.at[:, three], R_BACK)
    gin_ref[0:3, 0:6] = back_recv[0:3, 0:6].astype(F32)
    gin_ref[0:3, 6:12] = back_recv[0:3, 6:12].astype(F32)
    gin_ref[3:6, 0:6] = back_recv[3:6, 0:6].astype(F32)
    gin_ref[3:6, 6:12] = ginf[0:3, 0:6]

    arrived(rt3, R_TZ)
    value = t3[...]
    for d in range(7):
        value = value + rt3[d]
    mine_t = tf.at[span(16 * x, 16)]
    mine_t[...] = value * GRAD_SCALE
    for d in RING4:
        send(mine_t, mine_t, TXG, R_TXG, at_x((x + d) % 4))

    left(xw.at[:, three], XS)
    left(cw.at[:, three], COTS)
    for n in range(3):
        left(pads.at[n], PADS + n)
    left(nrm.at[1], PAIR)
    left(validb.at[1], PAIR + 1)
    left(cotf.at[1], PAIR + 2)
    left(gn_recv, PAIR + 3)
    for e in range(3):
        left(pay.at[0, pl.ds(0, 6 * chunk_rows[e])], RS1 + e)
    left(pay.at[0, pl.ds(0, 768)], RS2)
    left(r3, RS3)
    left(pay.at[0, pl.ds(0, 224)], AG1)
    left(rt1, TX)
    left(rt2, TY)
    left(rt3, TZ)
    left(back_recv.at[:, three], BACK)

    for d in (1, 3):
        arrived(pay.at[0, pl.ds(0, 1024)], into3[d][0])
        for p in range(2):
            forward(p, 512 * ((major[p] + 4 - d) % 4), 512)
        if d == 1:
            arrived(rt1, R_TXG)
            send(tf, tf_recv, TSIB, R_TSIB, sibling)
    for e in (0, 1, 3, 2):
        arrived(g1, into3[2][e])
        for p in range(2):
            forward(p, 512 * ((major[p] + 2) % 4) + 128 * ((minor[p] + 4 - e) % 4), 128)
    left(pay.at[0, pl.ds(0, 768)], AG2)
    left(pay.at[:, pl.ds(0, 1536)], AG3)
    left(rt1, TXG)

    arrived(tf_recv, R_TSIB)
    left(tf, TSIB)
    for half, at in ((tf, core), (tf_recv, 1 - core)):
        rows = pl.ds(pl.multiple_of(8 * at, 8), 8)
        for c in range(5):
            table_ref[rows, 128 * c:128 * c + 128] = half[8 * c:8 * c + 8, :]
        table_ref[rows, 640:NBIAS] = half[40:48, 0:NBIAS - 640]
    for c in range(4):
        ggain_ref[:, 128 * c:128 * c + 128] = tf[48 + c:49 + c, :] + tf_recv[48 + c:49 + c, :]

    arrived(big_ref.at[1 - core], R_SIB)
    left(pay, SIB)


def widen(big, gin, table, gain, gin_out, gain_out, wqkv_out, wout_out, table_out, wqkv, wout, sem):
    made = [
        pltpu.make_async_copy(gin, gin_out, sem.at[0]),
        pltpu.make_async_copy(gain, gain_out, sem.at[1]),
        pltpu.make_async_copy(table, table_out, sem.at[2]),
    ]
    for one in made:
        one.start()
    for step in range(4):
        rows = slice(128 * step, 128 * step + 128)
        for block in range(3):
            start = (512 * step + 384, 512 * step + 256, 512 * (step // 2) + 128 * (step % 2))[block]
            for core in range(2):
                for p in range(2):
                    lanes = slice(512 * block + 256 * core + 128 * p, 512 * block + 256 * core + 128 * p + 128)
                    wqkv[rows, lanes] = big[core, p, start:start + 128, :].astype(F32) * GRAD_SCALE
        one = pltpu.make_async_copy(wqkv.at[pl.ds(128 * step, 128)], wqkv_out.at[pl.ds(128 * step, 128)], sem.at[3 + step])
        one.start()
        made.append(one)
        core, half = step // 2, step % 2
        for p in range(2):
            for u in range(2):
                start = 1024 + 512 * u + 128 * half
                lanes = slice(256 * p + 128 * u, 256 * p + 128 * u + 128)
                wout[rows, lanes] = big[core, p, start:start + 128, :].astype(F32) * GRAD_SCALE
        one = pltpu.make_async_copy(wout.at[pl.ds(128 * step, 128)], wout_out.at[pl.ds(128 * step, 128)], sem.at[7 + step])
        one.start()
        made.append(one)
    for one in made:
        one.wait()


def per_device(inputs, cotangent, pad_mask, rel_index, bias_table, ln_gain, w_qkv, w_out):
    vmem = pl.BlockSpec(memory_space=pltpu.VMEM)
    hbm = pl.BlockSpec(memory_space=pltpu.HBM)
    big, grad_in, table, gain = pl.pallas_call(
        body,
        out_shape=(
            jax.ShapeDtypeStruct((2, 2, 2048, 128), BF16),
            jax.ShapeDtypeStruct((6, 12, 2, FEAT), F32),
            jax.ShapeDtypeStruct((HEADS, NBIAS), F32),
            jax.ShapeDtypeStruct((1, FEAT), F32),
        ),
        in_specs=[hbm] * 8,
        out_specs=[vmem] * 4,
        scratch_shapes=[
            pltpu.VMEM((6, 12), I32),
            pltpu.VMEM((WT, WT), I32),
            pltpu.VMEM((8, NBIAS), F32),
            pltpu.VMEM((1, FEAT), F32),
            pltpu.VMEM((FEAT, 768), BF16),
            pltpu.VMEM((256, FEAT), BF16),
            pltpu.VMEM((768, FEAT), BF16),
            pltpu.VMEM((FEAT, 256), BF16),
            pltpu.VMEM((6, 12, 2, FEAT), BF16),
            pltpu.VMEM((6, 12, 2, FEAT), BF16),
            pltpu.VMEM((3, 6, 12), I32),
            pltpu.VMEM((32, 128), F32),
            pltpu.VMEM((WT, 128), I32),
            pltpu.VMEM((8, 1, 768), F32),
            pltpu.VMEM((16, 256), I32),
            pltpu.VMEM((2, 16, 128), I32),
            pltpu.VMEM((2, 128, 128), F32),
            pltpu.VMEM((8, WT, 128), F32),
            pltpu.VMEM((WT, 128), F32),
            pltpu.VMEM((2, WT, 128), BF16),
            pltpu.VMEM((2, WT, 128), F32),
            pltpu.VMEM((2, WT, 128), F32),
            pltpu.VMEM((WT, FEAT), F32),
            pltpu.VMEM((WT, 1), F32),
            pltpu.VMEM((2, WT, FEAT), BF16),
            pltpu.VMEM((2, FEAT, WT), BF16),
            pltpu.VMEM((2, WT, FEAT), BF16),
            pltpu.VMEM((2, WT, 768), BF16),
            pltpu.VMEM((2, 768, WT), BF16),
            pltpu.VMEM((2, WT, 256), BF16),
            pltpu.VMEM((2, 256, WT), BF16),
            pltpu.VMEM((2, 256, WT), BF16),
            pltpu.VMEM((2, 256, WT), BF16),
            pltpu.VMEM((2, WT, 768), BF16),
            pltpu.VMEM((2, 8, WT, 128), F32),
            pltpu.VMEM((2, WT, 128), F32),
            pltpu.VMEM((WT, 256), F32),
            pltpu.VMEM((8, WT, 128), F32),
            pltpu.VMEM((256, 128), F32),
            pltpu.VMEM((WT, FEAT), F32),
            pltpu.VMEM((WT, FEAT), F32),
            pltpu.VMEM((2, 2048, 128), BF16),
            pltpu.VMEM((2, 3, 512, 128), BF16),
            pltpu.VMEM((2, 512, 128), BF16),
            pltpu.VMEM((2, 3, 128, 128), BF16),
            pltpu.VMEM((2, 128, 128), BF16),
            pltpu.VMEM((7, 2, 16, 128), BF16),
            pltpu.VMEM((2, 128, 128), BF16),
            pltpu.VMEM((64, 128), F32),
            pltpu.VMEM((3, 16, 128), F32),
            pltpu.VMEM((16, 128), F32),
            pltpu.VMEM((3, 16, 128), F32),
            pltpu.VMEM((16, 128), F32),
            pltpu.VMEM((7, 16, 128), F32),
            pltpu.VMEM((64, 128), F32),
            pltpu.VMEM((64, 128), F32),
            pltpu.VMEM((6, 12, 2, FEAT), BF16),
            pltpu.VMEM((6, 12, 2, FEAT), BF16),
            pltpu.VMEM((6, 12, 2, FEAT), F32),
            pltpu.SemaphoreType.DMA((SENDS,)),
            pltpu.SemaphoreType.DMA((RECVS,)),
            pltpu.SemaphoreType.DMA((10,)),
        ],
        compiler_params=pltpu.CompilerParams(
            collective_id=0, has_side_effects=True, vmem_limit_bytes=48 * 1024 * 1024
        ),
    )(
        *(
            pltpu.with_memory_space_constraint(one, pltpu.HBM)
            for one in (
                inputs.transpose(1, 2, 0, 3),
                cotangent.transpose(1, 2, 0, 3),
                pad_mask,
                rel_index,
                bias_table.T,
                ln_gain.reshape(1, FEAT),
                w_qkv,
                w_out,
            )
        )
    )
    grad_in, gain, wqkv, wout, table = pl.pallas_call(
        widen,
        out_shape=(
            jax.ShapeDtypeStruct((6, 12, 2, FEAT), F32),
            jax.ShapeDtypeStruct((1, FEAT), F32),
            jax.ShapeDtypeStruct((FEAT, 3 * FEAT), F32),
            jax.ShapeDtypeStruct((FEAT, FEAT), F32),
            jax.ShapeDtypeStruct((HEADS, NBIAS), F32),
        ),
        in_specs=[vmem] * 4,
        out_specs=[hbm] * 5,
        scratch_shapes=[
            pltpu.VMEM((FEAT, 3 * FEAT), F32),
            pltpu.VMEM((FEAT, FEAT), F32),
            pltpu.SemaphoreType.DMA((11,)),
        ],
        compiler_params=pltpu.CompilerParams(vmem_limit_bytes=24 * 1024 * 1024),
    )(big, grad_in, table, gain)
    return grad_in.transpose(2, 0, 1, 3), gain.reshape(FEAT), wqkv, wout, table.T


def solution(mesh):
    in_specs = (
        P(None, "lat", "lon", None),
        P(None, "lat", "lon", None),
        P("lat", "lon"),
        P(),
        P(),
        P(),
        P(),
        P(),
    )
    out_specs = (P(None, "lat", "lon", None), P(), P(), P(), P())
    return jax.shard_map(
        per_device, mesh=mesh, in_specs=in_specs, out_specs=out_specs, check_vma=False
    )
```

```python
import jax
import jax.numpy as jnp
from jax import lax
from jax.experimental import pallas as pl
from jax.experimental.pallas import tpu as pltpu
from jax.sharding import PartitionSpec as P

F32 = jnp.float32
BF16 = jnp.bfloat16
I32 = jnp.int32
MESH = pl.DeviceIdType.MESH

EPSILON = 1e-05
MASKED = -30000.0
WT = 144
FEAT = 512
HEADS = 16
HEAD_SIZE = 32
NBIAS = 759
SCORE_SCALE = HEAD_SIZE ** (-0.5)
GRAD_SCALE = 36864.0 ** (-0.5)

NN = (((1,), (0,)), ((), ()))
NT = (((1,), (1,)), ((), ()))

XS, COTS, PADS, PAIR, RS1, RS2, RS3, AG1, AG2, AG3, SIB = 0, 1, 2, 5, 9, 12, 13, 14, 15, 16, 17
TX, TY, TZ, TXG, TSIB, BACK = 18, 19, 20, 21, 22, 23
SENDS = 24
R_RS1, R_RS2, R_RS3, R_AG1, R_AG2, R_AG3, R_SIB = 9, 12, 14, 15, 16, 19, 23
R_TX, R_TY, R_TZ, R_TXG, R_TSIB, R_BACK = 24, 25, 26, 27, 28, 29
RECVS = 30

RING4 = (2, 1, 3)
RING8 = (4, 3, 5, 2, 6, 1, 7)


def mm(a, b, dims=NN):
    return lax.dot_general(a, b, dims, preferred_element_type=F32)


def iota(shape, dim):
    return lax.broadcasted_iota(I32, shape, dim)


def body(
    x_ref, cot_ref, pad_hbm, rel_hbm, bias_hbm, gain_hbm, wqkv_hbm, wout_hbm,
    big_ref, gin_ref, table_ref, ggain_ref,
    pad_ref, rel_ref, bias_ref, gain_ref, wq, wo, wqt, wot,
    xw, cw, pads, padf, relt, tab, edge_row, edge, edge_bias, bias, bias_rest, validb, allow, allow_rest, std, istd, nrm, nrmt, cotf,
    proj, projt, gatt, gattt, attt, gradt, gnat, probs, probs_rest, keys_rest, probs_b, ds, ds_rest, gn_send, gn_recv,
    pay, r1, s1, r2, s2, r3, g1,
    tb, rt1, t2, rt2, t3, rt3, tf, tf_recv,
    back_send, back_recv, ginf, ssem, rsem, lsem,
):
    lon = lax.axis_index("lon")
    lat = lax.axis_index("lat")
    z, xhi = lon // 2, lon % 2
    xlo, rest = lat // 8, lat % 8
    y, core = rest // 2, rest % 2
    x = xhi * 2 + xlo

    def at_x(value):
        return (z * 2 + value // 2, (value % 2) * 8 + rest)

    def at_y(value):
        return (lon, xlo * 8 + value * 2 + core)

    def at_z(value):
        return (value * 2 + xhi, lat)

    sibling = (lon, xlo * 8 + y * 2 + (1 - core))
    west, east = (lon + 15) % 16, (lon + 1) % 16
    south, north = (lat + 15) % 16, (lat + 1) % 16

    def send(src, dst, out, into, device):
        pltpu.make_async_remote_copy(
            src_ref=src, dst_ref=dst, send_sem=ssem.at[out], recv_sem=rsem.at[into],
            device_id=device, device_id_type=MESH,
        ).start()

    def arrived(bytes_of, into):
        pltpu.make_async_copy(bytes_of, bytes_of, rsem.at[into]).wait()

    def left(bytes_of, out):
        pltpu.make_async_copy(bytes_of, bytes_of, ssem.at[out]).wait()

    def span(start, count):
        return pl.ds(pl.multiple_of(start, 16), count)

    loads = {}
    heads_at = 256 * core
    parts = [
        ("rel", rel_hbm, rel_ref),
        ("bias", bias_hbm.at[pl.ds(pl.multiple_of(8 * core, 8), 8)], bias_ref),
        ("x", x_ref.at[pl.ds(3, 3), pl.ds(6, 6)], xw.at[pl.ds(0, 3), pl.ds(0, 6)]),
        ("cot", cot_ref.at[pl.ds(3, 3), pl.ds(6, 6)], cw.at[pl.ds(0, 3), pl.ds(0, 6)]),
        ("pad", pad_hbm, pad_ref),
        ("gain", gain_hbm, gain_ref),
        ("wo", wout_hbm.at[span(heads_at, 256)], wo),
    ]
    for block in range(3):
        lanes = pl.ds(pl.multiple_of(FEAT * block + heads_at, 128), 256)
        parts.append(("wq%d" % block, wqkv_hbm.at[:, lanes], wq.at[:, pl.ds(256 * block, 256)]))
    for n, (name, src, dst) in enumerate(parts):
        loads[name] = pltpu.make_async_copy(src, dst, lsem.at[n])
        loads[name].start()

    barrier = pltpu.get_barrier_semaphore()
    partners = [sibling, (west, lat), (lon, south), (west, south), (east, lat), (lon, north), (east, north)]
    partners += [at_x((x + d) % 4) for d in RING4]
    partners += [at_y((y + d) % 4) for d in RING4]
    partners += [at_z((z + d) % 8) for d in RING8]
    for device in partners:
        pl.semaphore_signal(barrier, inc=1, device_id=device, device_id_type=MESH)
    pl.semaphore_wait(barrier, len(partners))

    places = (
        ((0, 0), (3, 6), (west, south)),
        ((3, 0), (0, 6), (west, lat)),
        ((0, 6), (3, 0), (lon, south)),
    )
    three = pl.ds(0, 9)

    def send_quarters(field, window, index):
        for source, target, device in places:
            send(
                field.at[pl.ds(source[0], 3), pl.ds(source[1], 6)],
                window.at[pl.ds(target[0], 3), pl.ds(target[1], 6)],
                index, index, device,
            )

    send_quarters(x_ref, xw, XS)
    for n, (unused, unused, device) in enumerate(places):
        send(pad_hbm, pads.at[n], PADS + n, PADS + n, device)
    send_quarters(cot_ref, cw, COTS)

    for name in ("rel", "bias"):
        loads[name].wait()
    token = iota((WT, WT), 0)
    order = (iota((WT, WT), 1) == (token % 2) * 72 + token // 2).astype(BF16)
    rel = rel_ref[...]
    low = mm(mm(order, (rel & 255).astype(F32).astype(BF16), NT).astype(BF16), order, NT)
    high = mm(mm(order, (rel >> 8).astype(F32).astype(BF16), NT).astype(BF16), order, NT)
    index = (high * 256.0 + low).astype(I32)
    relt[...] = index[:, 0:128]
    edge_row[...] = jnp.zeros((16, 256), I32)
    edge_row[:, 0:WT] = index.T[128:WT, :]
    ds_rest[...] = jnp.zeros((256, 128), F32)
    edge[0] = edge_row[:, 0:128]
    edge[1] = edge_row[:, 128:256]
    tab[...] = jnp.zeros((8, 1, 768), F32)
    for head in range(8):
        tab[head, :, :NBIAS] = bias_ref[head:head + 1, :]

    def gather_heads(index, put):
        lane, chunk = index & 127, index >> 7
        inside = [chunk == c for c in range(6)]
        for head in range(8):
            found = jnp.zeros(index.shape, F32)
            for c in range(6):
                row = jnp.broadcast_to(tab[head, :, 128 * c:128 * c + 128], index.shape)
                taken = jnp.take_along_axis(row, lane, axis=1, mode="promise_in_bounds")
                found = jnp.where(inside[c], taken, found)
            put(head, found)

    def lookup(step, carry):
        rows = pl.ds(pl.multiple_of(8 * step, 8), 8)

        def put(head, found):
            bias[head, rows, :] = found

        gather_heads(relt[rows, :], put)
        return carry

    lax.fori_loop(0, WT // 8, lookup, 0)
    def lookup_rest(step, carry):
        part, half = step // 2, pl.ds(pl.multiple_of(8 * (step % 2), 8), 8)

        def put(head, found):
            edge_bias[part, pl.ds(pl.multiple_of(16 * head + 8 * (step % 2), 8), 8), :] = found

        gather_heads(edge[part, half, :], put)
        return carry

    lax.fori_loop(0, 4, lookup_rest, 0)
    bias_rest[0:128, :] = edge_bias[0].T
    bias_rest[128:WT, :] = edge_bias[1].T[0:16, :]
    deal = ((iota((WT, 128), 0) - 128) == iota((WT, 128), 1) % 16).astype(F32).astype(BF16)
    gather_up = (iota((128, WT), 0) % 16 == (iota((128, WT), 1) - 128)).astype(F32).astype(BF16)
    own_rows = (iota((256, 128), 0) // HEAD_SIZE == iota((256, 128), 1) // 16).astype(F32)
    own_cols = (iota((128, 256), 0) // 16 == iota((128, 256), 1) // HEAD_SIZE).astype(F32)

    for name in ("wo", "wq0", "wq1", "wq2", "pad", "x", "cot", "gain"):
        loads[name].wait()
    wot[...] = wo[...].T
    for block, start in enumerate((256, 0, 384, 128, 512, 640)):
        wqt[128 * block:128 * block + 128, :] = wq[:, start:start + 128].T

    arrived(xw.at[:, three], XS)
    tokens = xw[...].astype(F32).reshape(WT, FEAT)
    center = tokens - jnp.mean(tokens, axis=-1, keepdims=True)
    variance = jnp.mean(center * center, axis=-1, keepdims=True)
    inv_std = lax.rsqrt(variance + EPSILON)
    standard = center * inv_std
    std[...] = standard
    istd[...] = inv_std
    nrm[0] = (standard * gain_ref[...]).astype(BF16)
    send(nrm.at[0], nrm.at[1], PAIR, PAIR, sibling)

    def project(w):
        proj[w] = mm(nrm[w], wq[...]).astype(BF16)
        projt[w] = proj[w].T
        nrmt[w] = nrm[w].T

    project(0)

    for n in range(3):
        arrived(pads.at[n], PADS + n)
    padf[...] = jnp.zeros((32, 128), F32)
    padf[0:6, 0:12] = pad_ref[...].astype(F32)
    for n, slot_at in enumerate((3, 1, 2)):
        padf[8 * slot_at:8 * slot_at + 6, 0:12] = pads[n].astype(F32)

    def spot(token_at):
        row, col = token_at // 24, (token_at % 24) // 2
        slot = (row >= 3).astype(I32) * 2 + (col >= 6).astype(I32)
        return slot, row + jnp.where(row < 3, 3, -3), col + jnp.where(col < 6, 6, -6)

    slot, source_row, unused = spot(iota((WT, 32), 0))
    row_pick = (iota((WT, 32), 1) == slot * 8 + source_row).astype(BF16)
    unused, unused, source_col = spot(iota((WT, 128), 0))
    picked = mm(row_pick, padf[...].astype(BF16))
    valid = jnp.sum(jnp.where(iota((WT, 128), 1) == source_col, picked, 0.0), axis=1, keepdims=True)
    validb[0] = jnp.broadcast_to(valid, (WT, 128)).astype(BF16)
    send(validb.at[0], validb.at[1], PAIR + 1, PAIR + 1, sibling)

    def see(w):
        key, query = iota((WT, WT), 0), iota((WT, WT), 1)
        across = lat + w * (1 - 2 * core) == 15
        same_group = ((key >= 72) == (query >= 72)) | jnp.logical_not(across)
        valid_key = validb[w].astype(F32)[:, 0:1] > 0.5
        seen = (same_group & (valid_key | (key == query))).astype(F32)
        allow[w] = seen[:, 0:128]
        allow_rest[w] = mm(seen.astype(BF16), deal)

    see(0)

    def project_cot(w):
        gatt[w] = mm(cotf[w], wot[...]).astype(BF16)
        gattt[w] = gatt[w].T

    lane_head = iota((1, 128), 1) // HEAD_SIZE
    mine = [(lane_head == j).astype(F32).astype(BF16) for j in range(4)]

    def apart(group):
        return jnp.concatenate([group * mine[j] for j in range(4)], axis=0)

    def own_blocks(wide):
        return [wide[32 * j:32 * j + 32, 128 * j:128 * j + 128].astype(BF16) for j in range(4)]

    def softmax(scores, seen, added):
        scores = jnp.where(seen > 0.5, scores * SCORE_SCALE + added, MASKED)
        exponent = jnp.exp(scores - jnp.max(scores, axis=0, keepdims=True))
        return exponent * (1.0 / jnp.sum(exponent, axis=0, keepdims=True))

    def softmax_grad(prob, grad_probs):
        return prob * (grad_probs - jnp.sum(prob * grad_probs, axis=0, keepdims=True))

    def fold(wide):
        return mm((wide * own_rows).astype(BF16), gather_up)[:, 128:WT].astype(BF16)

    def attend(w):
        rest_queries = (mm(projt[w, 0:256, :], deal) * own_rows).astype(BF16)
        prob = softmax(mm(proj[w, :, 256:512], rest_queries), allow_rest[w], bias_rest[...])
        probs_rest[w] = prob
        attt[w, :, 128:WT] = fold(mm(projt[w, 512:768, :], prob.astype(BF16)))

        for group in range(2):
            here = slice(128 * group, 128 * group + 128)
            keys_at, values_at = slice(256 + here.start, 256 + here.stop), slice(512 + here.start, 512 + here.stop)
            scores = mm(apart(proj[w, :, keys_at]), projt[w, here, 0:128])
            four = []
            for j in range(4):
                head = group * 4 + j
                prob = softmax(scores[WT * j:WT * j + WT], allow[w], bias[head])
                probs[w, head] = prob
                four.append(prob.astype(BF16))
            four = jnp.concatenate(four, axis=1)
            for j, block in enumerate(own_blocks(mm(projt[w, values_at, :], four))):
                attt[w, 32 * (4 * group + j):32 * (4 * group + j) + 32, 0:128] = block
            probs_b[w, group] = four

    def values_grad(w):
        rest_cot = (mm(gather_up, gatt[w]) * own_cols).astype(BF16)
        rest = mm(probs_rest[w].astype(BF16), rest_cot)
        for group in range(2):
            here = slice(128 * group, 128 * group + 128)
            grad_values = rest[:, here] + mm(probs_b[w, group], apart(gatt[w, 0:128, here]))
            gnat[w, :, 512 + here.start:512 + here.stop] = grad_values.astype(BF16)

    def backward_rest(w):
        rest_cot = (mm(gattt[w], deal) * own_rows).astype(BF16)
        grad_scores = softmax_grad(probs_rest[w], mm(proj[w, :, 512:768], rest_cot))
        if w == 0:
            ds_rest[0:WT, :] = grad_scores
        else:
            ds_rest[0:WT, :] = ds_rest[0:WT, :] + grad_scores
        grad_b = grad_scores.astype(BF16)
        gradt[w, :, 128:WT] = fold(mm(projt[w, 256:512, :], grad_b) * SCORE_SCALE)
        rest_queries = (mm(gather_up, proj[w, :, 0:256]) * own_cols).astype(BF16)
        keys_rest[w] = mm(grad_b, rest_queries)

    def backward_group(w, group):
        here = slice(128 * group, 128 * group + 128)
        keys_at, values_at = slice(256 + here.start, 256 + here.stop), slice(512 + here.start, 512 + here.stop)
        grad_probs = mm(apart(proj[w, :, values_at]), gattt[w, here, 0:128])
        four = []
        for j in range(4):
            head = group * 4 + j
            grad_scores = softmax_grad(probs[w, head], grad_probs[WT * j:WT * j + WT])
            if w == 0:
                ds[head] = grad_scores
            else:
                ds[head] = ds[head] + grad_scores
            four.append(grad_scores.astype(BF16))
        four = jnp.concatenate(four, axis=1)
        for j, block in enumerate(own_blocks(mm(projt[w, keys_at, :], four) * SCORE_SCALE)):
            gradt[w, 32 * (4 * group + j):32 * (4 * group + j) + 32, 0:128] = block
        grad_keys = keys_rest[w, :, here] + mm(four, apart(proj[w, 0:128, here]))
        gnat[w, :, 256 * group:256 * group + 128] = (grad_keys * SCORE_SCALE).astype(BF16)
        gnat[w, :, 256 * group + 128:256 * group + 256] = gradt[w, here, :].T

    attend(0)
    arrived(cw.at[:, three], COTS)
    cotf[0] = cw[...].reshape(WT, FEAT)
    send(cotf.at[0], cotf.at[1], PAIR + 2, PAIR + 2, sibling)
    project_cot(0)
    arrived(nrm.at[1], PAIR)
    project(1)
    arrived(validb.at[1], PAIR + 1)
    see(1)
    attend(1)
    values_grad(0)
    arrived(cotf.at[1], PAIR + 2)
    project_cot(1)
    values_grad(1)

    major, minor = (x, y), (y, x)
    at_major, at_minor = (at_x, at_y), (at_y, at_x)
    chunk_at = (0, 1024, 1536)
    chunk_rows = (256, 128, 128)

    def columns(lanes):
        return mm(nrmt[0], gnat[0, :, lanes]) + mm(nrmt[1], gnat[1, :, lanes])

    def scatter_pay(e):
        count = chunk_rows[e]
        for d in RING4:
            for p in range(2):
                to = (major[p] + d) % 4
                send(
                    pay.at[p, span(chunk_at[e] + count * to, count)],
                    r1.at[p, d - 1, pl.ds(128 * e + 128 * (e > 0), count)],
                    RS1 + e, R_RS1 + e, at_major[p](to),
                )

    out = columns(slice(512, 768))
    for p in range(2):
        pay[p, 0:512, :] = out[:, 128 * p:128 * p + 128].astype(BF16)
    out = mm(attt[0], cotf[0]) + mm(attt[1], cotf[1])
    for p in range(2):
        for u in range(2):
            lanes = slice(256 * p + 128 * u, 256 * p + 128 * u + 128)
            pay[p, 512 + 256 * u:768 + 256 * u, :] = out[:, lanes].astype(BF16)
    scatter_pay(0)
    for w in range(2):
        backward_rest(w)
    for group in range(2):
        for w in range(2):
            backward_group(w, group)
        rows = slice(1024 + 512 * group, 1536 + 512 * group)
        out = columns(slice(256 * group, 256 * group + 256))
        for p in range(2):
            pay[p, rows, :] = out[:, 128 * p:128 * p + 128].astype(BF16)
        scatter_pay(1 + group)

    gn_send[...] = mm(gnat[1], wqt[...])
    send(gn_send, gn_recv, PAIR + 3, PAIR + 3, sibling)
    grad_normed = mm(gnat[0], wqt[...])

    def table_part(pairs):
        upper, pieces = [], []
        for index, rows_in in pairs:
            lanes = index.shape[1]
            upper.append((iota((48, lanes), 0) == (index >> 4)).astype(F32).astype(BF16))
            match = iota((16, lanes), 0) == (index & 15)
            pieces.append(jnp.concatenate(
                [jnp.where(match, jnp.broadcast_to(row, (16, lanes)), 0.0) for row in rows_in], axis=0
            ).astype(BF16))
        return mm(jnp.concatenate(pieces, axis=1), jnp.concatenate(upper, axis=1), NT)

    def scatter(step, total):
        rows = pl.ds(pl.multiple_of(8 * step, 8), 8)
        indices = relt[rows, :]
        values = [ds[h, rows, :] for h in range(8)]
        return total + table_part([(indices[k:k + 1, :], [one[k:k + 1, :] for one in values]) for k in range(8)])

    total = lax.fori_loop(0, WT // 8, scatter, jnp.zeros((128, 48), F32))

    for e in range(3):
        count = chunk_rows[e]
        rows = slice(128 * e + 128 * (e > 0), 128 * e + 128 * (e > 0) + count)
        arrived(r1.at[:, :, pl.ds(rows.start, count)], R_RS1 + e)
        for p in range(2):
            value = pay[p, span(chunk_at[e] + count * major[p], count), :].astype(F32)
            for d in range(3):
                value = value + r1[p, d, rows, :].astype(F32)
            s1[p, rows, :] = value.astype(BF16)
    for d in RING4:
        for p in range(2):
            to = (minor[p] + d) % 4
            send(s1.at[p, span(128 * to, 128)], r2.at[p, d - 1], RS2, R_RS2 + p, at_minor[p](to))

    arrived(gn_recv, PAIR + 3)
    grad_normed = grad_normed + gn_recv[...]
    standard = std[...]
    grad_gain = jnp.sum(grad_normed * standard, axis=0, keepdims=True)

    turned_rest = ds_rest[...].T
    turned = total
    for half in range(2):
        turned = turned + table_part([
            (edge_row[n:n + 1, :], [turned_rest[16 * h + n:16 * h + n + 1, :] for h in range(8)])
            for n in range(8 * half, 8 * half + 8)
        ])
    upper_part = turned.astype(BF16)
    lower_part = (turned - upper_part.astype(F32)).astype(BF16)
    spread = (iota((48, 768), 1) // 16 == iota((48, 768), 0)).astype(F32).astype(BF16)
    wide = mm(upper_part, spread) + mm(lower_part, spread)
    wide = jnp.where(iota((128, 768), 1) % 16 == iota((128, 768), 0) % 16, wide, 0.0)
    wide = jnp.sum(wide.reshape(8, 16, 768), axis=1)
    tb[...] = jnp.zeros((64, 128), F32)
    for c in range(6):
        tb[8 * c:8 * c + 8, :] = wide[:, 128 * c:128 * c + 128]
    for c in range(4):
        tb[48 + c:49 + c, :] = grad_gain[:, 128 * c:128 * c + 128]
    for d in RING4:
        to = (x + d) % 4
        send(tb.at[span(16 * to, 16)], rt1.at[d - 1], TX, R_TX, at_x(to))

    for p in range(2):
        arrived(r2.at[p], R_RS2 + p)
        value = s1[p, span(128 * minor[p], 128), :].astype(F32)
        for d in range(3):
            value = value + r2[p, d].astype(F32)
        s2[p] = value.astype(BF16)
    for d in RING8:
        to = (z + d) % 8
        send(s2.at[:, span(16 * to, 16)], r3.at[d - 1], RS3, R_RS3, at_z(to))

    grad_hat = grad_normed * gain_ref[...]
    grad_in = istd[...] * (
        grad_hat
        - jnp.mean(grad_hat, axis=-1, keepdims=True)
        - standard * jnp.mean(grad_hat * standard, axis=-1, keepdims=True)
    )
    back_send[...] = grad_in.astype(BF16).reshape(6, 12, 2, FEAT)
    ginf[...] = grad_in.reshape(6, 12, 2, FEAT)

    returns = (
        ((3, 6), (0, 0), (east, north)),
        ((0, 6), (3, 0), (east, lat)),
        ((3, 0), (0, 6), (lon, north)),
    )
    for source, target, device in returns:
        send(
            back_send.at[pl.ds(source[0], 3), pl.ds(source[1], 6)],
            back_recv.at[pl.ds(target[0], 3), pl.ds(target[1], 6)],
            BACK, R_BACK, device,
        )

    arrived(rt1, R_TX)
    value = tb[span(16 * x, 16), :]
    for d in range(3):
        value = value + rt1[d]
    t2[...] = value
    for d in RING4:
        send(t2, rt2.at[d - 1], TY, R_TY, at_y((y + d) % 4))

    arrived(r3, R_RS3)
    for p in range(2):
        value = s2[p, span(16 * z, 16), :].astype(F32)
        for d in range(7):
            value = value + r3[d, p].astype(F32)
        g1[p, span(16 * z, 16), :] = value.astype(BF16)
    mine_z = g1.at[:, span(16 * z, 16)]
    for d in RING8:
        send(mine_z, mine_z, AG1, R_AG1, at_z((z + d) % 8))

    arrived(rt2, R_TY)
    value = t2[...]
    for d in range(3):
        value = value + rt2[d]
    t3[...] = value
    for d in RING8:
        send(t3, rt3.at[d - 1], TZ, R_TZ, at_z((z + d) % 8))

    base1 = [512 * major[p] for p in range(2)]
    base2 = [base1[p] + 128 * minor[p] for p in range(2)]
    arrived(pay.at[0, pl.ds(0, 224)], R_AG1)
    into2 = {1: R_AG2, 3: R_AG2 + 1, 2: R_AG2 + 2}

    def spread_major(p, e):
        rows = span(base1[p] + 128 * ((minor[p] + 4 - e) % 4), 128)
        part = big_ref.at[core, p, rows]
        for d in RING4:
            send(g1.at[p] if e == 0 else part, part, AG3, R_AG3 + e, at_major[p]((major[p] + d) % 4))

    for d in RING4:
        for p in range(2):
            send(g1.at[p], big_ref.at[core, p, span(base2[p], 128)], AG2, into2[d], at_minor[p]((minor[p] + d) % 4))
    for p in range(2):
        spread_major(p, 0)
    for p in range(2):
        big_ref[core, p, span(base2[p], 128), :] = g1[p]

    arrived(rt3, R_TZ)
    value = t3[...]
    for d in range(7):
        value = value + rt3[d]
    mine_t = tf.at[span(16 * x, 16)]
    mine_t[...] = value * GRAD_SCALE
    for d in RING4:
        send(mine_t, mine_t, TXG, R_TXG, at_x((x + d) % 4))

    def forward(p, row, count):
        part = big_ref.at[core, p, span(row, count)]
        send(part, part, SIB, R_SIB, sibling)

    for e in (1, 3, 2):
        arrived(g1, into2[e])
        for p in range(2):
            spread_major(p, e)
    for p in range(2):
        forward(p, base1[p], 512)

    arrived(rt1, R_TXG)
    send(tf, tf_recv, TSIB, R_TSIB, sibling)

    arrived(back_recv.at[:, three], R_BACK)
    gin_ref[0:3, 0:6] = back_recv[0:3, 0:6].astype(F32)
    gin_ref[0:3, 6:12] = back_recv[0:3, 6:12].astype(F32)
    gin_ref[3:6, 0:6] = back_recv[3:6, 0:6].astype(F32)
    gin_ref[3:6, 6:12] = ginf[0:3, 0:6]

    left(xw.at[:, three], XS)
    left(cw.at[:, three], COTS)
    for n in range(3):
        left(pads.at[n], PADS + n)
    left(nrm.at[1], PAIR)
    left(validb.at[1], PAIR + 1)
    left(cotf.at[1], PAIR + 2)
    left(gn_recv, PAIR + 3)
    for e in range(3):
        left(pay.at[0, pl.ds(0, 6 * chunk_rows[e])], RS1 + e)
    left(pay.at[0, pl.ds(0, 768)], RS2)
    left(r3, RS3)
    left(pay.at[0, pl.ds(0, 224)], AG1)
    left(rt1, TX)
    left(rt2, TY)
    left(rt3, TZ)
    left(back_recv.at[:, three], BACK)

    for e in (0, 1, 3, 2):
        arrived(pay.at[0, pl.ds(0, 768)], R_AG3 + e)
        for d in (1, 3, 2):
            for p in range(2):
                forward(p, 512 * ((major[p] + 4 - d) % 4) + 128 * ((minor[p] + 4 - e) % 4), 128)
    left(pay.at[0, pl.ds(0, 768)], AG2)
    left(pay.at[:, pl.ds(0, 1536)], AG3)
    left(rt1, TXG)

    arrived(tf_recv, R_TSIB)
    left(tf, TSIB)
    for half, at in ((tf, core), (tf_recv, 1 - core)):
        rows = pl.ds(pl.multiple_of(8 * at, 8), 8)
        for c in range(5):
            table_ref[rows, 128 * c:128 * c + 128] = half[8 * c:8 * c + 8, :]
        table_ref[rows, 640:NBIAS] = half[40:48, 0:NBIAS - 640]
    for c in range(4):
        ggain_ref[:, 128 * c:128 * c + 128] = tf[48 + c:49 + c, :] + tf_recv[48 + c:49 + c, :]

    arrived(big_ref.at[1 - core], R_SIB)
    left(pay, SIB)


def widen(big, gin, table, gain, gin_out, gain_out, wqkv_out, wout_out, table_out, wqkv, wout, sem):
    made = [
        pltpu.make_async_copy(gin, gin_out, sem.at[0]),
        pltpu.make_async_copy(gain, gain_out, sem.at[1]),
        pltpu.make_async_copy(table, table_out, sem.at[2]),
    ]
    for one in made:
        one.start()
    for step in range(4):
        rows = slice(128 * step, 128 * step + 128)
        for block in range(3):
            for core in range(2):
                for p in range(2):
                    lanes = slice(512 * block + 256 * core + 128 * p, 512 * block + 256 * core + 128 * p + 128)
                    if block == 2:
                        column, start = p, 512 * (step // 2) + 128 * (step % 2)
                    else:
                        column, start = 1 - block, 512 * step + 256 + 128 * p
                    wqkv[rows, lanes] = big[core, column, start:start + 128, :].astype(F32) * GRAD_SCALE
        one = pltpu.make_async_copy(wqkv.at[pl.ds(128 * step, 128)], wqkv_out.at[pl.ds(128 * step, 128)], sem.at[3 + step])
        one.start()
        made.append(one)
        core, half = step // 2, step % 2
        for p in range(2):
            for u in range(2):
                start = 1024 + 512 * u + 128 * half
                lanes = slice(256 * p + 128 * u, 256 * p + 128 * u + 128)
                wout[rows, lanes] = big[core, p, start:start + 128, :].astype(F32) * GRAD_SCALE
        one = pltpu.make_async_copy(wout.at[pl.ds(128 * step, 128)], wout_out.at[pl.ds(128 * step, 128)], sem.at[7 + step])
        one.start()
        made.append(one)
    for one in made:
        one.wait()


def per_device(inputs, cotangent, pad_mask, rel_index, bias_table, ln_gain, w_qkv, w_out):
    vmem = pl.BlockSpec(memory_space=pltpu.VMEM)
    hbm = pl.BlockSpec(memory_space=pltpu.HBM)
    big, grad_in, table, gain = pl.pallas_call(
        body,
        out_shape=(
            jax.ShapeDtypeStruct((2, 2, 2048, 128), BF16),
            jax.ShapeDtypeStruct((6, 12, 2, FEAT), F32),
            jax.ShapeDtypeStruct((HEADS, NBIAS), F32),
            jax.ShapeDtypeStruct((1, FEAT), F32),
        ),
        in_specs=[hbm] * 8,
        out_specs=[vmem] * 4,
        scratch_shapes=[
            pltpu.VMEM((6, 12), I32),
            pltpu.VMEM((WT, WT), I32),
            pltpu.VMEM((8, NBIAS), F32),
            pltpu.VMEM((1, FEAT), F32),
            pltpu.VMEM((FEAT, 768), BF16),
            pltpu.VMEM((256, FEAT), BF16),
            pltpu.VMEM((768, FEAT), BF16),
            pltpu.VMEM((FEAT, 256), BF16),
            pltpu.VMEM((6, 12, 2, FEAT), BF16),
            pltpu.VMEM((6, 12, 2, FEAT), BF16),
            pltpu.VMEM((3, 6, 12), I32),
            pltpu.VMEM((32, 128), F32),
            pltpu.VMEM((WT, 128), I32),
            pltpu.VMEM((8, 1, 768), F32),
            pltpu.VMEM((16, 256), I32),
            pltpu.VMEM((2, 16, 128), I32),
            pltpu.VMEM((2, 128, 128), F32),
            pltpu.VMEM((8, WT, 128), F32),
            pltpu.VMEM((WT, 128), F32),
            pltpu.VMEM((2, WT, 128), BF16),
            pltpu.VMEM((2, WT, 128), F32),
            pltpu.VMEM((2, WT, 128), F32),
            pltpu.VMEM((WT, FEAT), F32),
            pltpu.VMEM((WT, 1), F32),
            pltpu.VMEM((2, WT, FEAT), BF16),
            pltpu.VMEM((2, FEAT, WT), BF16),
            pltpu.VMEM((2, WT, FEAT), BF16),
            pltpu.VMEM((2, WT, 768), BF16),
            pltpu.VMEM((2, 768, WT), BF16),
            pltpu.VMEM((2, WT, 256), BF16),
            pltpu.VMEM((2, 256, WT), BF16),
            pltpu.VMEM((2, 256, WT), BF16),
            pltpu.VMEM((2, 256, WT), BF16),
            pltpu.VMEM((2, WT, 768), BF16),
            pltpu.VMEM((2, 8, WT, 128), F32),
            pltpu.VMEM((2, WT, 128), F32),
            pltpu.VMEM((2, WT, 256), F32),
            pltpu.VMEM((2, 2, WT, 512), BF16),
            pltpu.VMEM((8, WT, 128), F32),
            pltpu.VMEM((256, 128), F32),
            pltpu.VMEM((WT, FEAT), F32),
            pltpu.VMEM((WT, FEAT), F32),
            pltpu.VMEM((2, 2048, 128), BF16),
            pltpu.VMEM((2, 3, 512, 128), BF16),
            pltpu.VMEM((2, 512, 128), BF16),
            pltpu.VMEM((2, 3, 128, 128), BF16),
            pltpu.VMEM((2, 128, 128), BF16),
            pltpu.VMEM((7, 2, 16, 128), BF16),
            pltpu.VMEM((2, 128, 128), BF16),
            pltpu.VMEM((64, 128), F32),
            pltpu.VMEM((3, 16, 128), F32),
            pltpu.VMEM((16, 128), F32),
            pltpu.VMEM((3, 16, 128), F32),
            pltpu.VMEM((16, 128), F32),
            pltpu.VMEM((7, 16, 128), F32),
            pltpu.VMEM((64, 128), F32),
            pltpu.VMEM((64, 128), F32),
            pltpu.VMEM((6, 12, 2, FEAT), BF16),
            pltpu.VMEM((6, 12, 2, FEAT), BF16),
            pltpu.VMEM((6, 12, 2, FEAT), F32),
            pltpu.SemaphoreType.DMA((SENDS,)),
            pltpu.SemaphoreType.DMA((RECVS,)),
            pltpu.SemaphoreType.DMA((10,)),
        ],
        compiler_params=pltpu.CompilerParams(
            collective_id=0, has_side_effects=True, vmem_limit_bytes=48 * 1024 * 1024
        ),
    )(
        *(
            pltpu.with_memory_space_constraint(one, pltpu.HBM)
            for one in (
                inputs.transpose(1, 2, 0, 3),
                cotangent.transpose(1, 2, 0, 3),
                pad_mask,
                rel_index,
                bias_table.T,
                ln_gain.reshape(1, FEAT),
                w_qkv,
                w_out,
            )
        )
    )
    grad_in, gain, wqkv, wout, table = pl.pallas_call(
        widen,
        out_shape=(
            jax.ShapeDtypeStruct((6, 12, 2, FEAT), F32),
            jax.ShapeDtypeStruct((1, FEAT), F32),
            jax.ShapeDtypeStruct((FEAT, 3 * FEAT), F32),
            jax.ShapeDtypeStruct((FEAT, FEAT), F32),
            jax.ShapeDtypeStruct((HEADS, NBIAS), F32),
        ),
        in_specs=[vmem] * 4,
        out_specs=[hbm] * 5,
        scratch_shapes=[
            pltpu.VMEM((FEAT, 3 * FEAT), F32),
            pltpu.VMEM((FEAT, FEAT), F32),
            pltpu.SemaphoreType.DMA((11,)),
        ],
        compiler_params=pltpu.CompilerParams(vmem_limit_bytes=24 * 1024 * 1024),
    )(big, grad_in, table, gain)
    return grad_in.transpose(2, 0, 1, 3), gain.reshape(FEAT), wqkv, wout, table.T


def solution(mesh):
    in_specs = (
        P(None, "lat", "lon", None),
        P(None, "lat", "lon", None),
        P("lat", "lon"),
        P(),
        P(),
        P(),
        P(),
        P(),
    )
    out_specs = (P(None, "lat", "lon", None), P(), P(), P(), P())
    return jax.shard_map(
        per_device, mesh=mesh, in_specs=in_specs, out_specs=out_specs, check_vma=False
    )
```

```python
import jax
import jax.numpy as jnp
from jax import lax
from jax.experimental import pallas as pl
from jax.experimental.pallas import tpu as pltpu
from jax.sharding import PartitionSpec as P

F32 = jnp.float32
BF16 = jnp.bfloat16
I32 = jnp.int32
MESH = pl.DeviceIdType.MESH

EPSILON = 1e-05
MASKED = -30000.0
WT = 144
FEAT = 512
HEADS = 16
HEAD_SIZE = 32
NBIAS = 759
SCORE_SCALE = HEAD_SIZE ** (-0.5)
GRAD_SCALE = 36864.0 ** (-0.5)

NN = (((1,), (0,)), ((), ()))
NT = (((1,), (1,)), ((), ()))

XS, COTS, PADS, PAIR, RS1, RS2, RS3, AG1, AG2, AG3, SIB = 0, 1, 2, 5, 9, 12, 13, 14, 15, 16, 17
TX, TY, TZ, TXG, TSIB, BACK = 18, 19, 20, 21, 22, 23
SENDS = 24
R_RS1, R_RS2, R_RS3, R_AG1, R_AG2, R_AG3, R_SIB = 9, 12, 14, 15, 16, 19, 23
R_TX, R_TY, R_TZ, R_TXG, R_TSIB, R_BACK = 24, 25, 26, 27, 28, 29
RECVS = 30

RING4 = (2, 1, 3)
RING8 = (4, 3, 5, 2, 6, 1, 7)


def mm(a, b, dims=NN):
    return lax.dot_general(a, b, dims, preferred_element_type=F32)


def iota(shape, dim):
    return lax.broadcasted_iota(I32, shape, dim)


def body(
    x_ref, cot_ref, pad_hbm, rel_hbm, bias_hbm, gain_hbm, wqkv_hbm, wout_hbm,
    big_ref, gin_ref, table_ref, ggain_ref,
    pad_ref, rel_ref, bias_ref, gain_ref, wq, wo, wqt, wot,
    xw, cw, pads, padf, relt, tab, edge_row, edge, edge_bias, bias, bias_rest, validb, allow, allow_rest, std, istd, nrm, nrmt, cotf,
    proj, projt, gatt, gattt, attt, gradt, gnat, probs, probs_rest, keys_rest, probs_b, ds, ds_rest, gn_send, gn_recv,
    pay, r1, s1, r2, s2, r3, g1,
    tb, rt1, t2, rt2, t3, rt3, tf, tf_recv,
    back_send, back_recv, ginf, ssem, rsem, lsem,
):
    lon = lax.axis_index("lon")
    lat = lax.axis_index("lat")
    z, xhi = lon // 2, lon % 2
    xlo, rest = lat // 8, lat % 8
    y, core = rest // 2, rest % 2
    x = xhi * 2 + xlo

    def at_x(value):
        return (z * 2 + value // 2, (value % 2) * 8 + rest)

    def at_y(value):
        return (lon, xlo * 8 + value * 2 + core)

    def at_z(value):
        return (value * 2 + xhi, lat)

    sibling = (lon, xlo * 8 + y * 2 + (1 - core))
    west, east = (lon + 15) % 16, (lon + 1) % 16
    south, north = (lat + 15) % 16, (lat + 1) % 16

    def send(src, dst, out, into, device):
        pltpu.make_async_remote_copy(
            src_ref=src, dst_ref=dst, send_sem=ssem.at[out], recv_sem=rsem.at[into],
            device_id=device, device_id_type=MESH,
        ).start()

    def arrived(bytes_of, into):
        pltpu.make_async_copy(bytes_of, bytes_of, rsem.at[into]).wait()

    def left(bytes_of, out):
        pltpu.make_async_copy(bytes_of, bytes_of, ssem.at[out]).wait()

    def span(start, count):
        return pl.ds(pl.multiple_of(start, 16), count)

    barrier = pltpu.get_barrier_semaphore()
    partners = [at_z((z + d) % 8) for d in RING8]
    partners += [(west, south), (east, north), (west, lat), (east, lat)]
    partners += [at_x((x + d) % 4) for d in RING4] + [at_y((y + d) % 4) for d in RING4]
    partners += [(lon, south), (lon, north), sibling]
    for device in partners:
        pl.semaphore_signal(barrier, inc=1, device_id=device, device_id_type=MESH)

    loads = {}
    heads_at = 256 * core
    parts = [
        ("rel", rel_hbm, rel_ref),
        ("bias", bias_hbm.at[pl.ds(pl.multiple_of(8 * core, 8), 8)], bias_ref),
        ("x", x_ref.at[pl.ds(3, 3), pl.ds(6, 6)], xw.at[pl.ds(0, 3), pl.ds(0, 6)]),
        ("cot", cot_ref.at[pl.ds(3, 3), pl.ds(6, 6)], cw.at[pl.ds(0, 3), pl.ds(0, 6)]),
        ("pad", pad_hbm, pad_ref),
        ("gain", gain_hbm, gain_ref),
        ("wo", wout_hbm.at[span(heads_at, 256)], wo),
    ]
    for block in range(3):
        lanes = pl.ds(pl.multiple_of(FEAT * block + heads_at, 128), 256)
        parts.append(("wq%d" % block, wqkv_hbm.at[:, lanes], wq.at[:, pl.ds(256 * block, 256)]))
    for n, (name, src, dst) in enumerate(parts):
        loads[name] = pltpu.make_async_copy(src, dst, lsem.at[n])
        loads[name].start()

    pl.semaphore_wait(barrier, len(partners))

    places = (
        ((0, 0), (3, 6), (west, south)),
        ((3, 0), (0, 6), (west, lat)),
        ((0, 6), (3, 0), (lon, south)),
    )
    three = pl.ds(0, 9)

    def send_quarters(field, window, index):
        for source, target, device in places:
            send(
                field.at[pl.ds(source[0], 3), pl.ds(source[1], 6)],
                window.at[pl.ds(target[0], 3), pl.ds(target[1], 6)],
                index, index, device,
            )

    send_quarters(x_ref, xw, XS)
    for n, (unused, unused, device) in enumerate(places):
        send(pad_hbm, pads.at[n], PADS + n, PADS + n, device)

    for name in ("rel", "bias"):
        loads[name].wait()
    token = iota((WT, WT), 0)
    order = (iota((WT, WT), 1) == (token % 2) * 72 + token // 2).astype(BF16)
    rel = rel_ref[...]
    low = mm(mm(order, (rel & 255).astype(F32).astype(BF16), NT).astype(BF16), order, NT)
    high = mm(mm(order, (rel >> 8).astype(F32).astype(BF16), NT).astype(BF16), order, NT)
    index = (high * 256.0 + low).astype(I32)
    relt[...] = index[:, 0:128]
    edge_row[...] = jnp.zeros((16, 256), I32)
    edge_row[:, 0:WT] = index.T[128:WT, :]
    ds_rest[...] = jnp.zeros((256, 128), F32)
    edge[0] = edge_row[:, 0:128]
    edge[1] = edge_row[:, 128:256]
    tab[...] = jnp.zeros((8, 1, 768), F32)
    for head in range(8):
        tab[head, :, :NBIAS] = bias_ref[head:head + 1, :]

    def gather_heads(index, put):
        lane, chunk = index & 127, index >> 7
        inside = [chunk == c for c in range(6)]
        for head in range(8):
            found = jnp.zeros(index.shape, F32)
            for c in range(6):
                row = jnp.broadcast_to(tab[head, :, 128 * c:128 * c + 128], index.shape)
                taken = jnp.take_along_axis(row, lane, axis=1, mode="promise_in_bounds")
                found = jnp.where(inside[c], taken, found)
            put(head, found)

    def lookup(step, carry):
        rows = pl.ds(pl.multiple_of(8 * step, 8), 8)

        def put(head, found):
            bias[head, rows, :] = found

        gather_heads(relt[rows, :], put)
        return carry

    lax.fori_loop(0, 9, lookup, 0)
    send_quarters(cot_ref, cw, COTS)
    lax.fori_loop(9, WT // 8, lookup, 0)
    def lookup_rest(step, carry):
        part, half = step // 2, pl.ds(pl.multiple_of(8 * (step % 2), 8), 8)

        def put(head, found):
            edge_bias[part, pl.ds(pl.multiple_of(16 * head + 8 * (step % 2), 8), 8), :] = found

        gather_heads(edge[part, half, :], put)
        return carry

    lax.fori_loop(0, 4, lookup_rest, 0)
    bias_rest[0:128, :] = edge_bias[0].T
    bias_rest[128:WT, :] = edge_bias[1].T[0:16, :]
    deal = ((iota((WT, 128), 0) - 128) == iota((WT, 128), 1) % 16).astype(F32).astype(BF16)
    gather_up = (iota((128, WT), 0) % 16 == (iota((128, WT), 1) - 128)).astype(F32).astype(BF16)
    own_rows = (iota((256, 128), 0) // HEAD_SIZE == iota((256, 128), 1) // 16).astype(F32)
    own_cols = (iota((128, 256), 0) // 16 == iota((128, 256), 1) // HEAD_SIZE).astype(F32)

    for name in ("wo", "wq0", "wq1", "wq2", "pad", "x", "cot", "gain"):
        loads[name].wait()
    wot[...] = wo[...].T
    for block, start in enumerate((256, 0, 384, 128, 512, 640)):
        wqt[128 * block:128 * block + 128, :] = wq[:, start:start + 128].T

    arrived(xw.at[:, three], XS)
    tokens = xw[...].astype(F32).reshape(WT, FEAT)
    center = tokens - jnp.mean(tokens, axis=-1, keepdims=True)
    variance = jnp.mean(center * center, axis=-1, keepdims=True)
    inv_std = lax.rsqrt(variance + EPSILON)
    standard = center * inv_std
    std[...] = standard
    istd[...] = inv_std
    nrm[0] = (standard * gain_ref[...]).astype(BF16)
    send(nrm.at[0], nrm.at[1], PAIR, PAIR, sibling)

    def project(w):
        proj[w] = mm(nrm[w], wq[...]).astype(BF16)
        projt[w] = proj[w].T
        nrmt[w] = nrm[w].T

    project(0)

    for n in range(3):
        arrived(pads.at[n], PADS + n)
    padf[...] = jnp.zeros((32, 128), F32)
    padf[0:6, 0:12] = pad_ref[...].astype(F32)
    for n, slot_at in enumerate((3, 1, 2)):
        padf[8 * slot_at:8 * slot_at + 6, 0:12] = pads[n].astype(F32)

    def spot(token_at):
        row, col = token_at // 24, (token_at % 24) // 2
        slot = (row >= 3).astype(I32) * 2 + (col >= 6).astype(I32)
        return slot, row + jnp.where(row < 3, 3, -3), col + jnp.where(col < 6, 6, -6)

    slot, source_row, unused = spot(iota((WT, 32), 0))
    row_pick = (iota((WT, 32), 1) == slot * 8 + source_row).astype(BF16)
    unused, unused, source_col = spot(iota((WT, 128), 0))
    picked = mm(row_pick, padf[...].astype(BF16))
    valid = jnp.sum(jnp.where(iota((WT, 128), 1) == source_col, picked, 0.0), axis=1, keepdims=True)
    validb[0] = jnp.broadcast_to(valid, (WT, 128)).astype(BF16)
    send(validb.at[0], validb.at[1], PAIR + 1, PAIR + 1, sibling)

    def see(w):
        key, query = iota((WT, WT), 0), iota((WT, WT), 1)
        across = lat + w * (1 - 2 * core) == 15
        same_group = ((key >= 72) == (query >= 72)) | jnp.logical_not(across)
        valid_key = validb[w].astype(F32)[:, 0:1] > 0.5
        seen = (same_group & (valid_key | (key == query))).astype(F32)
        allow[w] = seen[:, 0:128]
        allow_rest[w] = mm(seen.astype(BF16), deal)

    see(0)

    def project_cot(w):
        gatt[w] = mm(cotf[w], wot[...]).astype(BF16)
        gattt[w] = gatt[w].T

    lane_head = iota((1, 128), 1) // HEAD_SIZE
    mine = [(lane_head == j).astype(F32).astype(BF16) for j in range(4)]

    def apart(group):
        return jnp.concatenate([group * mine[j] for j in range(4)], axis=0)

    def own_blocks(wide):
        return [wide[32 * j:32 * j + 32, 128 * j:128 * j + 128].astype(BF16) for j in range(4)]

    def softmax(scores, seen, added):
        scores = jnp.where(seen > 0.5, scores * SCORE_SCALE + added, MASKED)
        exponent = jnp.exp(scores - jnp.max(scores, axis=0, keepdims=True))
        return exponent * (1.0 / jnp.sum(exponent, axis=0, keepdims=True))

    def softmax_grad(prob, grad_probs):
        return prob * (grad_probs - jnp.sum(prob * grad_probs, axis=0, keepdims=True))

    def fold(wide):
        return mm((wide * own_rows).astype(BF16), gather_up)[:, 128:WT].astype(BF16)

    def attend(w):
        rest_queries = (mm(projt[w, 0:256, :], deal) * own_rows).astype(BF16)
        prob = softmax(mm(proj[w, :, 256:512], rest_queries), allow_rest[w], bias_rest[...])
        probs_rest[w] = prob
        attt[w, :, 128:WT] = fold(mm(projt[w, 512:768, :], prob.astype(BF16)))

        for group in range(2):
            here = slice(128 * group, 128 * group + 128)
            keys_at, values_at = slice(256 + here.start, 256 + here.stop), slice(512 + here.start, 512 + here.stop)
            scores = mm(apart(proj[w, :, keys_at]), projt[w, here, 0:128])
            four = []
            for j in range(4):
                head = group * 4 + j
                prob = softmax(scores[WT * j:WT * j + WT], allow[w], bias[head])
                probs[w, head] = prob
                four.append(prob.astype(BF16))
            four = jnp.concatenate(four, axis=1)
            for j, block in enumerate(own_blocks(mm(projt[w, values_at, :], four))):
                attt[w, 32 * (4 * group + j):32 * (4 * group + j) + 32, 0:128] = block
            probs_b[w, group] = four

    def values_grad(w):
        rest_cot = (mm(gather_up, gatt[w]) * own_cols).astype(BF16)
        rest = mm(probs_rest[w].astype(BF16), rest_cot)
        for group in range(2):
            here = slice(128 * group, 128 * group + 128)
            grad_values = rest[:, here] + mm(probs_b[w, group], apart(gatt[w, 0:128, here]))
            gnat[w, :, 512 + here.start:512 + here.stop] = grad_values.astype(BF16)

    def backward_rest(w):
        rest_cot = (mm(gattt[w], deal) * own_rows).astype(BF16)
        grad_scores = softmax_grad(probs_rest[w], mm(proj[w, :, 512:768], rest_cot))
        if w == 0:
            ds_rest[0:WT, :] = grad_scores
        else:
            ds_rest[0:WT, :] = ds_rest[0:WT, :] + grad_scores
        grad_b = grad_scores.astype(BF16)
        gradt[w, :, 128:WT] = fold(mm(projt[w, 256:512, :], grad_b) * SCORE_SCALE)
        rest_queries = (mm(gather_up, proj[w, :, 0:256]) * own_cols).astype(BF16)
        keys_rest[w] = mm(grad_b, rest_queries)

    def backward_group(w, group):
        here = slice(128 * group, 128 * group + 128)
        keys_at, values_at = slice(256 + here.start, 256 + here.stop), slice(512 + here.start, 512 + here.stop)
        grad_probs = mm(apart(proj[w, :, values_at]), gattt[w, here, 0:128])
        four = []
        for j in range(4):
            head = group * 4 + j
            grad_scores = softmax_grad(probs[w, head], grad_probs[WT * j:WT * j + WT])
            if w == 0:
                ds[head] = grad_scores
            else:
                ds[head] = ds[head] + grad_scores
            four.append(grad_scores.astype(BF16))
        four = jnp.concatenate(four, axis=1)
        for j, block in enumerate(own_blocks(mm(projt[w, keys_at, :], four) * SCORE_SCALE)):
            gradt[w, 32 * (4 * group + j):32 * (4 * group + j) + 32, 0:128] = block
        grad_keys = keys_rest[w, :, here] + mm(four, apart(proj[w, 0:128, here]))
        gnat[w, :, 256 * group:256 * group + 128] = (grad_keys * SCORE_SCALE).astype(BF16)
        gnat[w, :, 256 * group + 128:256 * group + 256] = gradt[w, here, :].T

    attend(0)
    arrived(cw.at[:, three], COTS)
    cotf[0] = cw[...].reshape(WT, FEAT)
    send(cotf.at[0], cotf.at[1], PAIR + 2, PAIR + 2, sibling)
    project_cot(0)
    arrived(nrm.at[1], PAIR)
    project(1)
    arrived(validb.at[1], PAIR + 1)
    see(1)
    attend(1)
    values_grad(0)
    arrived(cotf.at[1], PAIR + 2)
    project_cot(1)
    values_grad(1)

    major, minor = (x, y), (y, x)
    at_major, at_minor = (at_x, at_y), (at_y, at_x)
    chunk_at = (0, 1024, 1536)
    chunk_rows = (256, 128, 128)

    def columns(lanes):
        return mm(nrmt[0], gnat[0, :, lanes]) + mm(nrmt[1], gnat[1, :, lanes])

    def scatter_pay(e):
        count = chunk_rows[e]
        for d in RING4:
            for p in range(2):
                to = (major[p] + d) % 4
                send(
                    pay.at[p, span(chunk_at[e] + count * to, count)],
                    r1.at[p, d - 1, pl.ds(128 * e + 128 * (e > 0), count)],
                    RS1 + e, R_RS1 + e, at_major[p](to),
                )

    out = columns(slice(512, 768))
    for p in range(2):
        pay[p, 0:512, :] = out[:, 128 * p:128 * p + 128].astype(BF16)
    out = mm(attt[0], cotf[0]) + mm(attt[1], cotf[1])
    for p in range(2):
        for u in range(2):
            lanes = slice(256 * p + 128 * u, 256 * p + 128 * u + 128)
            pay[p, 512 + 256 * u:768 + 256 * u, :] = out[:, lanes].astype(BF16)
    scatter_pay(0)
    for w in range(2):
        backward_rest(w)
    for group in range(2):
        for w in range(2):
            backward_group(w, group)
        rows = slice(1024 + 512 * group, 1536 + 512 * group)
        out = columns(slice(256 * group, 256 * group + 256))
        for p in range(2):
            pay[p, rows, :] = out[:, 128 * p:128 * p + 128].astype(BF16)
        scatter_pay(1 + group)

    gn_send[...] = mm(gnat[1], wqt[...])
    send(gn_send, gn_recv, PAIR + 3, PAIR + 3, sibling)
    grad_normed = mm(gnat[0], wqt[...])

    def table_part(pairs):
        upper, pieces = [], []
        for index, rows_in in pairs:
            lanes = index.shape[1]
            upper.append((iota((48, lanes), 0) == (index >> 4)).astype(F32).astype(BF16))
            match = iota((16, lanes), 0) == (index & 15)
            pieces.append(jnp.concatenate(
                [jnp.where(match, jnp.broadcast_to(row, (16, lanes)), 0.0) for row in rows_in], axis=0
            ).astype(BF16))
        return mm(jnp.concatenate(pieces, axis=1), jnp.concatenate(upper, axis=1), NT)

    def scatter(step, total):
        rows = pl.ds(pl.multiple_of(8 * step, 8), 8)
        indices = relt[rows, :]
        values = [ds[h, rows, :] for h in range(8)]
        return total + table_part([(indices[k:k + 1, :], [one[k:k + 1, :] for one in values]) for k in range(8)])

    total = lax.fori_loop(0, WT // 8, scatter, jnp.zeros((128, 48), F32))

    for e in range(3):
        count = chunk_rows[e]
        rows = slice(128 * e + 128 * (e > 0), 128 * e + 128 * (e > 0) + count)
        arrived(r1.at[:, :, pl.ds(rows.start, count)], R_RS1 + e)
        for p in range(2):
            value = pay[p, span(chunk_at[e] + count * major[p], count), :].astype(F32)
            for d in range(3):
                value = value + r1[p, d, rows, :].astype(F32)
            s1[p, rows, :] = value.astype(BF16)
    for d in RING4:
        for p in range(2):
            to = (minor[p] + d) % 4
            send(s1.at[p, span(128 * to, 128)], r2.at[p, d - 1], RS2, R_RS2 + p, at_minor[p](to))

    arrived(gn_recv, PAIR + 3)
    grad_normed = grad_normed + gn_recv[...]
    standard = std[...]
    grad_gain = jnp.sum(grad_normed * standard, axis=0, keepdims=True)

    turned_rest = ds_rest[...].T
    turned = total
    for half in range(2):
        turned = turned + table_part([
            (edge_row[n:n + 1, :], [turned_rest[16 * h + n:16 * h + n + 1, :] for h in range(8)])
            for n in range(8 * half, 8 * half + 8)
        ])
    upper_part = turned.astype(BF16)
    lower_part = (turned - upper_part.astype(F32)).astype(BF16)
    spread = (iota((48, 768), 1) // 16 == iota((48, 768), 0)).astype(F32).astype(BF16)
    wide = mm(upper_part, spread) + mm(lower_part, spread)
    wide = jnp.where(iota((128, 768), 1) % 16 == iota((128, 768), 0) % 16, wide, 0.0)
    wide = jnp.sum(wide.reshape(8, 16, 768), axis=1)
    tb[...] = jnp.zeros((64, 128), F32)
    for c in range(6):
        tb[8 * c:8 * c + 8, :] = wide[:, 128 * c:128 * c + 128]
    for c in range(4):
        tb[48 + c:49 + c, :] = grad_gain[:, 128 * c:128 * c + 128]
    for d in RING4:
        to = (x + d) % 4
        send(tb.at[span(16 * to, 16)], rt1.at[d - 1], TX, R_TX, at_x(to))

    for p in range(2):
        arrived(r2.at[p], R_RS2 + p)
        value = s1[p, span(128 * minor[p], 128), :].astype(F32)
        for d in range(3):
            value = value + r2[p, d].astype(F32)
        s2[p] = value.astype(BF16)
    for d in RING8:
        to = (z + d) % 8
        send(s2.at[:, span(16 * to, 16)], r3.at[d - 1], RS3, R_RS3, at_z(to))

    grad_hat = grad_normed * gain_ref[...]
    grad_in = istd[...] * (
        grad_hat
        - jnp.mean(grad_hat, axis=-1, keepdims=True)
        - standard * jnp.mean(grad_hat * standard, axis=-1, keepdims=True)
    )
    back_send[...] = grad_in.astype(BF16).reshape(6, 12, 2, FEAT)
    ginf[...] = grad_in.reshape(6, 12, 2, FEAT)

    returns = (
        ((3, 6), (0, 0), (east, north)),
        ((0, 6), (3, 0), (east, lat)),
        ((3, 0), (0, 6), (lon, north)),
    )
    for source, target, device in returns:
        send(
            back_send.at[pl.ds(source[0], 3), pl.ds(source[1], 6)],
            back_recv.at[pl.ds(target[0], 3), pl.ds(target[1], 6)],
            BACK, R_BACK, device,
        )

    arrived(rt1, R_TX)
    value = tb[span(16 * x, 16), :]
    for d in range(3):
        value = value + rt1[d]
    t2[...] = value
    for d in RING4:
        send(t2, rt2.at[d - 1], TY, R_TY, at_y((y + d) % 4))

    arrived(r3, R_RS3)
    for p in range(2):
        value = s2[p, span(16 * z, 16), :].astype(F32)
        for d in range(7):
            value = value + r3[d, p].astype(F32)
        g1[p, span(16 * z, 16), :] = value.astype(BF16)
    mine_z = g1.at[:, span(16 * z, 16)]
    for d in RING8:
        send(mine_z, mine_z, AG1, R_AG1, at_z((z + d) % 8))

    arrived(rt2, R_TY)
    value = t2[...]
    for d in range(3):
        value = value + rt2[d]
    t3[...] = value
    for d in RING8:
        send(t3, rt3.at[d - 1], TZ, R_TZ, at_z((z + d) % 8))

    base1 = [512 * major[p] for p in range(2)]
    base2 = [base1[p] + 128 * minor[p] for p in range(2)]
    arrived(pay.at[0, pl.ds(0, 224)], R_AG1)
    into2 = {1: R_AG2, 3: R_AG2 + 1, 2: R_AG2 + 2}

    def spread_major(p, e):
        rows = span(base1[p] + 128 * ((minor[p] + 4 - e) % 4), 128)
        part = big_ref.at[core, p, rows]
        for d in RING4:
            send(g1.at[p] if e == 0 else part, part, AG3, R_AG3 + e, at_major[p]((major[p] + d) % 4))

    for d in RING4:
        for p in range(2):
            send(g1.at[p], big_ref.at[core, p, span(base2[p], 128)], AG2, into2[d], at_minor[p]((minor[p] + d) % 4))
    for p in range(2):
        spread_major(p, 0)
    for p in range(2):
        big_ref[core, p, span(base2[p], 128), :] = g1[p]

    arrived(rt3, R_TZ)
    value = t3[...]
    for d in range(7):
        value = value + rt3[d]
    mine_t = tf.at[span(16 * x, 16)]
    mine_t[...] = value * GRAD_SCALE
    for d in RING4:
        send(mine_t, mine_t, TXG, R_TXG, at_x((x + d) % 4))

    def forward(p, row, count):
        part = big_ref.at[core, p, span(row, count)]
        send(part, part, SIB, R_SIB, sibling)

    for e in (1, 3, 2):
        arrived(g1, into2[e])
        for p in range(2):
            spread_major(p, e)
    for p in range(2):
        forward(p, base1[p], 512)

    arrived(rt1, R_TXG)
    send(tf, tf_recv, TSIB, R_TSIB, sibling)

    arrived(back_recv.at[:, three], R_BACK)
    gin_ref[0:3, 0:6] = back_recv[0:3, 0:6].astype(F32)
    gin_ref[0:3, 6:12] = back_recv[0:3, 6:12].astype(F32)
    gin_ref[3:6, 0:6] = back_recv[3:6, 0:6].astype(F32)
    gin_ref[3:6, 6:12] = ginf[0:3, 0:6]

    left(xw.at[:, three], XS)
    left(cw.at[:, three], COTS)
    for n in range(3):
        left(pads.at[n], PADS + n)
    left(nrm.at[1], PAIR)
    left(validb.at[1], PAIR + 1)
    left(cotf.at[1], PAIR + 2)
    left(gn_recv, PAIR + 3)
    for e in range(3):
        left(pay.at[0, pl.ds(0, 6 * chunk_rows[e])], RS1 + e)
    left(pay.at[0, pl.ds(0, 768)], RS2)
    left(r3, RS3)
    left(pay.at[0, pl.ds(0, 224)], AG1)
    left(rt1, TX)
    left(rt2, TY)
    left(rt3, TZ)
    left(back_recv.at[:, three], BACK)

    for e in (0, 1, 3, 2):
        arrived(pay.at[0, pl.ds(0, 768)], R_AG3 + e)
        for d in (1, 3, 2):
            for p in range(2):
                forward(p, 512 * ((major[p] + 4 - d) % 4) + 128 * ((minor[p] + 4 - e) % 4), 128)
    left(pay.at[0, pl.ds(0, 768)], AG2)
    left(pay.at[:, pl.ds(0, 1536)], AG3)
    left(rt1, TXG)

    arrived(tf_recv, R_TSIB)
    left(tf, TSIB)
    for half, at in ((tf, core), (tf_recv, 1 - core)):
        rows = pl.ds(pl.multiple_of(8 * at, 8), 8)
        for c in range(5):
            table_ref[rows, 128 * c:128 * c + 128] = half[8 * c:8 * c + 8, :]
        table_ref[rows, 640:NBIAS] = half[40:48, 0:NBIAS - 640]
    for c in range(4):
        ggain_ref[:, 128 * c:128 * c + 128] = tf[48 + c:49 + c, :] + tf_recv[48 + c:49 + c, :]

    arrived(big_ref.at[1 - core], R_SIB)
    left(pay, SIB)


def widen(big, gin, table, gain, gin_out, gain_out, wqkv_out, wout_out, table_out, wqkv, wout, sem):
    made = [
        pltpu.make_async_copy(gin, gin_out, sem.at[0]),
        pltpu.make_async_copy(gain, gain_out, sem.at[1]),
        pltpu.make_async_copy(table, table_out, sem.at[2]),
    ]
    for one in made:
        one.start()
    for step in range(4):
        rows = slice(128 * step, 128 * step + 128)
        for block in range(3):
            for core in range(2):
                for p in range(2):
                    lanes = slice(512 * block + 256 * core + 128 * p, 512 * block + 256 * core + 128 * p + 128)
                    if block == 2:
                        column, start = p, 512 * (step // 2) + 128 * (step % 2)
                    else:
                        column, start = 1 - block, 512 * step + 256 + 128 * p
                    wqkv[rows, lanes] = big[core, column, start:start + 128, :].astype(F32) * GRAD_SCALE
        one = pltpu.make_async_copy(wqkv.at[pl.ds(128 * step, 128)], wqkv_out.at[pl.ds(128 * step, 128)], sem.at[3 + step])
        one.start()
        made.append(one)
        core, half = step // 2, step % 2
        for p in range(2):
            for u in range(2):
                start = 1024 + 512 * u + 128 * half
                lanes = slice(256 * p + 128 * u, 256 * p + 128 * u + 128)
                wout[rows, lanes] = big[core, p, start:start + 128, :].astype(F32) * GRAD_SCALE
        one = pltpu.make_async_copy(wout.at[pl.ds(128 * step, 128)], wout_out.at[pl.ds(128 * step, 128)], sem.at[7 + step])
        one.start()
        made.append(one)
    for one in made:
        one.wait()


def per_device(inputs, cotangent, pad_mask, rel_index, bias_table, ln_gain, w_qkv, w_out):
    vmem = pl.BlockSpec(memory_space=pltpu.VMEM)
    hbm = pl.BlockSpec(memory_space=pltpu.HBM)
    big, grad_in, table, gain = pl.pallas_call(
        body,
        out_shape=(
            jax.ShapeDtypeStruct((2, 2, 2048, 128), BF16),
            jax.ShapeDtypeStruct((6, 12, 2, FEAT), F32),
            jax.ShapeDtypeStruct((HEADS, NBIAS), F32),
            jax.ShapeDtypeStruct((1, FEAT), F32),
        ),
        in_specs=[hbm] * 8,
        out_specs=[vmem] * 4,
        scratch_shapes=[
            pltpu.VMEM((6, 12), I32),
            pltpu.VMEM((WT, WT), I32),
            pltpu.VMEM((8, NBIAS), F32),
            pltpu.VMEM((1, FEAT), F32),
            pltpu.VMEM((FEAT, 768), BF16),
            pltpu.VMEM((256, FEAT), BF16),
            pltpu.VMEM((768, FEAT), BF16),
            pltpu.VMEM((FEAT, 256), BF16),
            pltpu.VMEM((6, 12, 2, FEAT), BF16),
            pltpu.VMEM((6, 12, 2, FEAT), BF16),
            pltpu.VMEM((3, 6, 12), I32),
            pltpu.VMEM((32, 128), F32),
            pltpu.VMEM((WT, 128), I32),
            pltpu.VMEM((8, 1, 768), F32),
            pltpu.VMEM((16, 256), I32),
            pltpu.VMEM((2, 16, 128), I32),
            pltpu.VMEM((2, 128, 128), F32),
            pltpu.VMEM((8, WT, 128), F32),
            pltpu.VMEM((WT, 128), F32),
            pltpu.VMEM((2, WT, 128), BF16),
            pltpu.VMEM((2, WT, 128), F32),
            pltpu.VMEM((2, WT, 128), F32),
            pltpu.VMEM((WT, FEAT), F32),
            pltpu.VMEM((WT, 1), F32),
            pltpu.VMEM((2, WT, FEAT), BF16),
            pltpu.VMEM((2, FEAT, WT), BF16),
            pltpu.VMEM((2, WT, FEAT), BF16),
            pltpu.VMEM((2, WT, 768), BF16),
            pltpu.VMEM((2, 768, WT), BF16),
            pltpu.VMEM((2, WT, 256), BF16),
            pltpu.VMEM((2, 256, WT), BF16),
            pltpu.VMEM((2, 256, WT), BF16),
            pltpu.VMEM((2, 256, WT), BF16),
            pltpu.VMEM((2, WT, 768), BF16),
            pltpu.VMEM((2, 8, WT, 128), F32),
            pltpu.VMEM((2, WT, 128), F32),
            pltpu.VMEM((2, WT, 256), F32),
            pltpu.VMEM((2, 2, WT, 512), BF16),
            pltpu.VMEM((8, WT, 128), F32),
            pltpu.VMEM((256, 128), F32),
            pltpu.VMEM((WT, FEAT), F32),
            pltpu.VMEM((WT, FEAT), F32),
            pltpu.VMEM((2, 2048, 128), BF16),
            pltpu.VMEM((2, 3, 512, 128), BF16),
            pltpu.VMEM((2, 512, 128), BF16),
            pltpu.VMEM((2, 3, 128, 128), BF16),
            pltpu.VMEM((2, 128, 128), BF16),
            pltpu.VMEM((7, 2, 16, 128), BF16),
            pltpu.VMEM((2, 128, 128), BF16),
            pltpu.VMEM((64, 128), F32),
            pltpu.VMEM((3, 16, 128), F32),
            pltpu.VMEM((16, 128), F32),
            pltpu.VMEM((3, 16, 128), F32),
            pltpu.VMEM((16, 128), F32),
            pltpu.VMEM((7, 16, 128), F32),
            pltpu.VMEM((64, 128), F32),
            pltpu.VMEM((64, 128), F32),
            pltpu.VMEM((6, 12, 2, FEAT), BF16),
            pltpu.VMEM((6, 12, 2, FEAT), BF16),
            pltpu.VMEM((6, 12, 2, FEAT), F32),
            pltpu.SemaphoreType.DMA((SENDS,)),
            pltpu.SemaphoreType.DMA((RECVS,)),
            pltpu.SemaphoreType.DMA((10,)),
        ],
        compiler_params=pltpu.CompilerParams(
            collective_id=0, has_side_effects=True, vmem_limit_bytes=48 * 1024 * 1024
        ),
    )(
        *(
            pltpu.with_memory_space_constraint(one, pltpu.HBM)
            for one in (
                inputs.transpose(1, 2, 0, 3),
                cotangent.transpose(1, 2, 0, 3),
                pad_mask,
                rel_index,
                bias_table.T,
                ln_gain.reshape(1, FEAT),
                w_qkv,
                w_out,
            )
        )
    )
    grad_in, gain, wqkv, wout, table = pl.pallas_call(
        widen,
        out_shape=(
            jax.ShapeDtypeStruct((6, 12, 2, FEAT), F32),
            jax.ShapeDtypeStruct((1, FEAT), F32),
            jax.ShapeDtypeStruct((FEAT, 3 * FEAT), F32),
            jax.ShapeDtypeStruct((FEAT, FEAT), F32),
            jax.ShapeDtypeStruct((HEADS, NBIAS), F32),
        ),
        in_specs=[vmem] * 4,
        out_specs=[hbm] * 5,
        scratch_shapes=[
            pltpu.VMEM((FEAT, 3 * FEAT), F32),
            pltpu.VMEM((FEAT, FEAT), F32),
            pltpu.SemaphoreType.DMA((11,)),
        ],
        compiler_params=pltpu.CompilerParams(vmem_limit_bytes=24 * 1024 * 1024),
    )(big, grad_in, table, gain)
    return grad_in.transpose(2, 0, 1, 3), gain.reshape(FEAT), wqkv, wout, table.T


def solution(mesh):
    in_specs = (
        P(None, "lat", "lon", None),
        P(None, "lat", "lon", None),
        P("lat", "lon"),
        P(),
        P(),
        P(),
        P(),
        P(),
    )
    out_specs = (P(None, "lat", "lon", None), P(), P(), P(), P())
    return jax.shard_map(
        per_device, mesh=mesh, in_specs=in_specs, out_specs=out_specs, check_vma=False
    )
```
